32 devices in a mesh: sp: 16 (over z, y, core), tp: 2 (over x).
Axes of the slice: x: 2, y: 2, z: 4, core: 2. Of those that a mesh axis runs over, the one named last changes fastest.
Arguments:
- tokens: bfloat16 [256, 128, 512], P(('sp', 'tp')), may hold values from -6 to 6
- cotangent: bfloat16 [256, 128, 512], P(('sp', 'tp')), may hold values from -12 to 12
- w_in: float32 [512, 2048], P('sp', 'tp'), may hold values from -0.25 to 0.25
- w_out: float32 [512, 2048], P('sp', 'tp'), may hold values from -0.125 to 0.125
- mixer_weights: float32 [2, 8, 2, 64, 64], replicated, may hold values from -0.75 to 0.75
- vectors: float32 [13, 512], replicated, may hold values from -0.6 to 1.6, as said below
- w_in_moment: float32 [512, 2048], P('sp', 'tp'), may hold values from -4 to 4
- w_out_moment: float32 [512, 2048], P('sp', 'tp'), may hold values from -4 to 4
- mixer_moment: float32 [2, 8, 2, 64, 64], replicated, may hold values from -4 to 4
- vectors_moment: float32 [13, 512], replicated, may hold values from -4 to 4
- w_in_average: float32 [512, 2048], P('sp', 'tp'), may hold values from -0.25 to 0.25
- w_out_average: float32 [512, 2048], P('sp', 'tp'), may hold values from -0.125 to 0.125
- mixer_average: float32 [2, 8, 2, 64, 64], replicated, may hold values from -0.75 to 0.75
- vectors_average: float32 [13, 512], replicated, may hold values from -0.6 to 1.6, as said below
Outputs:
- output: bfloat16 [256, 128, 512], P(('sp', 'tp'))
- grad_tokens: bfloat16 [256, 128, 512], P(('sp', 'tp'))
- new_w_in: float32 [512, 2048], P('sp', 'tp')
- new_w_out: float32 [512, 2048], P('sp', 'tp')
- new_mixer: float32 [2, 8, 2, 64, 64], replicated
- new_vectors: float32 [13, 512], replicated
- new_w_in_moment: float32 [512, 2048], P('sp', 'tp')
- new_w_out_moment: float32 [512, 2048], P('sp', 'tp')
- new_mixer_moment: float32 [2, 8, 2, 64, 64], replicated
- new_vectors_moment: float32 [13, 512], replicated
- new_w_in_average: float32 [512, 2048], P('sp', 'tp')
- new_w_out_average: float32 [512, 2048], P('sp', 'tp')
- new_mixer_average: float32 [2, 8, 2, 64, 64], replicated
- new_vectors_average: float32 [13, 512], replicated
- w_in_copy: bfloat16 [512, 2048], P('sp', 'tp')
- w_out_copy: bfloat16 [512, 2048], P('sp', 'tp')
The draws below stay inside these ranges and needn't reach their ends.
Inputs may be any that keep to these rules, and one draw needn't show every extreme that they name: `vectors`: gain rows 0 and 2 lie near one, the other rows near zero. `vectors_average`: gain rows 0 and 2 lie near one, the other rows near zero.
All inputs are finite; a program needn't handle non-finite values.
Results may differ from the reference program's by a relative error of at most 0.014.
The reference program's roundings to bfloat16 on the way count: a program that leaves them out, or rounds other values in their place, can miss the bound.
Values may be sent and summed in bfloat16 or wider, within the bound.
No kernel may reach another device: no remote copies, remote signals or barrier semaphores. Data moves between devices by JAX's collectives and lax.ppermute only.
A program may use at most 128 MiB of HBM per device.

```python
import math
import jax
import jax.numpy as jnp
from jax import lax

D = 512
NB = 8
BS = 64
FF = 2048
MODES = 32
G = 128
ITEMS = 2
GROWS = 256
TOKENS = 32768


def draw_cotangent(key, part):
    key = jax.random.fold_in(key, 11)
    values = jnp.clip(jax.random.normal(key, (GROWS, G, D), jnp.float32), -4.0, 4.0)
    highest = 2.0
    rising = 1.0 + highest * jnp.arange(GROWS, dtype=jnp.float32) / GROWS
    return (values * rising[:, None, None]).astype(jnp.bfloat16)


def gain_offset():
    row_index = jnp.arange(13, dtype=jnp.int32)
    return jnp.where((row_index == 0) | (row_index == 2), 1.0, 0.0).astype(jnp.float32)[:, None]


def draw_vectors(key, part):
    key = jax.random.fold_in(key, 21)
    values = jnp.clip(0.2 * jax.random.normal(key, (13, D), jnp.float32), -0.6, 0.6)
    return values + gain_offset()


def draw_vectors_average(key, part):
    key = jax.random.fold_in(key, 22)
    values = jnp.clip(0.2 * jax.random.normal(key, (13, D), jnp.float32), -0.6, 0.6)
    return values + gain_offset()


def raised(values, stream_key, source, target, blocks, factor):
    owner, partner = [(jnp.arange(values.shape[position]) // (values.shape[position] // blocks)).reshape([-1 if axis == position else 1 for axis in range(values.ndim)]) for position in (source, target)]
    chosen = jax.random.permutation(stream_key, blocks)[partner]
    strong = (owner == chosen) | (owner == (partner + blocks // 2) % blocks)
    return jnp.where(strong, factor * values, values)


def levels(rng, extent, shards, low, largest):
    def one(position, blocks):
        draws = jax.random.uniform(jax.random.fold_in(jax.random.fold_in(rng, 6), position), (blocks,), jnp.float32, low / len(shards), largest / len(shards))
        return jnp.repeat(jnp.exp(draws), extent[position] // blocks).reshape((-1,) + (1,) * (len(extent) - position - 1))

    level = one(*shards[0])
    for cut in shards[1:]:
        level = level * one(*cut)
    return level


def scatter_about(rng, extent, scale, reach, cuts=(), held_as=jnp.bfloat16):
    level = levels(rng, extent, cuts, -0.22, 0.18) if cuts else 1.0
    array = jax.random.normal(rng, extent, jnp.float32) * scale * level
    return jnp.minimum(jnp.maximum(array, -reach), reach).astype(held_as)


def noise_with(stream_key, shape, deviation, reach, pieces, heavy, held_as=jnp.bfloat16):
    values = deviation * jax.random.normal(stream_key, shape, jnp.float32)
    if pieces:
        values = values * levels(stream_key, shape, pieces, -0.22, 0.18)
    return jnp.clip(raised(values, jax.random.fold_in(stream_key, 3), *heavy), -reach, reach).astype(held_as)


def setup_inputs(seed: int = 0) -> dict:
    keys = jax.random.split(jax.random.key(seed), 15)
    return {
        "tokens": noise_with(keys[0], (GROWS, G, D), 1.0, 6.0, ((0, 32),), (0, 2, 32, 2.75)),
        "cotangent": draw_cotangent(jax.random.fold_in(keys[14], 71), 0),
        "w_in": scatter_about(keys[2], (D, FF), D ** -0.5, 0.25, ((0, 16), (1, 2)), jnp.float32),
        "w_out": scatter_about(keys[3], (D, FF), FF ** -0.5, 0.125, ((0, 16), (1, 2)), jnp.float32),
        "mixer_weights": scatter_about(keys[4], (2, NB, 2, BS, BS), BS ** -0.5, 0.75, (), jnp.float32),
        "vectors": draw_vectors(jax.random.fold_in(keys[14], 71), 0),
        "w_in_moment": scatter_about(keys[6], (D, FF), 0.6, 4.0, ((0, 16), (1, 2)), jnp.float32),
        "w_out_moment": scatter_about(keys[7], (D, FF), 1.2, 4.0, ((0, 16), (1, 2)), jnp.float32),
        "mixer_moment": scatter_about(keys[8], (2, NB, 2, BS, BS), 0.4, 4.0, (), jnp.float32),
        "vectors_moment": scatter_about(keys[9], (13, D), 1.0, 4.0, (), jnp.float32),
        "w_in_average": scatter_about(keys[10], (D, FF), D ** -0.5, 0.25, ((0, 16), (1, 2)), jnp.float32),
        "w_out_average": scatter_about(keys[11], (D, FF), FF ** -0.5, 0.125, ((0, 16), (1, 2)), jnp.float32),
        "mixer_average": scatter_about(keys[12], (2, NB, 2, BS, BS), BS ** -0.5, 0.75, (), jnp.float32),
        "vectors_average": draw_vectors_average(jax.random.fold_in(keys[14], 71), 0),
    }


EPSILON = 1e-05
LEARNING_RATE = 0.05
MOMENTUM = 0.9
WEIGHT_DECAY = 0.0001
AVERAGE = 0.75
HIGHEST = lax.Precision.HIGHEST

@jax.custom_vjp
def low(v):
    return lax.optimization_barrier(v.astype(jnp.bfloat16)).astype(jnp.float32)

@jax.custom_vjp
def low_back(v):
    return v

def low_keep(v):
    return (low(v), None)

def low_pass(kept, grad):
    return (grad,)

def back_keep(v):
    return (v, None)

def back_low(kept, grad):
    return (low(grad),)
low.defvjp(low_keep, low_pass)
low_back.defvjp(back_keep, back_low)

def dft_tables():
    positions = jnp.arange(G, dtype=jnp.int32)
    wave_index = jnp.arange(MODES, dtype=jnp.int32)
    norm_root = 1.0 / math.sqrt(G)
    step_angle = 2.0 * math.pi / G
    phase_w = (positions[:, None] * wave_index[None, :] % G).astype(jnp.float32) * step_angle
    factor = jnp.where(wave_index == 0, 1.0, 2.0).astype(jnp.float32)
    cos_w = jnp.cos(phase_w) * norm_root
    sin_w = jnp.sin(phase_w) * norm_root
    forward_w = jnp.stack([cos_w, -sin_w], axis=1)
    inverse_w = jnp.stack([cos_w * factor, -sin_w * factor], axis=1)
    frequency = jnp.where(wave_index < MODES // 2, wave_index, wave_index - MODES)
    phase_h = (frequency[:, None] * positions[None, :] % G).astype(jnp.float32) * step_angle
    cos_h = jnp.cos(phase_h) * norm_root
    sin_h = jnp.sin(phase_h) * norm_root
    forward_h = jnp.stack([jnp.stack([cos_h, -sin_h], -1), jnp.stack([sin_h, cos_h], -1)], -2)
    inverse_h = jnp.stack([jnp.stack([cos_h, sin_h], -1), jnp.stack([-sin_h, cos_h], -1)], -2)
    return (forward_w, inverse_w, forward_h, inverse_h)

def layer_norm(values, gain, shift):
    center = values - lax.optimization_barrier(jnp.mean(values, axis=-1, keepdims=True))
    spread = lax.optimization_barrier(jnp.mean(center * center, axis=-1, keepdims=True))
    return center * lax.rsqrt(spread + EPSILON) * gain + shift

def mix_matrices(weights):
    real_part = weights[:, 0]
    imag_part = weights[:, 1]
    upper_half = jnp.concatenate([real_part, imag_part], axis=2)
    lower_half = jnp.concatenate([-imag_part, real_part], axis=2)
    return jnp.concatenate([upper_half, lower_half], axis=1)

def item_layer(shared, one_item):
    w_in, w_out, mixer, vectors, tables = shared
    forward_w, inverse_w, forward_h, inverse_h = tables
    normed_one = low(layer_norm(one_item, vectors[0], vectors[1]))
    blocked = normed_one.reshape(G, G, NB, BS)
    across = low_back(low(jnp.einsum('hwbc,wek->hkbec', blocked, forward_w, precision=HIGHEST)))
    modal_part = low_back(low(jnp.einsum('mhef,hkbec->mkbfc', forward_h, across, precision=HIGHEST)))
    mixer_bias = vectors[9:13].reshape(2, NB, 2 * BS)
    first_matrix = mix_matrices(mixer[0])
    second_matrix = mix_matrices(mixer[1])
    flat_modes = modal_part.reshape(MODES, MODES, NB, 2 * BS)
    mix_inner = low_back(jnp.einsum('mkbi,bij->mkbj', flat_modes, first_matrix, precision=HIGHEST) + mixer_bias[0])
    active = low(jax.nn.gelu(mix_inner))
    mix_outer = low_back(low(jnp.einsum('mkbi,bij->mkbj', active, second_matrix, precision=HIGHEST) + mixer_bias[1]))
    mix_outer = mix_outer.reshape(MODES, MODES, NB, 2, BS)
    returned = low_back(low(jnp.einsum('mhef,mkbec->hkbfc', inverse_h, mix_outer, precision=HIGHEST)))
    spatial = jnp.einsum('hkbec,wek->hwbc', returned, inverse_w, precision=HIGHEST).reshape(G, G, D)
    spatial = low_back(spatial)
    middle = one_item + spatial
    normed_two = low(layer_norm(middle, vectors[2], vectors[3])).reshape(G * G, D)
    hidden = low_back(jnp.dot(normed_two, w_in, precision=HIGHEST) + vectors[5:9].reshape(FF))
    active_two = low(jax.nn.gelu(hidden))
    mlp_output = jnp.dot(active_two, w_out.T, precision=HIGHEST) + vectors[4]
    return middle + mlp_output.reshape(G, G, D)

def whole_layer(tables, tokens, w_in, w_out, mixer, vectors):
    item_stack = tokens.reshape(G, ITEMS, G, D).transpose(1, 0, 2, 3)
    shared = (low(w_in), low(w_out), low(mixer), vectors, tables)

    def one_layer(one_item):
        return item_layer(shared, one_item)
    result = lax.map(jax.checkpoint(one_layer), item_stack)
    return result.transpose(1, 0, 2, 3).reshape(G * ITEMS, G, D)

def update(weight, gradient, moment, average, decay_rate):
    step_grad = gradient + decay_rate * weight
    new_moment = MOMENTUM * moment + step_grad
    new_weight = weight - LEARNING_RATE * (step_grad + MOMENTUM * new_moment)
    new_average = AVERAGE * average + (1.0 - AVERAGE) * new_weight
    return (new_weight, new_moment, new_average)

def reference(tokens, cotangent, w_in, w_out, mixer_weights, vectors, w_in_moment, w_out_moment, mixer_moment, vectors_moment, w_in_average, w_out_average, mixer_average, vectors_average):
    tables = tuple([low(table) for table in dft_tables()])

    def forward_all(inputs, first_weight, second_weight, mixing, vector_rows):
        return whole_layer(tables, inputs, first_weight, second_weight, mixing, vector_rows)
    output, pullback = jax.vjp(forward_all, tokens.astype(jnp.float32), w_in, w_out, mixer_weights, vectors)
    gradients = pullback(cotangent.astype(jnp.float32))
    grad_scale = 1.0 / math.sqrt(TOKENS)
    new_in = update(w_in, gradients[1] * grad_scale, w_in_moment, w_in_average, WEIGHT_DECAY)
    new_out = update(w_out, gradients[2] * grad_scale, w_out_moment, w_out_average, WEIGHT_DECAY)
    new_mix = update(mixer_weights, gradients[3] * grad_scale, mixer_moment, mixer_average, WEIGHT_DECAY)
    new_vec = update(vectors, gradients[4] * grad_scale, vectors_moment, vectors_average, 0.0)
    return (output.astype(jnp.bfloat16), gradients[0].astype(jnp.bfloat16), new_in[0], new_out[0], new_mix[0], new_vec[0], new_in[1], new_out[1], new_mix[1], new_vec[1], new_in[2], new_out[2], new_mix[2], new_vec[2], new_in[0].astype(jnp.bfloat16), new_out[0].astype(jnp.bfloat16))
```

```python
import functools
import math

import jax
import jax.numpy as jnp
import ml_dtypes
import numpy as np
from jax import lax
from jax.experimental import pallas as pl
from jax.experimental.pallas import tpu as pltpu
from jax.sharding import PartitionSpec as P

MODES = 32
EPSILON = 1e-05
LEARNING_RATE = 0.05
MOMENTUM = 0.9
WEIGHT_DECAY = 0.0001
AVERAGE = 0.75
GELU_SCALE = math.sqrt(2.0 / math.pi)
GELU_CUBE = 0.044715
CHUNK = 512
ROWS = 256
BF16 = jnp.bfloat16
F32 = jnp.float32
AXES = ("sp", "tp")


def dft_tables(grid):
    positions = np.arange(grid)
    wave = np.arange(MODES)
    root = np.float32(1.0 / math.sqrt(grid))
    step = np.float32(2.0 * math.pi / grid)
    phase_w = (positions[:, None] * wave[None, :] % grid).astype(np.float32) * step
    factor = np.where(wave == 0, 1.0, 2.0).astype(np.float32)
    cos_w, sin_w = np.cos(phase_w) * root, np.sin(phase_w) * root
    forward_w = np.stack([cos_w, -sin_w], axis=1)
    inverse_w = np.stack([cos_w * factor, -sin_w * factor], axis=1)
    frequency = np.where(wave < MODES // 2, wave, wave - MODES)
    phase_h = (frequency[:, None] * positions[None, :] % grid).astype(np.float32) * step
    cos_h, sin_h = np.cos(phase_h) * root, np.sin(phase_h) * root
    forward_h = np.stack([np.stack([cos_h, -sin_h], -1), np.stack([sin_h, cos_h], -1)], -2)
    return [t.astype(ml_dtypes.bfloat16) for t in (forward_w, inverse_w, forward_h)]


def expanded_tables(grid, grid_rows, items):
    forward_w, inverse_w, forward_h = [t.astype(np.float32) for t in dft_tables(grid)]
    eye_r = np.eye(grid_rows, dtype=np.float32)
    wide_f = np.einsum("wek,rs->kresw", forward_w, eye_r).reshape(-1, grid_rows * grid)
    wide_i = np.einsum("wek,rs->kresw", inverse_w, eye_r).reshape(-1, grid_rows * grid)
    eye_i = np.eye(items, dtype=np.float32)
    high = np.einsum("mhef,ij->fimhje", forward_h, eye_i).reshape(2 * items * MODES, -1)
    ones = np.einsum("mhef,ek->kfm", forward_h.astype(np.float64), forward_w.astype(np.float64).sum(0))
    ones = np.repeat(ones[:, :, None], items, axis=2).reshape(MODES, -1).astype(np.float32)
    cast = [t.astype(ml_dtypes.bfloat16) for t in (wide_f, wide_i, high)]
    return cast[0], cast[1], cast[2], ones


def dot(left, right):
    return jnp.dot(left, right, preferred_element_type=F32)


def dot_nt(left, right):
    return lax.dot_general(left, right, (((1,), (1,)), ((), ())), preferred_element_type=F32)


def dot_tn(left, right):
    return lax.dot_general(left, right, (((0,), (0,)), ((), ())), preferred_element_type=F32)


def normalize(values):
    center = values - jnp.mean(values, axis=-1, keepdims=True)
    inverse = lax.rsqrt(jnp.mean(center * center, axis=-1, keepdims=True) + EPSILON)
    return center * inverse, inverse


def norm_back(upstream, normal, inverse, gain):
    scaled = upstream * gain
    centered = scaled - jnp.mean(scaled, axis=-1, keepdims=True)
    centered = centered - normal * jnp.mean(scaled * normal, axis=-1, keepdims=True)
    return centered * inverse


def gelu_pair(values):
    square = values * values
    bent = jnp.tanh(values * (GELU_SCALE + (GELU_SCALE * GELU_CUBE) * square))
    half = 0.5 + 0.5 * bent
    slope = half + (values * half) * (1.0 - bent) * (GELU_SCALE + (3.0 * GELU_SCALE * GELU_CUBE) * square)
    return values * half, slope


def gelu_value(values):
    square = values * values
    bent = jnp.tanh(values * (GELU_SCALE + (GELU_SCALE * GELU_CUBE) * square))
    return values * (0.5 + 0.5 * bent)


def gather_lanes(ref, groups):
    count = ref.shape[0] // groups
    width = ref.shape[2]
    parts = [ref[g * count : (g + 1) * count].reshape(count * ref.shape[1], width) for g in range(groups)]
    return parts[0] if groups == 1 else jnp.concatenate(parts, axis=1)


def scatter_lanes(ref, values, groups):
    count = ref.shape[0] // groups
    width = ref.shape[2]
    for g in range(groups):
        piece = values[:, g * width : (g + 1) * width]
        ref[g * count : (g + 1) * count] = piece.reshape(count, ref.shape[1], width)


def gather_modes(ref, modes):
    rows = ref.shape[1] // modes
    parts = [
        ref[:, k * rows : (k + 1) * rows, :].reshape(ref.shape[0] * rows, ref.shape[2]) for k in range(modes)
    ]
    return parts[0] if modes == 1 else jnp.concatenate(parts, axis=1)


def scatter_modes(ref, values, modes):
    rows = ref.shape[1] // modes
    width = ref.shape[2]
    for k in range(modes):
        piece = values[:, k * width : (k + 1) * width]
        ref[:, k * rows : (k + 1) * rows, :] = piece.reshape(ref.shape[0], rows, width)


def to_mix_rows(values, modes, width):
    half = values.shape[0] // 2
    parts = []
    for k in range(modes):
        piece = values[:, k * width : (k + 1) * width]
        parts.append(jnp.concatenate([piece[:half], piece[half:]], axis=1))
    return parts[0] if modes == 1 else jnp.concatenate(parts, axis=0)


def from_mix_rows(values, modes, width):
    half = values.shape[0] // modes
    parts = []
    for k in range(modes):
        piece = values[k * half : (k + 1) * half]
        parts.append(jnp.concatenate([piece[:, :width], piece[:, width:]], axis=0))
    return parts[0] if modes == 1 else jnp.concatenate(parts, axis=1)


def enter_kernel(groups, tokens_ref, table_ref, send_ref):
    normal, _ = normalize(tokens_ref[...].astype(F32))
    spectrum = dot(table_ref[...], normal.astype(BF16)).astype(BF16)
    scatter_lanes(send_ref, spectrum, groups)


def mix_kernel(
    modes, got_ref, high_ref, back_ref, mats_ref, bias_ref, gain_ref, shift_ref, ones_ref,
    send_ref, hat_ref, modal_ref, inner_ref, active_ref,
):
    width = got_ref.shape[2]
    hat = dot(high_ref[...], gather_modes(got_ref, modes))
    hat_ref[...] = hat
    pieces = []
    for k in range(modes):
        piece = hat[:, k * width : (k + 1) * width] * gain_ref[...]
        pieces.append(piece + ones_ref[:, k : k + 1] * shift_ref[...])
    modal = pieces[0] if modes == 1 else jnp.concatenate(pieces, axis=1)
    modal = to_mix_rows(modal.astype(BF16), modes, width)
    modal_ref[...] = modal
    inner = dot(modal, mats_ref[0]) + bias_ref[0:1, :]
    inner_ref[...] = inner
    active = gelu_value(inner).astype(BF16)
    active_ref[...] = active
    outer = (dot(active, mats_ref[1]) + bias_ref[1:2, :]).astype(BF16)
    gridded = dot(back_ref[...], from_mix_rows(outer, modes, width)).astype(BF16)
    scatter_modes(send_ref, gridded, modes)


def fold(grad, width, block):
    real = grad[:width, :width] + grad[width:, width:]
    imag = grad[:width, width:] - grad[width:, :width]
    out = []
    for part in (real, imag):
        if width == block:
            out.append(part)
        else:
            lane = lax.broadcasted_iota(jnp.int32, (block, width), 1)
            out.append(jnp.where(lane < block, part[:block], part[block:]))
    return jnp.concatenate(out, axis=0)


def unmix_kernel(
    modes, block, got_ref, high_ref, back_ref, mats_ref, ones_ref, hat_ref, modal_ref, inner_ref, active_ref,
    send_ref, small_ref,
):
    width = got_ref.shape[2]
    grad_outer = dot(high_ref[...], gather_modes(got_ref, modes)).astype(BF16)
    grad_outer = to_mix_rows(grad_outer, modes, width)
    _, slope = gelu_pair(inner_ref[...])
    grad_inner = (dot_nt(grad_outer, mats_ref[1]) * slope).astype(BF16)
    grad_modal = dot_nt(grad_inner, mats_ref[0]).astype(BF16)
    grad_modal = from_mix_rows(grad_modal, modes, width)
    spectrum = dot(back_ref[...], grad_modal).astype(BF16)
    scatter_modes(send_ref, spectrum, modes)
    rows = 2 * block
    small_ref[0:rows] = fold(dot_tn(modal_ref[...], grad_inner), width, block)
    small_ref[rows : 2 * rows] = fold(dot_tn(active_ref[...], grad_outer), width, block)
    bias_one = jnp.sum(grad_inner.astype(F32), axis=0, keepdims=True)
    bias_two = jnp.sum(grad_outer.astype(F32), axis=0, keepdims=True)
    gain = jnp.zeros((1, width), F32)
    shift = jnp.zeros((1, width), F32)
    for k in range(modes):
        lanes = slice(k * width, (k + 1) * width)
        upstream = grad_modal[:, lanes].astype(F32)
        gain = gain + jnp.sum(upstream * hat_ref[:, lanes], axis=0, keepdims=True)
        shift = shift + jnp.sum(upstream * ones_ref[:, k : k + 1], axis=0, keepdims=True)
    tail = [bias_one[:, :width], bias_one[:, width:], bias_two[:, :width], bias_two[:, width:], gain, shift]
    tail.append(jnp.zeros((2, width), F32))
    small_ref[2 * rows : 2 * rows + 8] = jnp.concatenate(tail, axis=0)


def mlp_kernel(
    groups, w_index, in_index, out_index,
    got_ref, tokens_ref, cotangent_ref, weights_ref, vectors_ref, bias_ref, wide_ref, wide_t_ref,
    output_ref, middle_ref, send_ref, grad_in_ref, grad_out_ref, small_ref,
    normed, normed_t, cotangent_t, normal, spread, total, grad_total, w_in, w_out, active, grad_hidden, grad_bias,
):
    step = pl.program_id(0)
    tokens = tokens_ref.shape[0]
    blocks = w_in.shape[0] // weights_ref.shape[2]
    block_rows = weights_ref.shape[2]
    per_half = weights_ref.shape[3] // CHUNK
    row_blocks = [slice(r, r + ROWS) for r in range(0, tokens, ROWS)]

    @pl.when(step == 0)
    def _():
        spectrum = gather_lanes(got_ref, groups)
        bias_out = jnp.zeros((1, tokens_ref.shape[1]), F32)
        for rows in row_blocks:
            spatial = dot(wide_t_ref[rows, :], spectrum)
            middle = tokens_ref[rows, :].astype(F32) + spatial
            unit, inverse = normalize(middle)
            normal[rows, :] = unit
            spread[rows, :] = inverse
            scaled = (unit * vectors_ref[2:3, :] + vectors_ref[3:4, :]).astype(BF16)
            normed[rows, :] = scaled
            normed_t[:, rows] = scaled.T
            total[rows, :] = middle + vectors_ref[4:5, :]
            upstream = cotangent_ref[rows, :]
            cotangent_t[:, rows] = upstream.T
            bias_out = bias_out + jnp.sum(upstream.astype(F32), axis=0, keepdims=True)
        small_ref[2:3, :] = bias_out
        small_ref[7:8, :] = jnp.zeros_like(bias_out)

    half = step // per_half
    columns = pl.ds(pl.multiple_of((step % per_half) * CHUNK, CHUNK), CHUNK)
    for j in range(blocks):
        rows = slice(j * block_rows, (j + 1) * block_rows)
        source = w_index[half * blocks + j]
        w_in[rows, :] = weights_ref[source, 0, :, columns]
        w_out[rows, :] = weights_ref[source, 1, :, columns]
    bias = bias_ref[pl.ds(step, 1), :]
    bias_grad = jnp.zeros((1, CHUNK), F32)
    for rows in row_blocks:
        hidden = dot(normed[rows, :], w_in[...]) + bias
        value, slope = gelu_pair(hidden)
        value = value.astype(BF16)
        active[rows, :] = value
        back = (dot(cotangent_ref[rows, :], w_out[...]) * slope).astype(BF16)
        grad_hidden[rows, :] = back
        bias_grad = bias_grad + jnp.sum(back.astype(F32), axis=0, keepdims=True)
        total[rows, :] += dot_nt(value, w_out[...])
        first = dot_nt(back, w_in[...])
        grad_total[rows, :] = jnp.where(step == 0, first, grad_total[rows, :] + first)
    grad_bias[pl.ds(step, 1), :] = bias_grad
    for grad, target, index in (
        (dot(normed_t[...], grad_hidden[...]), grad_in_ref, in_index),
        (dot(cotangent_t[...], active[...]), grad_out_ref, out_index),
    ):
        grad = grad.astype(BF16)
        for j in range(blocks):
            target[index[half * blocks + j], :, columns] = grad[j * block_rows : (j + 1) * block_rows]

    @pl.when(step == pl.num_programs(0) - 1)
    def _():
        gain = jnp.zeros((1, tokens_ref.shape[1]), F32)
        shift = jnp.zeros((1, tokens_ref.shape[1]), F32)
        for rows in row_blocks:
            upstream = grad_total[rows, :]
            unit = normal[rows, :]
            gain = gain + jnp.sum(upstream * unit, axis=0, keepdims=True)
            shift = shift + jnp.sum(upstream, axis=0, keepdims=True)
            back = norm_back(upstream, unit, spread[rows, :], vectors_ref[2:3, :])
            middle = cotangent_ref[rows, :].astype(F32) + back
            middle_ref[rows, :] = middle
            normed[rows, :] = middle.astype(BF16)
            output_ref[rows, :] = total[rows, :].astype(BF16)
        small_ref[0:1, :] = gain
        small_ref[1:2, :] = shift
        small_ref[3:7, :] = grad_bias[...]
        spectrum = dot(wide_ref[...], normed[...]).astype(BF16)
        scatter_lanes(send_ref, spectrum, groups)


def leave_kernel(groups, got_ref, tokens_ref, middle_ref, vectors_ref, table_ref, out_ref):
    spectrum = gather_lanes(got_ref, groups)
    for start in range(0, tokens_ref.shape[0], ROWS):
        rows = slice(start, start + ROWS)
        upstream = dot(table_ref[rows, :], spectrum)
        unit, inverse = normalize(tokens_ref[rows, :].astype(F32))
        back = norm_back(upstream, unit, inverse, vectors_ref[0:1, :])
        out_ref[rows, :] = (middle_ref[rows, :] + back).astype(BF16)


def update(weight, gradient, moment, average, decay_rate):
    step_grad = gradient + decay_rate * weight
    new_moment = MOMENTUM * moment + step_grad
    new_weight = weight - LEARNING_RATE * (step_grad + MOMENTUM * new_moment)
    new_average = AVERAGE * average + (1.0 - AVERAGE) * new_weight
    return (new_weight, new_moment, new_average)


def call(body, outs, *args, scratch=(), vmem=32, grid=None, prefetch=0, flops=0):
    params = pltpu.CompilerParams(vmem_limit_bytes=vmem << 20)
    whole = pl.BlockSpec(memory_space=pltpu.VMEM)
    outs = [jax.ShapeDtypeStruct(s, d) for s, d in outs]
    size = sum(math.prod(a.shape) * a.dtype.itemsize for a in list(args) + outs)
    return pl.pallas_call(
        body,
        out_shape=outs,
        grid_spec=pltpu.PrefetchScalarGridSpec(
            num_scalar_prefetch=prefetch,
            grid=(1,) if grid is None else grid,
            in_specs=[whole] * (len(args) - prefetch),
            out_specs=[whole] * len(outs),
            scratch_shapes=list(scratch),
        ),
        compiler_params=params,
        cost_estimate=pl.CostEstimate(flops=flops, bytes_accessed=size, transcendentals=0),
    )(*args)


def on_device(
    tokens, cotangent, w_in, w_out, mixer_weights, vectors, w_in_moment, w_out_moment, mixer_moment, vectors_moment,
    w_in_average, w_out_average, mixer_average, vectors_average,
):
    sp_count, tp_count = lax.axis_size("sp"), lax.axis_size("tp")
    devices = sp_count * tp_count
    grid_rows, grid, width = tokens.shape
    local = grid_rows * grid
    items = grid_rows * devices // grid
    block_count, block = mixer_weights.shape[1], mixer_weights.shape[3]
    hidden = w_in.shape[1] * tp_count
    model = w_in.shape[0] * sp_count
    lanes = 2 * block if devices * 2 * block <= MODES * width else block
    groups = width // lanes
    per_group = devices // groups
    modes = MODES // per_group
    joined = lanes // block
    scale = 1.0 / math.sqrt(local * devices)
    wide_f, wide_i, high, ones = expanded_tables(grid, grid_rows, items)
    me = lax.axis_index("sp") * tp_count + lax.axis_index("tp")
    group = me // per_group
    exchange = functools.partial(lax.all_to_all, axis_name=AXES, split_axis=0, concat_axis=0, tiled=True)
    chunk = (devices, modes * grid_rows * 2, lanes)
    rows_all = tokens.reshape(local, width)
    upstream_all = cotangent.reshape(local, width)
    shard_rows, shard_columns = w_in.shape
    near = devices == 32 and per_group == 8 and shard_rows % 16 == 0

    pair = jnp.stack([w_in.astype(BF16), w_out.astype(BF16)])
    if near:
        weights = lax.all_gather(pair, AXES)
        row_block = jnp.arange(sp_count, dtype=jnp.int32)
        half = jnp.arange(tp_count, dtype=jnp.int32)
        owner = row_block[None, :] * tp_count + half[:, None]
        w_index = owner.reshape(-1)
        offset = owner ^ me
        bits = [(offset >> b) & 1 for b in range(5)]
        far = bits[4] * 2 + bits[3]
        in_index = (((bits[1] * 2 + bits[0]) * 2 + bits[2]) * 4 + far).reshape(-1)
        out_index = (((bits[1] * 2 + bits[2]) * 2 + bits[0]) * 4 + far).reshape(-1)
    else:
        weights = lax.all_gather(pair, "sp", axis=1, tiled=True)
        weights = lax.all_gather(weights, "tp")
        w_index = in_index = out_index = jnp.arange(tp_count, dtype=jnp.int32)
    w_blocks = weights.shape[2]

    own_mixer = lax.dynamic_slice_in_dim(mixer_weights, group * joined, joined, 1).astype(BF16)
    eye = jnp.eye(joined, dtype=BF16)
    real = jnp.einsum("lbio,bc->lbico", own_mixer[:, :, 0], eye).reshape(2, lanes, lanes)
    imag = jnp.einsum("lbio,bc->lbico", own_mixer[:, :, 1], eye).reshape(2, lanes, lanes)
    mats = jnp.concatenate(
        [jnp.concatenate([real, imag], axis=2), jnp.concatenate([-imag, real], axis=2)], axis=1
    )
    own_bias = lax.dynamic_slice_in_dim(
        vectors[9:13].reshape(2, block_count, 2, block), group * joined, joined, 1
    )
    own_bias = jnp.swapaxes(own_bias, 1, 2).reshape(2, 2 * lanes)
    own_gain = lax.dynamic_slice_in_dim(vectors[0:1], group * lanes, lanes, 1)
    own_shift = lax.dynamic_slice_in_dim(vectors[1:2], group * lanes, lanes, 1)
    ones = jnp.asarray(np.swapaxes(ones.reshape(per_group, modes, -1), 1, 2))
    own_ones = lax.dynamic_index_in_dim(ones, me % per_group, 0, keepdims=False)

    wide_f, wide_f_t = jnp.asarray(wide_f), jnp.asarray(wide_f.T)
    wide_i, wide_i_t = jnp.asarray(wide_i), jnp.asarray(wide_i.T)
    high, high_t = jnp.asarray(high), jnp.asarray(high.T)
    wide_flops = 2 * wide_f.shape[0] * wide_f.shape[1] * width
    (sent,) = call(
        functools.partial(enter_kernel, groups), [(chunk, BF16)], rows_all, wide_f, flops=wide_flops
    )
    got = exchange(sent)
    half_rows = items * MODES
    sent, hat, modal, inner, active = call(
        functools.partial(mix_kernel, modes),
        [
            (chunk, BF16),
            ((2 * half_rows, modes * lanes), F32),
            ((modes * half_rows, 2 * lanes), BF16),
            ((modes * half_rows, 2 * lanes), F32),
            ((modes * half_rows, 2 * lanes), BF16),
        ],
        got, high, high_t, mats, own_bias, own_gain, own_shift, own_ones,
    )
    got = exchange(sent)
    steps = hidden // CHUNK
    blocks = model // w_blocks
    grad_shape = (tp_count * blocks, w_blocks, hidden // tp_count)
    output, middle, sent, grad_in, grad_out, mlp_small = call(
        functools.partial(mlp_kernel, groups),
        [
            ((local, width), BF16),
            ((local, width), F32),
            (chunk, BF16),
            (grad_shape, BF16),
            (grad_shape, BF16),
            ((8, width), F32),
        ],
        w_index, in_index, out_index,
        got, rows_all, upstream_all, weights, vectors, vectors[5:9].reshape(steps, CHUNK), wide_i, wide_i_t,
        scratch=[
            pltpu.VMEM((local, width), BF16),
            pltpu.VMEM((width, local), BF16),
            pltpu.VMEM((width, local), BF16),
            pltpu.VMEM((local, width), F32),
            pltpu.VMEM((local, 1), F32),
            pltpu.VMEM((local, width), F32),
            pltpu.VMEM((local, width), F32),
            pltpu.VMEM((model, CHUNK), BF16),
            pltpu.VMEM((model, CHUNK), BF16),
            pltpu.VMEM((local, CHUNK), BF16),
            pltpu.VMEM((local, CHUNK), BF16),
            pltpu.VMEM((steps, CHUNK), F32),
        ],
        vmem=50, grid=(steps,), prefetch=3, flops=12 * local * width * hidden + 2 * wide_flops,
    )

    got = exchange(sent)
    small_rows = 4 * block + 8
    sent, mix_small = call(
        functools.partial(unmix_kernel, modes, block),
        [(chunk, BF16), ((small_rows, lanes), F32)],
        got, high, high_t, mats, own_ones, hat, modal, inner, active,
    )
    got = exchange(sent)
    (grad_tokens,) = call(
        functools.partial(leave_kernel, groups),
        [((local, width), BF16)],
        got, rows_all, middle, vectors, wide_f_t, flops=wide_flops,
    )

    def permute(values, mask):
        return lax.ppermute(values, AXES, [(d, d ^ mask) for d in range(devices)])

    if near:
        shard = (4, shard_rows, shard_columns)
        grad_in = grad_in.reshape((2, 2, 2) + shard)
        grad_out = grad_out.reshape((2, 2, 2) + shard)
        sums = []
        for grad, first, second in ((grad_in, 1, 4), (grad_out, 4, 1)):
            one = permute(grad[1], 2)
            two = permute((grad[0, 1].astype(F32) + one[1].astype(F32)).astype(BF16), first)
            three = grad[0, 0, 1].astype(F32) + one[0, 1].astype(F32) + two[1].astype(F32)
            three = permute(three.astype(BF16), second)
            total = grad[0, 0, 0].astype(F32) + one[0, 0].astype(F32) + two[0].astype(F32) + three.astype(F32)
            sums.append(total)
        both = jnp.stack(sums, axis=1)
        away = [permute(both[j].astype(BF16), 8 * j) for j in (1, 2, 3)]
        both = both[0] + away[0].astype(F32) + away[1].astype(F32) + away[2].astype(F32)
        grad_in, grad_out = both[0], both[1]
    else:
        grads = jnp.stack([grad_in, grad_out]).astype(F32)
        grads = lax.psum_scatter(grads, "tp", scatter_dimension=1, tiled=True)
        grads = lax.psum_scatter(grads, "sp", scatter_dimension=2, tiled=True)
        grad_in, grad_out = grads[0, 0], grads[1, 0]
    new_in = update(w_in, grad_in * scale, w_in_moment, w_in_average, WEIGHT_DECAY)
    new_out = update(w_out, grad_out * scale, w_out_moment, w_out_average, WEIGHT_DECAY)

    onehot = (jnp.arange(groups, dtype=jnp.int32) == group).astype(F32)
    mix_all, mlp_all = lax.psum((onehot[:, None, None] * mix_small[None], mlp_small), AXES)
    mixer_grad = mix_all[:, : 4 * block].reshape(groups, 2, 2, block, joined, block)
    mixer_grad = mixer_grad.transpose(1, 0, 4, 2, 3, 5).reshape(mixer_weights.shape)
    tail = mix_all[:, 4 * block :]
    bias_grad = tail[:, :4].reshape(groups, 2, 2, joined, block).transpose(1, 0, 3, 2, 4).reshape(4, width)
    vector_grad = jnp.concatenate(
        [
            tail[:, 4].reshape(1, width),
            tail[:, 5].reshape(1, width),
            mlp_all[:7],
            bias_grad,
        ],
        axis=0,
    )
    new_mix = update(mixer_weights, mixer_grad * scale, mixer_moment, mixer_average, WEIGHT_DECAY)
    new_vec = update(vectors, vector_grad * scale, vectors_moment, vectors_average, 0.0)
    shape = tokens.shape
    return (
        output.reshape(shape), grad_tokens.reshape(shape),
        new_in[0], new_out[0], new_mix[0], new_vec[0],
        new_in[1], new_out[1], new_mix[1], new_vec[1],
        new_in[2], new_out[2], new_mix[2], new_vec[2],
        new_in[0].astype(BF16), new_out[0].astype(BF16),
    )


def solution(mesh):
    rows, split, whole = P(AXES, None, None), P("sp", "tp"), P()
    state = (split, split, whole, whole)
    return jax.shard_map(
        on_device,
        mesh=mesh,
        in_specs=(rows, rows) + state * 3,
        out_specs=(rows, rows) + state * 3 + (split, split),
        check_vma=False,
    )
```

```python
import functools
import math

import jax
import jax.numpy as jnp
import ml_dtypes
import numpy as np
from jax import lax
from jax.experimental import pallas as pl
from jax.experimental.pallas import tpu as pltpu
from jax.sharding import PartitionSpec as P

MODES = 32
EPSILON = 1e-05
LEARNING_RATE = 0.05
MOMENTUM = 0.9
WEIGHT_DECAY = 0.0001
AVERAGE = 0.75
GELU_SCALE = math.sqrt(2.0 / math.pi)
GELU_CUBE = 0.044715
CHUNK = 512
ROWS = 256
BF16 = jnp.bfloat16
F32 = jnp.float32
AXES = ("sp", "tp")
COST = 60 << 20


def dft_tables(grid):
    positions = np.arange(grid)
    wave = np.arange(MODES)
    root = np.float32(1.0 / math.sqrt(grid))
    step = np.float32(2.0 * math.pi / grid)
    phase_w = (positions[:, None] * wave[None, :] % grid).astype(np.float32) * step
    factor = np.where(wave == 0, 1.0, 2.0).astype(np.float32)
    cos_w, sin_w = np.cos(phase_w) * root, np.sin(phase_w) * root
    forward_w = np.stack([cos_w, -sin_w], axis=1)
    inverse_w = np.stack([cos_w * factor, -sin_w * factor], axis=1)
    frequency = np.where(wave < MODES // 2, wave, wave - MODES)
    phase_h = (frequency[:, None] * positions[None, :] % grid).astype(np.float32) * step
    cos_h, sin_h = np.cos(phase_h) * root, np.sin(phase_h) * root
    forward_h = np.stack([np.stack([cos_h, -sin_h], -1), np.stack([sin_h, cos_h], -1)], -2)
    return [t.astype(ml_dtypes.bfloat16) for t in (forward_w, inverse_w, forward_h)]


def expanded_tables(grid, grid_rows, items):
    forward_w, inverse_w, forward_h = [t.astype(np.float32) for t in dft_tables(grid)]
    eye_r = np.eye(grid_rows, dtype=np.float32)
    wide_f = np.einsum("wek,rs->kresw", forward_w, eye_r).reshape(-1, grid_rows * grid)
    wide_i = np.einsum("wek,rs->kresw", inverse_w, eye_r).reshape(-1, grid_rows * grid)
    eye_i = np.eye(items, dtype=np.float32)
    high = np.einsum("mhef,ij->fimhje", forward_h, eye_i).reshape(2 * items * MODES, -1)
    ones = np.einsum("mhef,ek->kfm", forward_h.astype(np.float64), forward_w.astype(np.float64).sum(0))
    ones = np.repeat(ones[:, :, None], items, axis=2).reshape(MODES, -1).astype(np.float32)
    cast = [t.astype(ml_dtypes.bfloat16) for t in (wide_f, wide_i, high)]
    return cast[0], cast[1], cast[2], ones


def dot(left, right):
    return jnp.dot(left, right, preferred_element_type=F32)


def dot_nt(left, right):
    return lax.dot_general(left, right, (((1,), (1,)), ((), ())), preferred_element_type=F32)


def dot_tn(left, right):
    return lax.dot_general(left, right, (((0,), (0,)), ((), ())), preferred_element_type=F32)


def normalize(values):
    center = values - jnp.mean(values, axis=-1, keepdims=True)
    inverse = lax.rsqrt(jnp.mean(center * center, axis=-1, keepdims=True) + EPSILON)
    return center * inverse, inverse


def norm_back(upstream, normal, inverse, gain):
    scaled = upstream * gain
    centered = scaled - jnp.mean(scaled, axis=-1, keepdims=True)
    centered = centered - normal * jnp.mean(scaled * normal, axis=-1, keepdims=True)
    return centered * inverse


def gelu_pair(values):
    square = values * values
    bent = jnp.tanh(values * (GELU_SCALE + (GELU_SCALE * GELU_CUBE) * square))
    half = 0.5 + 0.5 * bent
    slope = half + (values * half) * (1.0 - bent) * (GELU_SCALE + (3.0 * GELU_SCALE * GELU_CUBE) * square)
    return values * half, slope


def gelu_value(values):
    square = values * values
    bent = jnp.tanh(values * (GELU_SCALE + (GELU_SCALE * GELU_CUBE) * square))
    return values * (0.5 + 0.5 * bent)


def gather_lanes(ref, groups):
    count = ref.shape[0] // groups
    width = ref.shape[2]
    parts = [ref[g * count : (g + 1) * count].reshape(count * ref.shape[1], width) for g in range(groups)]
    return parts[0] if groups == 1 else jnp.concatenate(parts, axis=1)


def scatter_lanes(ref, values, groups):
    count = ref.shape[0] // groups
    width = ref.shape[2]
    for g in range(groups):
        piece = values[:, g * width : (g + 1) * width]
        ref[g * count : (g + 1) * count] = piece.reshape(count, ref.shape[1], width)


def gather_modes(ref, modes):
    rows = ref.shape[1] // modes
    parts = [
        ref[:, k * rows : (k + 1) * rows, :].reshape(ref.shape[0] * rows, ref.shape[2]) for k in range(modes)
    ]
    return parts[0] if modes == 1 else jnp.concatenate(parts, axis=1)


def scatter_modes(ref, values, modes):
    rows = ref.shape[1] // modes
    width = ref.shape[2]
    for k in range(modes):
        piece = values[:, k * width : (k + 1) * width]
        ref[:, k * rows : (k + 1) * rows, :] = piece.reshape(ref.shape[0], rows, width)


def to_mix_rows(values, modes, width):
    half = values.shape[0] // 2
    parts = []
    for k in range(modes):
        piece = values[:, k * width : (k + 1) * width]
        parts.append(jnp.concatenate([piece[:half], piece[half:]], axis=1))
    return parts[0] if modes == 1 else jnp.concatenate(parts, axis=0)


def from_mix_rows(values, modes, width):
    half = values.shape[0] // modes
    parts = []
    for k in range(modes):
        piece = values[k * half : (k + 1) * half]
        parts.append(jnp.concatenate([piece[:, :width], piece[:, width:]], axis=0))
    return parts[0] if modes == 1 else jnp.concatenate(parts, axis=1)


def enter_kernel(groups, tokens_ref, table_ref, send_ref):
    normal, _ = normalize(tokens_ref[...].astype(F32))
    spectrum = dot(table_ref[...], normal.astype(BF16)).astype(BF16)
    scatter_lanes(send_ref, spectrum, groups)


def mix_kernel(
    modes, got_ref, high_ref, back_ref, mats_ref, bias_ref, gain_ref, shift_ref, ones_ref,
    send_ref, hat_ref, modal_ref, inner_ref, active_ref,
):
    width = got_ref.shape[2]
    hat = dot(high_ref[...], gather_modes(got_ref, modes))
    hat_ref[...] = hat
    hat_ref.flush()
    pieces = []
    for k in range(modes):
        piece = hat[:, k * width : (k + 1) * width] * gain_ref[...]
        pieces.append(piece + ones_ref[:, k : k + 1] * shift_ref[...])
    modal = pieces[0] if modes == 1 else jnp.concatenate(pieces, axis=1)
    modal = to_mix_rows(modal.astype(BF16), modes, width)
    modal_ref[...] = modal
    modal_ref.flush()
    inner = dot(modal, mats_ref[0]) + bias_ref[0:1, :]
    inner_ref[...] = inner
    inner_ref.flush()
    active = gelu_value(inner).astype(BF16)
    active_ref[...] = active
    active_ref.flush()
    outer = (dot(active, mats_ref[1]) + bias_ref[1:2, :]).astype(BF16)
    gridded = dot(back_ref[...], from_mix_rows(outer, modes, width)).astype(BF16)
    scatter_modes(send_ref, gridded, modes)


def fold(grad, width, block):
    real = grad[:width, :width] + grad[width:, width:]
    imag = grad[:width, width:] - grad[width:, :width]
    out = []
    for part in (real, imag):
        if width == block:
            out.append(part)
        else:
            lane = lax.broadcasted_iota(jnp.int32, (block, width), 1)
            out.append(jnp.where(lane < block, part[:block], part[block:]))
    return jnp.concatenate(out, axis=0)


def by_block(sums, width, block):
    real, imag = sums[:, :width], sums[:, width:]
    if width == block:
        return [real, imag]
    lane = lax.broadcasted_iota(jnp.int32, real.shape, 1)
    turned_real, turned_imag = pltpu.roll(real, block, 1), pltpu.roll(imag, block, 1)
    return [jnp.where(lane < block, real, turned_imag), jnp.where(lane < block, turned_real, imag)]


def unmix_kernel(
    modes, block, got_ref, high_ref, back_ref, mats_ref, ones_ref, hat_ref, modal_ref, inner_ref, active_ref,
    mlp_ref, send_ref, small_ref,
):
    width = got_ref.shape[2]
    grad_outer = dot(high_ref[...], gather_modes(got_ref, modes)).astype(BF16)
    grad_outer = to_mix_rows(grad_outer, modes, width)
    _, slope = gelu_pair(inner_ref[...])
    grad_inner = (dot_nt(grad_outer, mats_ref[1]) * slope).astype(BF16)
    grad_modal = dot_nt(grad_inner, mats_ref[0]).astype(BF16)
    grad_modal = from_mix_rows(grad_modal, modes, width)
    spectrum = dot(back_ref[...], grad_modal).astype(BF16)
    scatter_modes(send_ref, spectrum, modes)
    rows = 2 * block
    grads = [fold(dot_tn(modal_ref[...], grad_inner), width, block)]
    grads.append(fold(dot_tn(active_ref[...], grad_outer), width, block))
    bias_one = by_block(jnp.sum(grad_inner.astype(F32), axis=0, keepdims=True), width, block)
    bias_two = by_block(jnp.sum(grad_outer.astype(F32), axis=0, keepdims=True), width, block)
    gain = jnp.zeros((1, width), F32)
    shift = jnp.zeros((1, width), F32)
    for k in range(modes):
        lanes = slice(k * width, (k + 1) * width)
        upstream = grad_modal[:, lanes].astype(F32)
        gain = gain + jnp.sum(upstream * hat_ref[:, lanes], axis=0, keepdims=True)
        shift = shift + jnp.sum(upstream * ones_ref[:, k : k + 1], axis=0, keepdims=True)
    tail = jnp.concatenate(bias_one + bias_two + [gain, shift, jnp.zeros((2, width), F32)], axis=0)
    mlp = [mlp_ref[:, q : q + width] for q in range(0, mlp_ref.shape[1], width)]
    message = jnp.concatenate(grads + [tail] + mlp, axis=0).astype(BF16)
    small_ref[0 : message.shape[0]] = message
    rest = small_ref.shape[0] - message.shape[0]
    small_ref[message.shape[0] :] = jnp.zeros((rest, width), BF16)


def add_up(*values):
    total = values[0].astype(F32)
    for value in values[1:]:
        total = total + value.astype(F32)
    return total


def first_kernel(kept_ref, one_ref, in_ref, out_ref):
    for part, ref in enumerate((in_ref, out_ref)):
        ref[...] = add_up(kept_ref[part, 1], one_ref[part, 1]).astype(BF16)


def second_kernel(kept_ref, one_ref, in_ref, out_ref, mine_ref, core_ref, y_ref, x_ref, small_ref):
    small = add_up(mine_ref[...], core_ref[...]).astype(BF16)
    small_ref[...] = small
    for part, source, ref in ((0, in_ref, y_ref), (1, out_ref, x_ref)):
        rows = 0
        for z in range(4):
            value = add_up(kept_ref[part, 0, 1, z], one_ref[part, 0, 1, z], source[1, z]).astype(BF16)
            ref[rows : rows + value.shape[0]] = value
            rows += value.shape[0]
        ref[rows:] = small


def third_kernel(kept_ref, one_ref, in_ref, out_ref, y_ref, x_ref, small_ref, other_ref, own_ref, mine_ref, *away_refs):
    size = kept_ref.shape[4]
    along_x = small_ref[...].astype(F32) + x_ref[4 * size :].astype(F32)
    along_y = y_ref[4 * size :].astype(F32) + other_ref[...].astype(F32)
    small = (along_x + along_y).astype(BF16)
    mine_ref[...] = small
    for part, source, last in ((0, in_ref, y_ref), (1, out_ref, x_ref)):
        for z in range(4):
            rows = slice(z * size, (z + 1) * size)
            total = add_up(kept_ref[part, 0, 0, z], one_ref[part, 0, 0, z], source[0, z], last[rows])
            if z == 0:
                own_ref[part] = total
            else:
                away_refs[z - 1][part * size : (part + 1) * size] = total.astype(BF16)
    for ref in away_refs:
        ref[2 * size :] = small


def step_small(
    block, scale, held, mixer_ref, moment_ref, average_ref, vectors_ref, vec_moment_ref,
    vec_average_ref, new_mixer, new_moment, new_average, new_vectors, new_vec_moment, new_vec_average, grad_ref,
):
    groups, _, width = held.shape
    joined = width // block
    rows = 2 * block
    for group in range(groups):
        for layer in range(2):
            grad = held[group, layer * rows : (layer + 1) * rows] * scale
            for part in range(2):
                for j in range(joined):
                    b = group * joined + j
                    piece = grad[part * block : (part + 1) * block, j * block : (j + 1) * block]
                    value, moment, average = update(
                        mixer_ref[layer, b, part], piece, moment_ref[layer, b, part], average_ref[layer, b, part],
                        WEIGHT_DECAY,
                    )
                    new_mixer[layer, b, part] = value
                    new_moment[layer, b, part] = moment
                    new_average[layer, b, part] = average
        tail = held[group, 2 * rows : 2 * rows + 8]
        grad_ref[0:2, group * width : (group + 1) * width] = tail[4:6]
        for layer in range(2):
            for j in range(2):
                b = group * joined + (j if joined == 2 else 0)
                per_row = vectors_ref.shape[1] // (2 * block)
                lane = (b % per_row) * 2 * block + (0 if joined == 2 else j * block)
                row = 9 + layer * 2 + b // per_row
                grad_ref[row : row + 1, lane : lane + width] = tail[2 * layer + j : 2 * layer + j + 1]
    for q in range(groups):
        part = slice(2 * rows + 8 + 8 * q, 2 * rows + 16 + 8 * q)
        total = held[0, part]
        for group in range(1, groups):
            total = total + held[group, part]
        grad_ref[2:9, q * width : (q + 1) * width] = total[0:7]
    value, moment, average = update(
        vectors_ref[...], grad_ref[0:13, :] * scale, vec_moment_ref[...], vec_average_ref[...], 0.0
    )
    new_vectors[...] = value
    new_vec_moment[...] = moment
    new_vec_average[...] = average


def step_all(block, scale, place_ref, own_ref, mine_ref, *refs):
    away_refs, weights, small = refs[:3], refs[3:9], refs[9:15]
    new_weights, new_small, (held, grad_ref) = refs[15:23], refs[23:29], refs[29:]
    size = own_ref.shape[1]
    far = place_ref[0] >> 3
    held[far] = mine_ref[...].astype(F32)
    for z, ref in enumerate(away_refs):
        held[far ^ (z + 1)] = ref[2 * size :].astype(F32)
    for part in range(2):
        rows = slice(part * size, (part + 1) * size)
        total = own_ref[part] + add_up(*[ref[rows] for ref in away_refs])
        count = weights[part].shape[0]
        for q in range(size // count):
            lanes = slice(q * 128, (q + 1) * 128)
            grad = total[q * count : (q + 1) * count] * scale
            values = update(
                weights[part][:, lanes], grad, weights[2 + part][:, lanes], weights[4 + part][:, lanes], WEIGHT_DECAY
            )
            for i, value in enumerate(values):
                new_weights[2 * i + part][:, lanes] = value
            new_weights[6 + part][:, lanes] = values[0].astype(BF16)
    step_small(block, scale, held, *small, *new_small, grad_ref)


def load_weights(near, place_ref, pieces, w_in, w_out, sems):
    copies = []
    if not near:
        copies = [(pieces[0].at[:, part], target) for part, target in enumerate((w_in, w_out))]
    else:
        me = place_ref[0]
        at = [(me >> 1) & 1, (me >> 2) & 1, me & 1, me >> 3]
        size = pieces[0].shape[3]
        for i, ref in enumerate(pieces):
            for j in range(2):
                x, y = (i >> 1 & 1, j) if i & 1 else (j, i >> 1 & 1)
                for k in range(2):
                    z = 2 * (i & 1) + k
                    row = (((at[3] ^ z) * 2 + (at[1] ^ y)) * 2 + (at[0] ^ (i >> 2))) * size
                    rows = pl.ds(pl.multiple_of(row, size), size)
                    for part, target in enumerate((w_in, w_out)):
                        copies.append((ref.at[j, k, part], target.at[at[2] ^ x, rows]))
    copies = [pltpu.make_async_copy(source, target, sems.at[i]) for i, (source, target) in enumerate(copies)]
    for copy in copies:
        copy.start()
    return copies


def mlp_kernel(
    groups, near, place_ref, got_ref, wide_t_ref, tokens_ref, cotangent_ref, vectors_ref, bias_ref, wide_ref, *refs
):
    count = 8 if near else 1
    pieces, refs = refs[:count], refs[count:]
    output_ref, middle_ref, send_ref, small_ref, *refs = refs
    grad_refs, refs = refs[:2], refs[2:]
    normed, normed_t, cotangent_t, normal, spread, upstream_ref, w_in, w_out, active, grad_hidden, sems = refs
    copies = load_weights(near, place_ref, pieces, w_in, w_out, sems)
    tokens, width = tokens_ref.shape
    halves, _, columns = w_in.shape
    gain, shift, bias_out = vectors_ref[2:3, :], vectors_ref[3:4, :], vectors_ref[4:5, :]
    row_blocks = [slice(r, r + ROWS) for r in range(0, tokens, ROWS)]
    spectrum = gather_lanes(got_ref, groups)
    bias_out_grad = jnp.zeros((1, width), F32)
    for rows in row_blocks:
        middle = tokens_ref[rows, :].astype(F32) + dot(wide_t_ref[rows, :], spectrum)
        unit, inverse = normalize(middle)
        normal[rows, :] = unit
        spread[rows, :] = inverse
        scaled = (unit * gain + shift).astype(BF16)
        normed[rows, :] = scaled
        normed_t[:, rows] = scaled.T
        middle_ref[rows, :] = middle + bias_out
        upstream = cotangent_ref[rows, :]
        cotangent_t[:, rows] = upstream.T
        bias_out_grad = bias_out_grad + jnp.sum(upstream.astype(F32), axis=0, keepdims=True)
    for copy in copies:
        copy.wait()
    gain_grad = jnp.zeros((1, width), F32)
    shift_grad = jnp.zeros((1, width), F32)
    chunks = [(h, c) for h in range(halves) for c in range(0, columns, CHUNK)]
    bias_grads = [jnp.zeros((1, CHUNK), F32) for _ in chunks]
    for rows in row_blocks:
        for i, (h, c) in enumerate(chunks):
            lanes, flat = slice(c, c + CHUNK), slice(h * columns + c, h * columns + c + CHUNK)
            hidden = dot(normed[rows, :], w_in[h, :, lanes]) + bias_ref[i : i + 1, :]
            value, slope = gelu_pair(hidden)
            active[rows, flat] = value.astype(BF16)
            back = (dot(cotangent_ref[rows, :], w_out[h, :, lanes]) * slope).astype(BF16)
            grad_hidden[rows, flat] = back
            bias_grads[i] = bias_grads[i] + jnp.sum(back.astype(F32), axis=0, keepdims=True)
        total, back = middle_ref[rows, :], None
        for h in range(halves):
            flat = slice(h * columns, (h + 1) * columns)
            total = total + dot_nt(active[rows, flat], w_out[h])
            term = dot_nt(grad_hidden[rows, flat], w_in[h])
            back = term if back is None else back + term
        output_ref[rows, :] = total.astype(BF16)
        unit = normal[rows, :]
        gain_grad = gain_grad + jnp.sum(back * unit, axis=0, keepdims=True)
        shift_grad = shift_grad + jnp.sum(back, axis=0, keepdims=True)
        middle = cotangent_ref[rows, :].astype(F32) + norm_back(back, unit, spread[rows, :], gain)
        middle_ref[rows, :] = middle
        upstream_ref[rows, :] = middle.astype(BF16)
    output_ref.flush()
    middle_ref.flush()
    small_ref[0:3, :] = jnp.concatenate([gain_grad, shift_grad, bias_out_grad], axis=0)
    small_ref[3:7, :] = jnp.concatenate(bias_grads, axis=0)
    small_ref[7:8, :] = jnp.zeros((1, width), F32)
    spectrum = dot(wide_ref[...], upstream_ref[...]).astype(BF16)
    scatter_lanes(send_ref, spectrum, groups)
    for i, (h, c) in enumerate(chunks):
        flat = slice(h * columns + c, h * columns + c + CHUNK)
        grads = [
            dot(normed_t[...], grad_hidden[:, flat]).astype(BF16), dot(cotangent_t[...], active[:, flat]).astype(BF16)
        ]
        if not near:
            for ref, grad in zip(grad_refs, grads, strict=True):
                ref[h, :, c : c + CHUNK] = grad
            continue
        me = place_ref[0]
        at = [(me >> 1) & 1, (me >> 2) & 1, me & 1, me >> 3]
        size = w_in.shape[1] // 16
        x = h ^ at[2]
        for core in range(2):
            for ref, mine in ((grad_refs[0], core), (grad_refs[1], 1 - core)):

                @pl.when(at[0] == mine)
                def _(ref=ref, core=core, c=c, x=x, grads=grads):
                    for z in range(4):
                        for y in range(2):
                            rows = slice(((z * 2 + y) * 2 + core) * size, ((z * 2 + y) * 2 + core + 1) * size)
                            for q in range(CHUNK // 128):
                                lanes = slice(q * 128, (q + 1) * 128)
                                place = slice((c // 128 + q) * size, (c // 128 + q + 1) * size)
                                ref[0, x, y ^ at[1], z ^ at[3], place, :] = grads[0][rows, lanes]
                                ref[1, y ^ at[1], x, z ^ at[3], place, :] = grads[1][rows, lanes]


def leave_kernel(groups, got_ref, tokens_ref, middle_ref, vectors_ref, table_ref, out_ref):
    spectrum = gather_lanes(got_ref, groups)
    for start in range(0, tokens_ref.shape[0], ROWS):
        rows = slice(start, start + ROWS)
        upstream = dot(table_ref[rows, :], spectrum)
        unit, inverse = normalize(tokens_ref[rows, :].astype(F32))
        back = norm_back(upstream, unit, inverse, vectors_ref[0:1, :])
        out_ref[rows, :] = (middle_ref[rows, :] + back).astype(BF16)


def update(weight, gradient, moment, average, decay_rate):
    step_grad = gradient + decay_rate * weight
    new_moment = MOMENTUM * moment + step_grad
    new_weight = weight - LEARNING_RATE * (step_grad + MOMENTUM * new_moment)
    new_average = AVERAGE * average + (1.0 - AVERAGE) * new_weight
    return (new_weight, new_moment, new_average)


class Source:
    def __init__(self, ref, copy):
        self.ref, self.copy, self.shape = ref, copy, ref.shape

    def __getitem__(self, index):
        if self.copy is not None:
            self.copy.wait()
            self.copy = None
        return self.ref[index]


class Sink:
    def __init__(self, ref, copy):
        self.ref, self.copy, self.shape, self.sent = ref, copy, ref.shape, False

    def __getitem__(self, index):
        return self.ref[index]

    def __setitem__(self, index, value):
        self.ref[index] = value

    def flush(self):
        if not self.sent:
            self.copy.start()
            self.sent = True


class Far:
    def __init__(self, *what):
        self.what = what


def call(body, outs, *args, scalars=(), raw=(), scratch=(), flops=0, carry=(), cost=None, vmem=20):
    near, far, there = [pl.BlockSpec(memory_space=m) for m in (pltpu.VMEM, pltpu.HBM, pl.ANY)]
    in_far, out_far = [isinstance(a, Far) for a in args], [isinstance(o, Far) for o in outs]
    args = [
        pltpu.with_memory_space_constraint(*((a.what[0], pltpu.HBM) if f else (a, pltpu.VMEM)))
        for a, f in zip(args, in_far, strict=True)
    ]
    raw = [pltpu.with_memory_space_constraint(a, pltpu.HBM) for a in raw]
    outs = [o.what if f else o for o, f in zip(outs, out_far, strict=True)]
    outs = [jax.ShapeDtypeStruct(s, d) for s, d in outs]
    n_scalar, n_in, n_raw, n_carry, n_out = len(scalars), len(args), len(raw), len(carry), len(outs)
    buffers = [pltpu.VMEM(a.shape, a.dtype) for a, f in zip(args + outs, in_far + out_far, strict=True) if f]

    def inner(*refs):
        refs = list(refs)

        def take(count):
            taken = refs[:count]
            del refs[:count]
            return taken

        scalar_refs, in_refs, raw_refs, _, out_refs, _ = [
            take(n) for n in (n_scalar, n_in, n_raw, n_carry, n_out, n_carry)
        ]
        space = take(len(buffers))
        sems = take(1)[0] if buffers else None
        sources, sinks, used = [], [], 0
        for ref, away in zip(in_refs, in_far, strict=True):
            if away:
                copy = pltpu.make_async_copy(ref, space[used], sems.at[used])
                copy.start()
                ref = Source(space[used], copy)
                used += 1
            sources.append(ref)
        for ref, away in zip(out_refs, out_far, strict=True):
            if away:
                ref = Sink(space[used], pltpu.make_async_copy(space[used], ref, sems.at[used]))
                used += 1
            sinks.append(ref)
        body(*scalar_refs, *sources, *raw_refs, *sinks, *refs)
        for source in sources:
            if isinstance(source, Source) and source.copy is not None:
                source.copy.wait()
        sinks = [sink for sink in sinks if isinstance(sink, Sink)]
        for sink in sinks:
            sink.flush()
        for sink in sinks:
            sink.copy.wait()

    every = list(args) + list(raw)
    size = sum(math.prod(a.shape) * a.dtype.itemsize for a in every + outs) if cost is None else cost
    sems = [pltpu.SemaphoreType.DMA((len(buffers),))] if buffers else []
    return pl.pallas_call(
        inner,
        out_shape=[(pltpu.HBM if f else pltpu.VMEM)(o.shape, o.dtype) for o, f in zip(outs, out_far, strict=True)]
        + [jax.ShapeDtypeStruct(a.shape, a.dtype) for a in carry],
        in_specs=[pl.BlockSpec(memory_space=pltpu.SMEM)] * n_scalar
        + [far if f else near for f in in_far]
        + [far] * n_raw
        + [there] * n_carry,
        out_specs=[far if f else near for f in out_far] + [there] * n_carry,
        scratch_shapes=buffers + sems + list(scratch),
        input_output_aliases={n_scalar + n_in + n_raw + i: n_out + i for i in range(n_carry)},
        compiler_params=pltpu.CompilerParams(vmem_limit_bytes=vmem << 20),
        cost_estimate=pl.CostEstimate(flops=flops, bytes_accessed=size, transcendentals=0),
    )(*scalars, *args, *raw, *carry)


def on_device(
    tokens, cotangent, w_in, w_out, mixer_weights, vectors, w_in_moment, w_out_moment, mixer_moment, vectors_moment,
    w_in_average, w_out_average, mixer_average, vectors_average,
):
    sp_count, tp_count = lax.axis_size("sp"), lax.axis_size("tp")
    devices = sp_count * tp_count
    grid_rows, grid, width = tokens.shape
    local = grid_rows * grid
    items = grid_rows * devices // grid
    block_count, block = mixer_weights.shape[1], mixer_weights.shape[3]
    hidden = w_in.shape[1] * tp_count
    model = w_in.shape[0] * sp_count
    lanes = 2 * block if devices * 2 * block <= MODES * width else block
    groups = width // lanes
    per_group = devices // groups
    modes = MODES // per_group
    joined = lanes // block
    scale = 1.0 / math.sqrt(local * devices)
    wide_f, wide_i, high, ones = expanded_tables(grid, grid_rows, items)
    me = lax.axis_index("sp") * tp_count + lax.axis_index("tp")
    group = me // per_group
    exchange = functools.partial(lax.all_to_all, axis_name=AXES, split_axis=0, concat_axis=0, tiled=True)
    chunk = (devices, modes * grid_rows * 2, lanes)
    rows_all = tokens.reshape(local, width)
    upstream_all = cotangent.reshape(local, width)
    shard_rows, shard_columns = w_in.shape
    shard_size = shard_rows * shard_columns // 128
    near = devices == 32 and per_group == 8 and shard_rows % 16 == 0

    def permute(values, mask):
        return lax.ppermute(values, AXES, [(d, d ^ mask) for d in range(devices)])

    pair = jnp.stack([w_in.astype(BF16), w_out.astype(BF16)])
    if near:
        line = [pair] + [permute(pair, 8 * z) for z in (1, 2, 3)]
        carried = [jnp.stack([v, permute(v, m)]) for v, m in ((jnp.stack(line[:2]), 1), (jnp.stack(line[2:]), 4))]
    else:
        weights = lax.all_gather(pair, "sp", axis=1, tiled=True)
        pieces, carried = [lax.all_gather(weights, "tp")], []

    own_mixer = lax.dynamic_slice_in_dim(mixer_weights, group * joined, joined, 1).astype(BF16)
    eye = jnp.eye(joined, dtype=BF16)
    real = jnp.einsum("lbio,bc->lbico", own_mixer[:, :, 0], eye).reshape(2, lanes, lanes)
    imag = jnp.einsum("lbio,bc->lbico", own_mixer[:, :, 1], eye).reshape(2, lanes, lanes)
    mats = jnp.concatenate(
        [jnp.concatenate([real, imag], axis=2), jnp.concatenate([-imag, real], axis=2)], axis=1
    )
    own_bias = lax.dynamic_slice_in_dim(
        vectors[9:13].reshape(2, block_count, 2, block), group * joined, joined, 1
    )
    own_bias = jnp.swapaxes(own_bias, 1, 2).reshape(2, 2 * lanes)
    own_gain = lax.dynamic_slice_in_dim(vectors[0:1], group * lanes, lanes, 1)
    own_shift = lax.dynamic_slice_in_dim(vectors[1:2], group * lanes, lanes, 1)
    ones = jnp.asarray(np.swapaxes(ones.reshape(per_group, modes, -1), 1, 2))
    own_ones = lax.dynamic_index_in_dim(ones, me % per_group, 0, keepdims=False)

    wide_f, wide_f_t = jnp.asarray(wide_f), jnp.asarray(wide_f.T)
    wide_i, wide_i_t = jnp.asarray(wide_i), jnp.asarray(wide_i.T)
    high, high_t = jnp.asarray(high), jnp.asarray(high.T)
    wide_flops = 2 * wide_f.shape[0] * wide_f.shape[1] * width
    (sent,) = call(
        functools.partial(enter_kernel, groups), [(chunk, BF16)], Far(rows_all), Far(wide_f), flops=wide_flops
    )
    got = exchange(sent)
    half_rows = items * MODES
    sent, hat, modal, inner, active, *carried = call(
        functools.partial(mix_kernel, modes),
        [
            (chunk, BF16),
            Far((2 * half_rows, modes * lanes), F32),
            Far((modes * half_rows, 2 * lanes), BF16),
            Far((modes * half_rows, 2 * lanes), F32),
            Far((modes * half_rows, 2 * lanes), BF16),
        ],
        got, high, high_t, mats, own_bias, own_gain, own_shift, own_ones,
        carry=carried,
    )
    if near:
        pieces = carried + [permute(carried[0], 4), permute(carried[1], 1)]
        pieces += [permute(p, 2) for p in pieces]
    got = exchange(sent)
    steps = hidden // CHUNK
    grads = [((2, 2, 2, 4, shard_size, 128), BF16)] * 2 if near else [((tp_count, model, shard_columns), BF16)] * 2
    output, middle, sent, mlp_small, *grads = call(
        functools.partial(mlp_kernel, groups, near),
        [Far((local, width), BF16), Far((local, width), F32), (chunk, BF16), ((8, width), F32)] + grads,
        got, Far(wide_i_t), Far(rows_all), Far(upstream_all), vectors, vectors[5:9].reshape(steps, CHUNK), Far(wide_i),
        scalars=[me[None]], raw=pieces,
        scratch=[
            pltpu.VMEM((local, width), BF16),
            pltpu.VMEM((width, local), BF16),
            pltpu.VMEM((width, local), BF16),
            pltpu.VMEM((local, width), F32),
            pltpu.VMEM((local, 1), F32),
            pltpu.VMEM((local, width), BF16),
            pltpu.VMEM((tp_count, model, shard_columns), BF16),
            pltpu.VMEM((tp_count, model, shard_columns), BF16),
            pltpu.VMEM((local, hidden), BF16),
            pltpu.VMEM((local, hidden), BF16),
            pltpu.SemaphoreType.DMA((64 if near else 2,)),
        ],
        flops=12 * local * width * hidden + 2 * wide_flops, vmem=44,
    )

    carried = []
    if near:
        shard = (4, shard_size, 128)
        kept, one = grads[0], permute(grads[1], 2)
        sent_in, sent_out = call(
            first_kernel, [((2,) + shard, BF16)] * 2, kept, one, cost=0,
        )
        carried = [permute(sent_in, 1), permute(sent_out, 4)]

    got = exchange(sent)
    small_rows = -(-(4 * block + 8 + 8 * groups) // 16) * 16
    sent, small = call(
        functools.partial(unmix_kernel, modes, block),
        [(chunk, BF16), ((small_rows, lanes), BF16)],
        got, Far(high), Far(high_t), Far(mats), own_ones, Far(hat), Far(modal), Far(inner), Far(active), mlp_small,
        cost=COST,
    )
    if near:
        over_y, over_x, small = call(
            second_kernel, [((4 * shard_size + small_rows, 128), BF16)] * 2 + [((small_rows, 128), BF16)],
            kept, one, *carried, small, permute(small, 2), cost=0,
        )
        from_y, from_x, from_both = permute(over_y, 4), permute(over_x, 1), permute(small, 5)
        own, mine, *away = call(
            third_kernel,
            [((2, shard_size, 128), F32), ((small_rows, 128), BF16)] + [((2 * shard_size + small_rows, 128), BF16)] * 3,
            kept, one, *carried, from_y, from_x, small, from_both, cost=0,
        )
        away = [permute(a, 8 * (z + 1)) for z, a in enumerate(away)]
    got = exchange(sent)
    (grad_tokens,) = call(
        functools.partial(leave_kernel, groups),
        [Far((local, width), BF16)],
        got, Far(rows_all), Far(middle), vectors, Far(wide_f_t), flops=wide_flops,
    )

    state = [mixer_weights, mixer_moment, mixer_average, vectors, vectors_moment, vectors_average]
    new_state = [Far(a.shape, F32) for a in state]
    scratch = [pltpu.VMEM((16, width), F32)]
    if near:
        weights = [w_in, w_out, w_in_moment, w_out_moment, w_in_average, w_out_average]
        *stepped, grad_tokens = call(
            functools.partial(step_all, block, scale),
            [Far(w_in.shape, F32)] * 6 + [Far(w_in.shape, BF16)] * 2 + new_state,
            own, mine, *away, *weights, *state,
            scalars=[me[None]], scratch=[pltpu.VMEM((groups, small_rows, lanes), F32)] + scratch, carry=[grad_tokens],
        )
        new_in, new_out = stepped[0:8:2], stepped[1:8:2]
        stepped = stepped[8:]
    else:
        grads = jnp.stack(grads).astype(F32)
        grads = lax.psum_scatter(grads, "tp", scatter_dimension=1, tiled=True)
        grads = lax.psum_scatter(grads, "sp", scatter_dimension=2, tiled=True)
        new_in = update(w_in, grads[0, 0] * scale, w_in_moment, w_in_average, WEIGHT_DECAY)
        new_out = update(w_out, grads[1, 0] * scale, w_out_moment, w_out_average, WEIGHT_DECAY)
        new_in, new_out = new_in + (new_in[0].astype(BF16),), new_out + (new_out[0].astype(BF16),)
        onehot = (jnp.arange(groups, dtype=jnp.int32) == group).astype(F32)[:, None, None]
        held = lax.psum(onehot * small.astype(F32), AXES)
        stepped = call(functools.partial(step_small, block, scale), new_state, held, *state, scratch=scratch)
    new_mix, new_vec = stepped[0:3], stepped[3:6]
    shape = tokens.shape
    return (
        output.reshape(shape), grad_tokens.reshape(shape),
        new_in[0], new_out[0], new_mix[0], new_vec[0],
        new_in[1], new_out[1], new_mix[1], new_vec[1],
        new_in[2], new_out[2], new_mix[2], new_vec[2],
        new_in[3], new_out[3],
    )


def solution(mesh):
    rows, split, whole = P(AXES, None, None), P("sp", "tp"), P()
    state = (split, split, whole, whole)
    return jax.shard_map(
        on_device,
        mesh=mesh,
        in_specs=(rows, rows) + state * 3,
        out_specs=(rows, rows) + state * 3 + (split, split),
        check_vma=False,
    )
```

```python
import functools
import math

import jax
import jax.numpy as jnp
import ml_dtypes
import numpy as np
from jax import lax
from jax.experimental import pallas as pl
from jax.experimental.pallas import tpu as pltpu
from jax.sharding import PartitionSpec as P

MODES = 32
EPSILON = 1e-05
LEARNING_RATE = 0.05
MOMENTUM = 0.9
WEIGHT_DECAY = 0.0001
AVERAGE = 0.75
GELU_SCALE = math.sqrt(2.0 / math.pi)
GELU_CUBE = 0.044715
CHUNK = 512
ROWS = 256
BF16 = jnp.bfloat16
F32 = jnp.float32
AXES = ("sp", "tp")
COST = 60 << 20


def dft_tables(grid):
    positions = np.arange(grid)
    wave = np.arange(MODES)
    root = np.float32(1.0 / math.sqrt(grid))
    step = np.float32(2.0 * math.pi / grid)
    phase_w = (positions[:, None] * wave[None, :] % grid).astype(np.float32) * step
    factor = np.where(wave == 0, 1.0, 2.0).astype(np.float32)
    cos_w, sin_w = np.cos(phase_w) * root, np.sin(phase_w) * root
    forward_w = np.stack([cos_w, -sin_w], axis=1)
    inverse_w = np.stack([cos_w * factor, -sin_w * factor], axis=1)
    frequency = np.where(wave < MODES // 2, wave, wave - MODES)
    phase_h = (frequency[:, None] * positions[None, :] % grid).astype(np.float32) * step
    cos_h, sin_h = np.cos(phase_h) * root, np.sin(phase_h) * root
    forward_h = np.stack([np.stack([cos_h, -sin_h], -1), np.stack([sin_h, cos_h], -1)], -2)
    return [t.astype(ml_dtypes.bfloat16) for t in (forward_w, inverse_w, forward_h)]


def expanded_tables(grid, grid_rows, items):
    forward_w, inverse_w, forward_h = [t.astype(np.float32) for t in dft_tables(grid)]
    eye_r = np.eye(grid_rows, dtype=np.float32)
    wide_f = np.einsum("wek,rs->kresw", forward_w, eye_r).reshape(-1, grid_rows * grid)
    wide_i = np.einsum("wek,rs->kresw", inverse_w, eye_r).reshape(-1, grid_rows * grid)
    eye_i = np.eye(items, dtype=np.float32)
    high = np.einsum("mhef,ij->fimhje", forward_h, eye_i).reshape(2 * items * MODES, -1)
    ones = np.einsum("mhef,ek->kfm", forward_h.astype(np.float64), forward_w.astype(np.float64).sum(0))
    ones = np.repeat(ones[:, :, None], items, axis=2).reshape(MODES, -1).astype(np.float32)
    cast = [t.astype(ml_dtypes.bfloat16) for t in (wide_f, wide_i, high)]
    return cast[0], cast[1], cast[2], ones


def dot(left, right):
    return jnp.dot(left, right, preferred_element_type=F32)


def dot_nt(left, right):
    return lax.dot_general(left, right, (((1,), (1,)), ((), ())), preferred_element_type=F32)


def dot_tn(left, right):
    return lax.dot_general(left, right, (((0,), (0,)), ((), ())), preferred_element_type=F32)


def normalize(values):
    center = values - jnp.mean(values, axis=-1, keepdims=True)
    inverse = lax.rsqrt(jnp.mean(center * center, axis=-1, keepdims=True) + EPSILON)
    return center * inverse, inverse


def norm_back(upstream, normal, inverse, gain):
    scaled = upstream * gain
    centered = scaled - jnp.mean(scaled, axis=-1, keepdims=True)
    centered = centered - normal * jnp.mean(scaled * normal, axis=-1, keepdims=True)
    return centered * inverse


def gelu_pair(values):
    square = values * values
    bent = jnp.tanh(values * (GELU_SCALE + (GELU_SCALE * GELU_CUBE) * square))
    half = 0.5 + 0.5 * bent
    slope = half + (values * half) * (1.0 - bent) * (GELU_SCALE + (3.0 * GELU_SCALE * GELU_CUBE) * square)
    return values * half, slope


def gelu_value(values):
    square = values * values
    bent = jnp.tanh(values * (GELU_SCALE + (GELU_SCALE * GELU_CUBE) * square))
    return values * (0.5 + 0.5 * bent)


def gather_lanes(ref, groups):
    count = ref.shape[0] // groups
    width = ref.shape[2]
    parts = [ref[g * count : (g + 1) * count].reshape(count * ref.shape[1], width) for g in range(groups)]
    return parts[0] if groups == 1 else jnp.concatenate(parts, axis=1)


def scatter_lanes(ref, values, groups):
    count = ref.shape[0] // groups
    width = ref.shape[2]
    for g in range(groups):
        piece = values[:, g * width : (g + 1) * width]
        ref[g * count : (g + 1) * count] = piece.reshape(count, ref.shape[1], width)


def gather_modes(ref, modes):
    rows = ref.shape[1] // modes
    parts = [
        ref[:, k * rows : (k + 1) * rows, :].reshape(ref.shape[0] * rows, ref.shape[2]) for k in range(modes)
    ]
    return parts[0] if modes == 1 else jnp.concatenate(parts, axis=1)


def scatter_modes(ref, values, modes):
    rows = ref.shape[1] // modes
    width = ref.shape[2]
    for k in range(modes):
        piece = values[:, k * width : (k + 1) * width]
        ref[:, k * rows : (k + 1) * rows, :] = piece.reshape(ref.shape[0], rows, width)


def to_mix_rows(values, modes, width):
    half = values.shape[0] // 2
    parts = []
    for k in range(modes):
        piece = values[:, k * width : (k + 1) * width]
        parts.append(jnp.concatenate([piece[:half], piece[half:]], axis=1))
    return parts[0] if modes == 1 else jnp.concatenate(parts, axis=0)


def from_mix_rows(values, modes, width):
    half = values.shape[0] // modes
    parts = []
    for k in range(modes):
        piece = values[k * half : (k + 1) * half]
        parts.append(jnp.concatenate([piece[:, :width], piece[:, width:]], axis=0))
    return parts[0] if modes == 1 else jnp.concatenate(parts, axis=1)


def enter_kernel(groups, tokens_ref, table_ref, send_ref):
    normal, _ = normalize(tokens_ref[...].astype(F32))
    spectrum = dot(table_ref[...], normal.astype(BF16)).astype(BF16)
    scatter_lanes(send_ref, spectrum, groups)


def mix_kernel(
    modes, got_ref, high_ref, back_ref, mats_ref, bias_ref, gain_ref, shift_ref, ones_ref,
    send_ref, hat_ref, modal_ref, inner_ref, active_ref,
):
    width = got_ref.shape[2]
    hat = dot(high_ref[...], gather_modes(got_ref, modes))
    hat_ref[...] = hat
    hat_ref.flush()
    pieces = []
    for k in range(modes):
        piece = hat[:, k * width : (k + 1) * width] * gain_ref[...]
        pieces.append(piece + ones_ref[:, k : k + 1] * shift_ref[...])
    modal = pieces[0] if modes == 1 else jnp.concatenate(pieces, axis=1)
    modal = to_mix_rows(modal.astype(BF16), modes, width)
    modal_ref[...] = modal
    modal_ref.flush()
    inner = dot(modal, mats_ref[0]) + bias_ref[0:1, :]
    inner_ref[...] = inner
    inner_ref.flush()
    active = gelu_value(inner).astype(BF16)
    active_ref[...] = active
    active_ref.flush()
    outer = (dot(active, mats_ref[1]) + bias_ref[1:2, :]).astype(BF16)
    gridded = dot(back_ref[...], from_mix_rows(outer, modes, width)).astype(BF16)
    scatter_modes(send_ref, gridded, modes)


def fold(grad, width, block):
    real = grad[:width, :width] + grad[width:, width:]
    imag = grad[:width, width:] - grad[width:, :width]
    out = []
    for part in (real, imag):
        if width == block:
            out.append(part)
        else:
            lane = lax.broadcasted_iota(jnp.int32, (block, width), 1)
            out.append(jnp.where(lane < block, part[:block], part[block:]))
    return jnp.concatenate(out, axis=0)


def by_block(sums, width, block):
    real, imag = sums[:, :width], sums[:, width:]
    if width == block:
        return [real, imag]
    lane = lax.broadcasted_iota(jnp.int32, real.shape, 1)
    turned_real, turned_imag = pltpu.roll(real, block, 1), pltpu.roll(imag, block, 1)
    return [jnp.where(lane < block, real, turned_imag), jnp.where(lane < block, turned_real, imag)]


def unmix_kernel(
    modes, block, place_ref, got_ref, high_ref, back_ref, mats_ref, ones_ref, hat_ref, modal_ref, inner_ref, active_ref,
    mlp_ref, send_ref, keep_ref, give_ref,
):
    width = got_ref.shape[2]
    grad_outer = dot(high_ref[...], gather_modes(got_ref, modes)).astype(BF16)
    grad_outer = to_mix_rows(grad_outer, modes, width)
    _, slope = gelu_pair(inner_ref[...])
    grad_inner = (dot_nt(grad_outer, mats_ref[1]) * slope).astype(BF16)
    grad_modal = dot_nt(grad_inner, mats_ref[0]).astype(BF16)
    grad_modal = from_mix_rows(grad_modal, modes, width)
    spectrum = dot(back_ref[...], grad_modal).astype(BF16)
    scatter_modes(send_ref, spectrum, modes)
    send_ref.flush()
    rows = 2 * block
    grads = [fold(dot_tn(modal_ref[...], grad_inner), width, block)]
    grads.append(fold(dot_tn(active_ref[...], grad_outer), width, block))
    bias_one = by_block(jnp.sum(grad_inner.astype(F32), axis=0, keepdims=True), width, block)
    bias_two = by_block(jnp.sum(grad_outer.astype(F32), axis=0, keepdims=True), width, block)
    gain = jnp.zeros((1, width), F32)
    shift = jnp.zeros((1, width), F32)
    for k in range(modes):
        lanes = slice(k * width, (k + 1) * width)
        upstream = grad_modal[:, lanes].astype(F32)
        gain = gain + jnp.sum(upstream * hat_ref[:, lanes], axis=0, keepdims=True)
        shift = shift + jnp.sum(upstream * ones_ref[:, k : k + 1], axis=0, keepdims=True)
    tail = jnp.concatenate(bias_one + bias_two + [gain, shift, jnp.zeros((2, width), F32)], axis=0)
    mlp = [mlp_ref[:, q : q + width] for q in range(0, mlp_ref.shape[1], width)]
    count = len(mlp) // 2
    rows = keep_ref.shape[0] - 2 * block - 8 - 8 * count
    rest = [jnp.zeros((rows, width), F32)] if rows else []
    for half, parts in enumerate(([grads[0], tail] + mlp[:count], [grads[1], jnp.zeros_like(tail)] + mlp[count:])):
        message = jnp.concatenate(parts + rest, axis=0).astype(BF16)
        for ref, core in ((keep_ref, half), (give_ref, 1 - half)):

            @pl.when(place_ref[0] == core)
            def _(ref=ref, message=message):
                ref[...] = message


def add_up(*values):
    total = values[0].astype(F32)
    for value in values[1:]:
        total = total + value.astype(F32)
    return total


def first_kernel(kept_ref, one_ref, in_ref, out_ref):
    for part, ref in enumerate((in_ref, out_ref)):
        ref[...] = add_up(kept_ref[part, 1], one_ref[part]).astype(BF16)


def second_kernel(kept_ref, in_ref, out_ref, mine_ref, core_ref, one_ref, small_ref, y_ref, x_ref):
    small_ref[...] = add_up(mine_ref[...], core_ref[...]).astype(BF16)
    for part, source, ref in ((0, in_ref, y_ref), (1, out_ref, x_ref)):
        ref[...] = add_up(kept_ref[part, 0, 1], one_ref[part], source[1]).astype(BF16)


def third_kernel(place_ref, kept_ref, in_ref, out_ref, y_ref, x_ref, *refs):
    small_refs, (one_ref, line_ref, own_ref), away_refs = refs[:4], refs[4:7], refs[7:]
    for z, ref in enumerate(small_refs):
        line_ref[(place_ref[0] >> 3) ^ z] = ref[...]
    for part, source, last in ((0, in_ref, y_ref), (1, out_ref, x_ref)):
        for z in range(4):
            total = add_up(kept_ref[part, 0, 0, z], one_ref[part, z], source[0, z], last[z])
            if z == 0:
                own_ref[part] = total
            else:
                away_refs[z - 1][part] = total.astype(BF16)


def plane_kernel(mine_ref, x_ref, y_ref, other_ref, total_ref):
    total_ref[...] = (add_up(mine_ref[...], x_ref[...]) + add_up(y_ref[...], other_ref[...])).astype(BF16)


def step_rest(
    block, scale, place_ref, own_ref, other_ref, mixer_ref, moment_ref, average_ref, vectors_ref, vec_moment_ref,
    vec_average_ref, new_mixer, new_moment, new_average, new_vectors, new_vec_moment, new_vec_average, grad_ref,
):
    groups, _, width = own_ref.shape
    joined = width // block
    rows = 2 * block
    slices = groups // 2
    core = place_ref[0]

    def held(half, group, part):
        mine, theirs = own_ref[group, part, :], other_ref[group, part, :]
        return jnp.where(core == half, mine, theirs).astype(F32)

    for group in range(groups):
        for layer in range(2):
            grad = held(layer, group, slice(0, rows)) * scale
            for part in range(2):
                for j in range(joined):
                    b = group * joined + j
                    piece = grad[part * block : (part + 1) * block, j * block : (j + 1) * block]
                    value, moment, average = update(
                        mixer_ref[layer, b, part], piece, moment_ref[layer, b, part], average_ref[layer, b, part],
                        WEIGHT_DECAY,
                    )
                    new_mixer[layer, b, part] = value
                    new_moment[layer, b, part] = moment
                    new_average[layer, b, part] = average
    for ref in (new_mixer, new_moment, new_average):
        ref.flush()
    for group in range(groups):
        tail = held(0, group, slice(rows, rows + 16))
        grad_ref[0:2, group * width : (group + 1) * width] = tail[4:6]
        for layer in range(2):
            for j in range(2):
                b = group * joined + (j if joined == 2 else 0)
                per_row = vectors_ref.shape[1] // (2 * block)
                lane = (b % per_row) * 2 * block + (0 if joined == 2 else j * block)
                row = 9 + layer * 2 + b // per_row
                grad_ref[row : row + 1, lane : lane + width] = tail[2 * layer + j : 2 * layer + j + 1]
    for half in range(2):
        part = slice(rows, rows + 8 + 8 * slices + 8 * ((slices + 1) % 2))
        total = held(half, 0, part)
        for group in range(1, groups):
            total = total + held(half, group, part)
        for q in range(slices):
            lane = (half * slices + q) * width
            grad_ref[2:9, lane : lane + width] = total[8 + 8 * q : 15 + 8 * q]
    value, moment, average = update(
        vectors_ref[...], grad_ref[0:13, :] * scale, vec_moment_ref[...], vec_average_ref[...], 0.0
    )
    new_vectors[...] = value
    new_vec_moment[...] = moment
    new_vec_average[...] = average


def step_all(block, scale, place_ref, *refs):
    step_weights(scale, *refs[:10], *refs[18:26])
    step_rest(block, scale, place_ref, *refs[10:18], *refs[26:])


def step_weights(scale, own_ref, *refs):
    away_refs, weights, new_weights = refs[:3], refs[3:9], refs[9:17]
    for part in range(2):
        total = add_up(own_ref[part], *[ref[part] for ref in away_refs])
        count = weights[part].shape[0]
        for q in range(total.shape[0] // count):
            lanes = slice(q * 128, (q + 1) * 128)
            grad = total[q * count : (q + 1) * count] * scale
            values = update(
                weights[part][:, lanes], grad, weights[2 + part][:, lanes], weights[4 + part][:, lanes], WEIGHT_DECAY
            )
            for i, value in enumerate(values):
                new_weights[2 * i + part][:, lanes] = value
            new_weights[6 + part][:, lanes] = values[0].astype(BF16)
    for ref in new_weights:
        ref.flush()


def load_weights(near, place_ref, pieces, w_in, w_out, sems):
    copies = []
    if not near:
        copies = [(pieces[0].at[:, part], target) for part, target in enumerate((w_in, w_out))]
    else:
        me = place_ref[0]
        at = [(me >> 1) & 1, (me >> 2) & 1, me & 1, me >> 3]
        size = pieces[0].shape[3]
        for i, ref in enumerate(pieces):
            for j in range(2):
                x, y = (i >> 1 & 1, j) if i & 1 else (j, i >> 1 & 1)
                for k in range(2):
                    z = 2 * (i & 1) + k
                    row = (((at[3] ^ z) * 2 + (at[1] ^ y)) * 2 + (at[0] ^ (i >> 2))) * size
                    rows = pl.ds(pl.multiple_of(row, size), size)
                    for part, target in enumerate((w_in, w_out)):
                        copies.append((ref.at[j, k, part], target.at[at[2] ^ x, rows]))
    copies = [pltpu.make_async_copy(source, target, sems.at[i]) for i, (source, target) in enumerate(copies)]
    for copy in copies:
        copy.start()
    return copies


def mlp_kernel(
    groups, near, place_ref, got_ref, wide_t_ref, tokens_ref, cotangent_ref, vectors_ref, bias_ref, wide_ref, *refs
):
    count = 8 if near else 1
    pieces, refs = refs[:count], refs[count:]
    output_ref, middle_ref, send_ref, small_ref, *refs = refs
    grad_refs, refs = refs[:2], refs[2:]
    normed, normed_t, cotangent_t, normal, spread, upstream_ref, w_in, w_out, active, grad_hidden, sems = refs
    copies = load_weights(near, place_ref, pieces, w_in, w_out, sems)
    tokens, width = tokens_ref.shape
    halves, _, columns = w_in.shape
    gain, shift, bias_out = vectors_ref[2:3, :], vectors_ref[3:4, :], vectors_ref[4:5, :]
    row_blocks = [slice(r, r + ROWS) for r in range(0, tokens, ROWS)]
    spectrum = gather_lanes(got_ref, groups)
    bias_out_grad = jnp.zeros((1, width), F32)
    for rows in row_blocks:
        middle = tokens_ref[rows, :].astype(F32) + dot(wide_t_ref[rows, :], spectrum)
        unit, inverse = normalize(middle)
        normal[rows, :] = unit
        spread[rows, :] = inverse
        scaled = (unit * gain + shift).astype(BF16)
        normed[rows, :] = scaled
        normed_t[:, rows] = scaled.T
        middle_ref[rows, :] = middle + bias_out
        upstream = cotangent_ref[rows, :]
        cotangent_t[:, rows] = upstream.T
        bias_out_grad = bias_out_grad + jnp.sum(upstream.astype(F32), axis=0, keepdims=True)
    for copy in copies:
        copy.wait()
    gain_grad = jnp.zeros((1, width), F32)
    shift_grad = jnp.zeros((1, width), F32)
    chunks = [(h, c) for h in range(halves) for c in range(0, columns, CHUNK)]
    bias_grads = [jnp.zeros((1, CHUNK), F32) for _ in chunks]
    for rows in row_blocks:
        for i, (h, c) in enumerate(chunks):
            lanes, flat = slice(c, c + CHUNK), slice(h * columns + c, h * columns + c + CHUNK)
            hidden = dot(normed[rows, :], w_in[h, :, lanes]) + bias_ref[i : i + 1, :]
            value, slope = gelu_pair(hidden)
            active[rows, flat] = value.astype(BF16)
            back = (dot(cotangent_ref[rows, :], w_out[h, :, lanes]) * slope).astype(BF16)
            grad_hidden[rows, flat] = back
            bias_grads[i] = bias_grads[i] + jnp.sum(back.astype(F32), axis=0, keepdims=True)
        total, back = middle_ref[rows, :], None
        for h in range(halves):
            flat = slice(h * columns, (h + 1) * columns)
            total = total + dot_nt(active[rows, flat], w_out[h])
            term = dot_nt(grad_hidden[rows, flat], w_in[h])
            back = term if back is None else back + term
        output_ref[rows, :] = total.astype(BF16)
        unit = normal[rows, :]
        gain_grad = gain_grad + jnp.sum(back * unit, axis=0, keepdims=True)
        shift_grad = shift_grad + jnp.sum(back, axis=0, keepdims=True)
        middle = cotangent_ref[rows, :].astype(F32) + norm_back(back, unit, spread[rows, :], gain)
        middle_ref[rows, :] = middle
        upstream_ref[rows, :] = middle.astype(BF16)
    output_ref.flush()
    middle_ref.flush()
    small_ref[0:3, :] = jnp.concatenate([gain_grad, shift_grad, bias_out_grad], axis=0)
    small_ref[3:7, :] = jnp.concatenate(bias_grads, axis=0)
    small_ref[7:8, :] = jnp.zeros((1, width), F32)
    spectrum = dot(wide_ref[...], upstream_ref[...]).astype(BF16)
    scatter_lanes(send_ref, spectrum, groups)
    send_ref.flush()
    for i, (h, c) in enumerate(chunks):
        flat = slice(h * columns + c, h * columns + c + CHUNK)
        grads = [
            dot(normed_t[...], grad_hidden[:, flat]).astype(BF16), dot(cotangent_t[...], active[:, flat]).astype(BF16)
        ]
        if not near:
            for ref, grad in zip(grad_refs, grads, strict=True):
                ref[h, :, c : c + CHUNK] = grad
            continue
        me = place_ref[0]
        at = [(me >> 1) & 1, (me >> 2) & 1, me & 1, me >> 3]
        size = w_in.shape[1] // 16
        x = h ^ at[2]
        for core in range(2):
            for ref, mine in ((grad_refs[0], core), (grad_refs[1], 1 - core)):

                @pl.when(at[0] == mine)
                def _(ref=ref, core=core, c=c, x=x, grads=grads):
                    for z in range(4):
                        for y in range(2):
                            rows = slice(((z * 2 + y) * 2 + core) * size, ((z * 2 + y) * 2 + core + 1) * size)
                            for q in range(CHUNK // 128):
                                lanes = slice(q * 128, (q + 1) * 128)
                                place = slice((c // 128 + q) * size, (c // 128 + q + 1) * size)
                                ref[0, x, y ^ at[1], z ^ at[3], place, :] = grads[0][rows, lanes]
                                ref[1, y ^ at[1], x, z ^ at[3], place, :] = grads[1][rows, lanes]


def leave_kernel(groups, got_ref, tokens_ref, middle_ref, vectors_ref, table_ref, out_ref):
    spectrum = gather_lanes(got_ref, groups)
    for start in range(0, tokens_ref.shape[0], ROWS):
        rows = slice(start, start + ROWS)
        upstream = dot(table_ref[rows, :], spectrum)
        unit, inverse = normalize(tokens_ref[rows, :].astype(F32))
        back = norm_back(upstream, unit, inverse, vectors_ref[0:1, :])
        out_ref[rows, :] = (middle_ref[rows, :] + back).astype(BF16)


def update(weight, gradient, moment, average, decay_rate):
    step_grad = gradient + decay_rate * weight
    new_moment = MOMENTUM * moment + step_grad
    new_weight = weight - LEARNING_RATE * (step_grad + MOMENTUM * new_moment)
    new_average = AVERAGE * average + (1.0 - AVERAGE) * new_weight
    return (new_weight, new_moment, new_average)


class Source:
    def __init__(self, ref, copy):
        self.ref, self.copy, self.shape = ref, copy, ref.shape

    def __getitem__(self, index):
        if self.copy is not None:
            self.copy.wait()
            self.copy = None
        return self.ref[index]


class Sink:
    def __init__(self, ref, copy):
        self.ref, self.copy, self.shape, self.sent = ref, copy, ref.shape, False

    def __getitem__(self, index):
        return self.ref[index]

    def __setitem__(self, index, value):
        self.ref[index] = value

    def flush(self):
        if not self.sent:
            self.copy.start()
            self.sent = True


class Far:
    def __init__(self, *what):
        self.what = what


def call(body, outs, *args, scalars=(), raw=(), scratch=(), flops=0, carry=(), cost=None, vmem=20):
    near, far, there = [pl.BlockSpec(memory_space=m) for m in (pltpu.VMEM, pltpu.HBM, pl.ANY)]
    in_far, out_far = [isinstance(a, Far) for a in args], [isinstance(o, Far) for o in outs]
    index = [a.what[1:] if f else () for a, f in zip(args, in_far, strict=True)]
    args = [
        pltpu.with_memory_space_constraint(*((a.what[0], pltpu.HBM) if f else (a, pltpu.VMEM)))
        for a, f in zip(args, in_far, strict=True)
    ]
    raw = [pltpu.with_memory_space_constraint(a, pltpu.HBM) for a in raw]
    outs = [o.what if f else o for o, f in zip(outs, out_far, strict=True)]
    outs = [jax.ShapeDtypeStruct(s, d) for s, d in outs]
    n_scalar, n_in, n_raw, n_carry, n_out = len(scalars), len(args), len(raw), len(carry), len(outs)
    shapes = [np.empty(a.shape, np.bool_)[i].shape if i else a.shape for a, i in zip(args, index, strict=True)]
    shapes += [o.shape for o in outs]
    buffers = [
        pltpu.VMEM(shape, a.dtype) for shape, a, f in zip(shapes, args + outs, in_far + out_far, strict=True) if f
    ]

    def inner(*refs):
        refs = list(refs)

        def take(count):
            taken = refs[:count]
            del refs[:count]
            return taken

        scalar_refs, in_refs, raw_refs, _, out_refs, _ = [
            take(n) for n in (n_scalar, n_in, n_raw, n_carry, n_out, n_carry)
        ]
        space = take(len(buffers))
        sems = take(1)[0] if buffers else None
        sources, sinks, used = [], [], 0
        for ref, away, part in zip(in_refs, in_far, index, strict=True):
            if away:
                copy = pltpu.make_async_copy(ref.at[part] if part else ref, space[used], sems.at[used])
                copy.start()
                ref = Source(space[used], copy)
                used += 1
            sources.append(ref)
        for ref, away in zip(out_refs, out_far, strict=True):
            if away:
                ref = Sink(space[used], pltpu.make_async_copy(space[used], ref, sems.at[used]))
                used += 1
            sinks.append(ref)
        body(*scalar_refs, *sources, *raw_refs, *sinks, *refs)
        for source in sources:
            if isinstance(source, Source) and source.copy is not None:
                source.copy.wait()
        sinks = [sink for sink in sinks if isinstance(sink, Sink)]
        for sink in sinks:
            sink.flush()
        for sink in sinks:
            sink.copy.wait()

    every = list(args) + list(raw)
    size = sum(math.prod(a.shape) * a.dtype.itemsize for a in every + outs) if cost is None else cost
    sems = [pltpu.SemaphoreType.DMA((len(buffers),))] if buffers else []
    return pl.pallas_call(
        inner,
        out_shape=[(pltpu.HBM if f else pltpu.VMEM)(o.shape, o.dtype) for o, f in zip(outs, out_far, strict=True)]
        + [jax.ShapeDtypeStruct(a.shape, a.dtype) for a in carry],
        in_specs=[pl.BlockSpec(memory_space=pltpu.SMEM)] * n_scalar
        + [far if f else near for f in in_far]
        + [far] * n_raw
        + [there] * n_carry,
        out_specs=[far if f else near for f in out_far] + [there] * n_carry,
        scratch_shapes=buffers + sems + list(scratch),
        input_output_aliases={n_scalar + n_in + n_raw + i: n_out + i for i in range(n_carry)},
        compiler_params=pltpu.CompilerParams(vmem_limit_bytes=vmem << 20),
        cost_estimate=pl.CostEstimate(flops=flops, bytes_accessed=size, transcendentals=0),
    )(*scalars, *args, *raw, *carry)


def on_device(
    tokens, cotangent, w_in, w_out, mixer_weights, vectors, w_in_moment, w_out_moment, mixer_moment, vectors_moment,
    w_in_average, w_out_average, mixer_average, vectors_average,
):
    sp_count, tp_count = lax.axis_size("sp"), lax.axis_size("tp")
    devices = sp_count * tp_count
    grid_rows, grid, width = tokens.shape
    local = grid_rows * grid
    items = grid_rows * devices // grid
    block_count, block = mixer_weights.shape[1], mixer_weights.shape[3]
    hidden = w_in.shape[1] * tp_count
    model = w_in.shape[0] * sp_count
    lanes = 2 * block if devices * 2 * block <= MODES * width else block
    groups = width // lanes
    per_group = devices // groups
    modes = MODES // per_group
    joined = lanes // block
    scale = 1.0 / math.sqrt(local * devices)
    wide_f, wide_i, high, ones = expanded_tables(grid, grid_rows, items)
    me = lax.axis_index("sp") * tp_count + lax.axis_index("tp")
    group = me // per_group
    exchange = functools.partial(lax.all_to_all, axis_name=AXES, split_axis=0, concat_axis=0, tiled=True)
    chunk = (devices, modes * grid_rows * 2, lanes)
    rows_all = tokens.reshape(local, width)
    upstream_all = cotangent.reshape(local, width)
    shard_rows, shard_columns = w_in.shape
    shard_size = shard_rows * shard_columns // 128
    near = devices == 32 and per_group == 8 and shard_rows % 16 == 0

    def permute(values, mask):
        return lax.ppermute(values, AXES, [(d, d ^ mask) for d in range(devices)])

    pair = jnp.stack([w_in.astype(BF16), w_out.astype(BF16)])
    if near:
        line = [pair] + [permute(pair, 8 * z) for z in (1, 2, 3)]
        carried = [jnp.stack([v, permute(v, m)]) for v, m in ((jnp.stack(line[:2]), 1), (jnp.stack(line[2:]), 4))]
    else:
        weights = lax.all_gather(pair, "sp", axis=1, tiled=True)
        pieces, carried = [lax.all_gather(weights, "tp")], []

    own_mixer = lax.dynamic_slice_in_dim(mixer_weights, group * joined, joined, 1).astype(BF16)
    eye = jnp.eye(joined, dtype=BF16)
    real = jnp.einsum("lbio,bc->lbico", own_mixer[:, :, 0], eye).reshape(2, lanes, lanes)
    imag = jnp.einsum("lbio,bc->lbico", own_mixer[:, :, 1], eye).reshape(2, lanes, lanes)
    mats = jnp.concatenate(
        [jnp.concatenate([real, imag], axis=2), jnp.concatenate([-imag, real], axis=2)], axis=1
    )
    own_bias = lax.dynamic_slice_in_dim(
        vectors[9:13].reshape(2, block_count, 2, block), group * joined, joined, 1
    )
    own_bias = jnp.swapaxes(own_bias, 1, 2).reshape(2, 2 * lanes)
    own_gain = lax.dynamic_slice_in_dim(vectors[0:1], group * lanes, lanes, 1)
    own_shift = lax.dynamic_slice_in_dim(vectors[1:2], group * lanes, lanes, 1)
    ones = jnp.asarray(np.swapaxes(ones.reshape(per_group, modes, -1), 1, 2))
    own_ones = lax.dynamic_index_in_dim(ones, me % per_group, 0, keepdims=False)

    wide_f, wide_f_t = jnp.asarray(wide_f), jnp.asarray(wide_f.T)
    wide_i, wide_i_t = jnp.asarray(wide_i), jnp.asarray(wide_i.T)
    high, high_t = jnp.asarray(high), jnp.asarray(high.T)
    wide_flops = 2 * wide_f.shape[0] * wide_f.shape[1] * width
    (sent,) = call(
        functools.partial(enter_kernel, groups), [(chunk, BF16)], Far(rows_all), Far(wide_f), flops=wide_flops
    )
    got = exchange(sent)
    half_rows = items * MODES
    sent, hat, modal, inner, active, *carried = call(
        functools.partial(mix_kernel, modes),
        [
            (chunk, BF16),
            Far((2 * half_rows, modes * lanes), F32),
            Far((modes * half_rows, 2 * lanes), BF16),
            Far((modes * half_rows, 2 * lanes), F32),
            Far((modes * half_rows, 2 * lanes), BF16),
        ],
        got, high, high_t, mats, own_bias, own_gain, own_shift, own_ones,
        carry=carried,
    )
    if near:
        pieces = carried + [permute(carried[0], 4), permute(carried[1], 1)]
        pieces += [permute(p, 2) for p in pieces]
    got = exchange(sent)
    steps = hidden // CHUNK
    grads = [((2, 2, 2, 4, shard_size, 128), BF16)] * 2 if near else [((tp_count, model, shard_columns), BF16)] * 2
    output, middle, sent, mlp_small, *grads = call(
        functools.partial(mlp_kernel, groups, near),
        [Far((local, width), BF16), Far((local, width), F32), Far(chunk, BF16), ((8, width), F32)] + grads,
        Far(got), Far(wide_i_t), Far(rows_all), Far(upstream_all), vectors, vectors[5:9].reshape(steps, CHUNK), Far(wide_i),
        scalars=[me[None]], raw=pieces,
        scratch=[
            pltpu.VMEM((local, width), BF16),
            pltpu.VMEM((width, local), BF16),
            pltpu.VMEM((width, local), BF16),
            pltpu.VMEM((local, width), F32),
            pltpu.VMEM((local, 1), F32),
            pltpu.VMEM((local, width), BF16),
            pltpu.VMEM((tp_count, model, shard_columns), BF16),
            pltpu.VMEM((tp_count, model, shard_columns), BF16),
            pltpu.VMEM((local, hidden), BF16),
            pltpu.VMEM((local, hidden), BF16),
            pltpu.SemaphoreType.DMA((64 if near else 2,)),
        ],
        flops=12 * local * width * hidden + 2 * wide_flops, vmem=44,
    )

    carried = []
    if near:
        shard = (4, shard_size, 128)
        kept, one = grads[0], permute(grads[1], 2)
        sent_in, sent_out = call(
            first_kernel, [((2,) + shard, BF16)] * 2, kept, Far(one, slice(None), 1), cost=0
        )
        carried = [permute(sent_in, 1), permute(sent_out, 4)]

    got = exchange(sent)
    small_rows = -(-(2 * block + 8 + 8 * (groups // 2)) // 16) * 16
    place = ((me >> 1) & 1 if near else jnp.int32(0))[None]
    sent, small, given = call(
        functools.partial(unmix_kernel, modes, block),
        [Far(chunk, BF16), ((small_rows, lanes), BF16), ((small_rows, lanes), BF16)],
        got, Far(high), Far(high_t), Far(mats), own_ones, Far(hat), Far(modal), Far(inner), Far(active), mlp_small,
        scalars=[place], cost=COST, vmem=20 if near else 48,
    )
    if near:
        both = slice(None)
        small, over_y, over_x = call(
            second_kernel, [((small_rows, lanes), BF16)] + [(shard, BF16)] * 2,
            kept, *carried, small, permute(given, 2), Far(one, both, 0, 1), cost=0,
        )
        line, own, *away = call(
            third_kernel,
            [((4, small_rows, lanes), BF16), ((2, shard_size, 128), F32)] + [((2, shard_size, 128), BF16)] * 3,
            kept, *carried, permute(over_y, 4), permute(over_x, 1),
            small, *[permute(small, 8 * z) for z in (1, 2, 3)], Far(one, both, 0, 0),
            scalars=[me[None]], cost=0,
        )
        away = [permute(a, 8 * (z + 1)) for z, a in enumerate(away)]
    got = exchange(sent)
    (grad_tokens,) = call(
        functools.partial(leave_kernel, groups),
        [Far((local, width), BF16)],
        got, Far(rows_all), Far(middle), vectors, Far(wide_f_t), cost=COST,
    )

    if near:
        line, *away, grad_tokens = call(
            plane_kernel, [(line.shape, BF16)], line, *[permute(line, m) for m in (1, 4, 5)], cost=0, carry=[*away, grad_tokens]
        )
        other = permute(line, 2)

    state = [mixer_weights, mixer_moment, mixer_average, vectors, vectors_moment, vectors_average]
    new_state = [Far(a.shape, F32) for a in state]
    if near:
        weights = [w_in, w_out, w_in_moment, w_out_moment, w_in_average, w_out_average]
        *stepped, grad_tokens = call(
            functools.partial(step_all, block, scale),
            [Far(w_in.shape, F32)] * 6 + [Far(w_in.shape, BF16)] * 2 + new_state,
            own, *away, *weights, line, other, *state,
            scalars=[place], scratch=[pltpu.VMEM((16, width), F32)], carry=[grad_tokens], cost=0,
        )
        new_in, new_out = stepped[0:8:2], stepped[1:8:2]
        stepped = stepped[8:]
    else:
        grads = jnp.stack(grads).astype(F32)
        grads = lax.psum_scatter(grads, "tp", scatter_dimension=1, tiled=True)
        grads = lax.psum_scatter(grads, "sp", scatter_dimension=2, tiled=True)
        new_in = update(w_in, grads[0, 0] * scale, w_in_moment, w_in_average, WEIGHT_DECAY)
        new_out = update(w_out, grads[1, 0] * scale, w_out_moment, w_out_average, WEIGHT_DECAY)
        new_in, new_out = new_in + (new_in[0].astype(BF16),), new_out + (new_out[0].astype(BF16),)
        onehot = (jnp.arange(groups, dtype=jnp.int32) == group).astype(F32)[:, None, None]
        line, other = lax.psum((onehot * small.astype(F32), onehot * given.astype(F32)), AXES)
        stepped = call(
            functools.partial(step_rest, block, scale), new_state, line, other, *state,
            scalars=[place], scratch=[pltpu.VMEM((16, width), F32)],
        )
    new_mix, new_vec = stepped[0:3], stepped[3:6]
    shape = tokens.shape
    return (
        output.reshape(shape), grad_tokens.reshape(shape),
        new_in[0], new_out[0], new_mix[0], new_vec[0],
        new_in[1], new_out[1], new_mix[1], new_vec[1],
        new_in[2], new_out[2], new_mix[2], new_vec[2],
        new_in[3], new_out[3],
    )


def solution(mesh):
    rows, split, whole = P(AXES, None, None), P("sp", "tp"), P()
    state = (split, split, whole, whole)
    return jax.shard_map(
        on_device,
        mesh=mesh,
        in_specs=(rows, rows) + state * 3,
        out_specs=(rows, rows) + state * 3 + (split, split),
        check_vma=False,
    )
```

```python
import functools
import math

import jax
import jax.numpy as jnp
import ml_dtypes
import numpy as np
from jax import lax
from jax.experimental import pallas as pl
from jax.experimental.pallas import tpu as pltpu
from jax.sharding import PartitionSpec as P

MODES = 32
EPSILON = 1e-05
LEARNING_RATE = 0.05
MOMENTUM = 0.9
WEIGHT_DECAY = 0.0001
AVERAGE = 0.75
GELU_SCALE = math.sqrt(2.0 / math.pi)
GELU_CUBE = 0.044715
CHUNK = 512
ROWS = 256
SPAN = 4
BF16 = jnp.bfloat16
F32 = jnp.float32
AXES = ("sp", "tp")
COST = 60 << 20
OUT_BLOCKS = 4


def dft_tables(grid):
    positions = np.arange(grid)
    wave = np.arange(MODES)
    root = np.float32(1.0 / math.sqrt(grid))
    step = np.float32(2.0 * math.pi / grid)
    phase_w = (positions[:, None] * wave[None, :] % grid).astype(np.float32) * step
    factor = np.where(wave == 0, 1.0, 2.0).astype(np.float32)
    cos_w, sin_w = np.cos(phase_w) * root, np.sin(phase_w) * root
    forward_w = np.stack([cos_w, -sin_w], axis=1)
    inverse_w = np.stack([cos_w * factor, -sin_w * factor], axis=1)
    frequency = np.where(wave < MODES // 2, wave, wave - MODES)
    phase_h = (frequency[:, None] * positions[None, :] % grid).astype(np.float32) * step
    cos_h, sin_h = np.cos(phase_h) * root, np.sin(phase_h) * root
    forward_h = np.stack([np.stack([cos_h, -sin_h], -1), np.stack([sin_h, cos_h], -1)], -2)
    return [t.astype(ml_dtypes.bfloat16) for t in (forward_w, inverse_w, forward_h)]


def expanded_tables(grid, items):
    forward_w, inverse_w, forward_h = [t.astype(np.float32) for t in dft_tables(grid)]
    eye_r = np.eye(SPAN, dtype=np.float32)
    wide_f = np.einsum("wek,rs->kresw", forward_w, eye_r).reshape(-1, SPAN * grid)
    wide_i = np.einsum("wek,rs->kresw", inverse_w, eye_r).reshape(-1, SPAN * grid)
    eye_i = np.eye(items, dtype=np.float32)
    high = np.einsum("mhef,ij->fimhje", forward_h, eye_i).reshape(2 * items * MODES, -1)
    ones = np.einsum("mhef,ek->kfm", forward_h.astype(np.float64), forward_w.astype(np.float64).sum(0))
    ones = np.repeat(ones[:, :, None], items, axis=2).reshape(MODES, -1).astype(np.float32)
    cast = [t.astype(ml_dtypes.bfloat16) for t in (wide_f, wide_i, high)]
    return cast[0], cast[1], cast[2], ones


def dot(left, right):
    return jnp.dot(left, right, preferred_element_type=F32)


def dot_nt(left, right):
    return lax.dot_general(left, right, (((1,), (1,)), ((), ())), preferred_element_type=F32)


def dot_tn(left, right):
    return lax.dot_general(left, right, (((0,), (0,)), ((), ())), preferred_element_type=F32)


def normalize(values):
    center = values - jnp.mean(values, axis=-1, keepdims=True)
    inverse = lax.rsqrt(jnp.mean(center * center, axis=-1, keepdims=True) + EPSILON)
    return center * inverse, inverse


def norm_back(upstream, normal, inverse, gain):
    scaled = upstream * gain
    centered = scaled - jnp.mean(scaled, axis=-1, keepdims=True)
    centered = centered - normal * jnp.mean(scaled * normal, axis=-1, keepdims=True)
    return centered * inverse


def gelu_pair(values):
    square = values * values
    bent = jnp.tanh(values * (GELU_SCALE + (GELU_SCALE * GELU_CUBE) * square))
    half = 0.5 + 0.5 * bent
    slope = half + (values * half) * (1.0 - bent) * (GELU_SCALE + (3.0 * GELU_SCALE * GELU_CUBE) * square)
    return values * half, slope


def gelu_value(values):
    square = values * values
    bent = jnp.tanh(values * (GELU_SCALE + (GELU_SCALE * GELU_CUBE) * square))
    return values * (0.5 + 0.5 * bent)


def along_w(table_ref, values, rows):
    table = table_ref[...]
    span = table.shape[1]
    parts = [dot(table, values[r : r + span]).reshape(MODES, -1, values.shape[1]) for r in range(0, rows, span)]
    return jnp.concatenate(parts, axis=1).reshape(-1, values.shape[1]).astype(BF16)


def spans(spectrum):
    whole = spectrum.astype(F32).reshape(MODES, -1, spectrum.shape[1])
    size = 2 * SPAN
    return [
        whole[:, r : r + size].reshape(MODES * size, -1).astype(BF16) for r in range(0, whole.shape[1], size)
    ]


def gather_lanes(ref, groups):
    count = ref.shape[0] // groups
    width = ref.shape[2]
    parts = [ref[g * count : (g + 1) * count].reshape(count * ref.shape[1], width) for g in range(groups)]
    return parts[0] if groups == 1 else jnp.concatenate(parts, axis=1)


def scatter_lanes(ref, values, groups):
    count = ref.shape[0] // groups
    width = ref.shape[2]
    for g in range(groups):
        piece = values[:, g * width : (g + 1) * width]
        ref[g * count : (g + 1) * count] = piece.reshape(count, ref.shape[1], width)


def gather_modes(ref, modes):
    rows = ref.shape[1] // modes
    parts = [
        ref[:, k * rows : (k + 1) * rows, :].reshape(ref.shape[0] * rows, ref.shape[2]) for k in range(modes)
    ]
    return parts[0] if modes == 1 else jnp.concatenate(parts, axis=1)


def scatter_modes(ref, values, modes):
    rows = ref.shape[1] // modes
    width = ref.shape[2]
    for k in range(modes):
        piece = values[:, k * width : (k + 1) * width]
        ref[:, k * rows : (k + 1) * rows, :] = piece.reshape(ref.shape[0], rows, width)


def to_mix_rows(values, modes, width):
    half = values.shape[0] // 2
    parts = []
    for k in range(modes):
        piece = values[:, k * width : (k + 1) * width]
        parts.append(jnp.concatenate([piece[:half], piece[half:]], axis=1))
    return parts[0] if modes == 1 else jnp.concatenate(parts, axis=0)


def from_mix_rows(values, modes, width):
    half = values.shape[0] // modes
    parts = []
    for k in range(modes):
        piece = values[k * half : (k + 1) * half]
        parts.append(jnp.concatenate([piece[:, :width], piece[:, width:]], axis=0))
    return parts[0] if modes == 1 else jnp.concatenate(parts, axis=1)


def enter_kernel(groups, tokens_ref, table_ref, send_ref):
    normal, _ = normalize(tokens_ref[...].astype(F32))
    scatter_lanes(send_ref, along_w(table_ref, normal.astype(BF16), normal.shape[0]), groups)


def mix_kernel(
    modes, got_ref, high_ref, back_ref, mats_ref, bias_ref, gain_ref, shift_ref, ones_ref,
    send_ref, hat_ref, modal_ref, inner_ref, active_ref,
):
    width = got_ref.shape[2]
    hat = dot(high_ref[...], gather_modes(got_ref, modes))
    hat_ref[...] = hat
    hat_ref.flush()
    pieces = []
    for k in range(modes):
        piece = hat[:, k * width : (k + 1) * width] * gain_ref[...]
        pieces.append(piece + ones_ref[:, k : k + 1] * shift_ref[...])
    modal = pieces[0] if modes == 1 else jnp.concatenate(pieces, axis=1)
    modal = to_mix_rows(modal.astype(BF16), modes, width)
    modal_ref[...] = modal
    modal_ref.flush()
    inner = dot(modal, mats_ref[0]) + bias_ref[0:1, :]
    inner_ref[...] = inner
    inner_ref.flush()
    active = gelu_value(inner).astype(BF16)
    active_ref[...] = active
    active_ref.flush()
    outer = (dot(active, mats_ref[1]) + bias_ref[1:2, :]).astype(BF16)
    gridded = dot(back_ref[...], from_mix_rows(outer, modes, width)).astype(BF16)
    scatter_modes(send_ref, gridded, modes)


def fold(grad, width, block):
    real = grad[:width, :width] + grad[width:, width:]
    imag = grad[:width, width:] - grad[width:, :width]
    out = []
    for part in (real, imag):
        if width == block:
            out.append(part)
        else:
            lane = lax.broadcasted_iota(jnp.int32, (block, width), 1)
            out.append(jnp.where(lane < block, part[:block], part[block:]))
    return jnp.concatenate(out, axis=0)


def by_block(sums, width, block):
    real, imag = sums[:, :width], sums[:, width:]
    if width == block:
        return [real, imag]
    lane = lax.broadcasted_iota(jnp.int32, real.shape, 1)
    turned_real, turned_imag = pltpu.roll(real, block, 1), pltpu.roll(imag, block, 1)
    return [jnp.where(lane < block, real, turned_imag), jnp.where(lane < block, turned_real, imag)]


def unmix_kernel(
    modes, block, place_ref, got_ref, high_ref, back_ref, mats_ref, ones_ref, hat_ref, modal_ref, inner_ref, active_ref,
    mlp_ref, send_ref, keep_ref, give_ref,
):
    width = got_ref.shape[2]
    grad_outer = dot(high_ref[...], gather_modes(got_ref, modes)).astype(BF16)
    grad_outer = to_mix_rows(grad_outer, modes, width)
    _, slope = gelu_pair(inner_ref[...])
    grad_inner = (dot_nt(grad_outer, mats_ref[1]) * slope).astype(BF16)
    grad_modal = dot_nt(grad_inner, mats_ref[0]).astype(BF16)
    grad_modal = from_mix_rows(grad_modal, modes, width)
    spectrum = dot(back_ref[...], grad_modal).astype(BF16)
    scatter_modes(send_ref, spectrum, modes)
    send_ref.flush()
    rows = 2 * block
    grads = [fold(dot_tn(modal_ref[...], grad_inner), width, block)]
    grads.append(fold(dot_tn(active_ref[...], grad_outer), width, block))
    bias_one = by_block(jnp.sum(grad_inner.astype(F32), axis=0, keepdims=True), width, block)
    bias_two = by_block(jnp.sum(grad_outer.astype(F32), axis=0, keepdims=True), width, block)
    gain = jnp.zeros((1, width), F32)
    shift = jnp.zeros((1, width), F32)
    for k in range(modes):
        lanes = slice(k * width, (k + 1) * width)
        upstream = grad_modal[:, lanes].astype(F32)
        gain = gain + jnp.sum(upstream * hat_ref[:, lanes], axis=0, keepdims=True)
        shift = shift + jnp.sum(upstream * ones_ref[:, k : k + 1], axis=0, keepdims=True)
    tail = jnp.concatenate(bias_one + bias_two + [gain, shift, jnp.zeros((2, width), F32)], axis=0)
    mlp = [mlp_ref[:, q : q + width] for q in range(0, mlp_ref.shape[1], width)]
    count = len(mlp) // 2
    rows = keep_ref.shape[0] - 2 * block - 8 - 8 * count
    rest = [jnp.zeros((rows, width), F32)] if rows else []
    for half, parts in enumerate(([grads[0], tail] + mlp[:count], [grads[1], jnp.zeros_like(tail)] + mlp[count:])):
        message = jnp.concatenate(parts + rest, axis=0).astype(BF16)
        for ref, core in ((keep_ref, half), (give_ref, 1 - half)):

            @pl.when(place_ref[0] == core)
            def _(ref=ref, message=message):
                ref[...] = message


def add_up(*values):
    total = values[0].astype(F32)
    for value in values[1:]:
        total = total + value.astype(F32)
    return total


def first_kernel(kept_ref, one_ref, in_ref, out_ref):
    for part, ref in enumerate((in_ref, out_ref)):
        ref[...] = add_up(kept_ref[part, 1], one_ref[part]).astype(BF16)


def second_kernel(kept_ref, in_ref, out_ref, mine_ref, core_ref, one_ref, small_ref, y_ref, x_ref):
    small_ref[...] = add_up(mine_ref[...], core_ref[...]).astype(BF16)
    for part, source, ref in ((0, in_ref, y_ref), (1, out_ref, x_ref)):
        ref[...] = add_up(kept_ref[part, 0, 1], one_ref[part], source[...]).astype(BF16)


def third_kernel(place_ref, kept_ref, in_ref, out_ref, y_ref, x_ref, *refs):
    small_refs, (one_ref, line_ref, own_ref), away_refs = refs[:4], refs[4:7], refs[7:]
    for z, ref in enumerate(small_refs):
        line_ref[(place_ref[0] >> 3) ^ z] = ref[...]
    for part, source, last in ((0, in_ref, y_ref), (1, out_ref, x_ref)):
        for z in range(4):
            total = add_up(kept_ref[part, 0, 0, z], one_ref[part, z], source[z], last[z])
            if z == 0:
                own_ref[part] = total
            else:
                away_refs[z - 1][part] = total.astype(BF16)


def plane_kernel(mine_ref, x_ref, y_ref, other_ref, total_ref):
    total_ref[...] = (add_up(mine_ref[...], x_ref[...]) + add_up(y_ref[...], other_ref[...])).astype(BF16)


def step_rest(
    block, scale, place_ref, own_ref, other_ref, mixer_ref, moment_ref, average_ref, vectors_ref, vec_moment_ref,
    vec_average_ref, new_mixer, new_moment, new_average, new_vectors, new_vec_moment, new_vec_average, grad_ref,
):
    groups, _, width = own_ref.shape
    joined = width // block
    rows = 2 * block
    slices = groups // 2
    core = place_ref[0]

    def held(half, group, part):
        mine, theirs = own_ref[group, part, :], other_ref[group, part, :]
        return jnp.where(core == half, mine, theirs).astype(F32)

    for group in range(groups):
        for layer in range(2):
            grad = held(layer, group, slice(0, rows)) * scale
            for part in range(2):
                for j in range(joined):
                    b = group * joined + j
                    piece = grad[part * block : (part + 1) * block, j * block : (j + 1) * block]
                    value, moment, average = update(
                        mixer_ref[layer, b, part], piece, moment_ref[layer, b, part], average_ref[layer, b, part],
                        WEIGHT_DECAY,
                    )
                    new_mixer[layer, b, part] = value
                    new_moment[layer, b, part] = moment
                    new_average[layer, b, part] = average
    for ref in (new_mixer, new_moment, new_average):
        ref.flush()
    for group in range(groups):
        tail = held(0, group, slice(rows, rows + 16))
        grad_ref[0:2, group * width : (group + 1) * width] = tail[4:6]
        for layer in range(2):
            for j in range(2):
                b = group * joined + (j if joined == 2 else 0)
                per_row = vectors_ref.shape[1] // (2 * block)
                lane = (b % per_row) * 2 * block + (0 if joined == 2 else j * block)
                row = 9 + layer * 2 + b // per_row
                grad_ref[row : row + 1, lane : lane + width] = tail[2 * layer + j : 2 * layer + j + 1]
    for half in range(2):
        part = slice(rows, rows + 8 + 8 * slices + 8 * ((slices + 1) % 2))
        total = held(half, 0, part)
        for group in range(1, groups):
            total = total + held(half, group, part)
        for q in range(slices):
            lane = (half * slices + q) * width
            grad_ref[2:9, lane : lane + width] = total[8 + 8 * q : 15 + 8 * q]
    value, moment, average = update(
        vectors_ref[...], grad_ref[0:13, :] * scale, vec_moment_ref[...], vec_average_ref[...], 0.0
    )
    new_vectors[...] = value
    new_vec_moment[...] = moment
    new_vec_average[...] = average


def step_all(block, scale, place_ref, *refs):
    step_rest(block, scale, place_ref, *refs[10:18], *refs[26:])
    step_weights(scale, *refs[:10], *refs[18:26])


def step_weights(scale, own_ref, *refs):
    away_refs, weights, new_weights = refs[:3], refs[3:9], refs[9:17]
    for part in range(2):
        total = add_up(own_ref[part], *[ref[part] for ref in away_refs])
        count = weights[part].shape[0]
        for q in range(total.shape[0] // count):
            lanes = slice(q * 128, (q + 1) * 128)
            grad = total[q * count : (q + 1) * count] * scale
            values = update(
                weights[part][:, lanes], grad, weights[2 + part][:, lanes], weights[4 + part][:, lanes], WEIGHT_DECAY
            )
            for i, value in enumerate(values):
                new_weights[2 * i + part][:, lanes] = value
            new_weights[6 + part][:, lanes] = values[0].astype(BF16)
    for ref in new_weights:
        ref.flush()


def load_weights(near, place_ref, pieces, targets, sems):
    copies = []
    if not near:
        copies = [(pieces[0].at[:, part], target) for part, target in targets]
    else:
        me = place_ref[0]
        at = [(me >> 1) & 1, (me >> 2) & 1, me & 1, me >> 3]
        size = pieces[0].shape[3]
        for i, ref in enumerate(pieces):
            for j in range(2):
                x, y = (i >> 1 & 1, j) if i & 1 else (j, i >> 1 & 1)
                for k in range(2):
                    z = 2 * (i & 1) + k
                    row = (((at[3] ^ z) * 2 + (at[1] ^ y)) * 2 + (at[0] ^ (i >> 2))) * size
                    rows = pl.ds(pl.multiple_of(row, size), size)
                    for part, target in targets:
                        copies.append((ref.at[j, k, part], target.at[at[2] ^ x, rows]))
    copies = [pltpu.make_async_copy(source, target, sems.at[i]) for i, (source, target) in enumerate(copies)]
    for copy in copies:
        copy.start()
    return copies


def place_rows(ref, values, columns, orders):
    if not orders:
        ref[:, columns] = values
        return
    size = values.shape[0] // len(orders)
    for block, order in enumerate(orders):
        ref[pl.ds(pl.multiple_of(order * size, size), size), columns] = values[block * size : (block + 1) * size]


def mlp_kernel(
    groups, near, place_ref, got_ref, wide_t_ref, tokens_ref, cotangent_ref, vectors_ref, bias_ref, wide_ref, *refs
):
    count = 8 if near else 1
    pieces, refs = refs[:count], refs[count:]
    active, total_ref, middle_ref, send_ref, small_ref, *refs = refs
    grad_refs, refs = refs[:2], refs[2:]
    normed, normed_t, cotangent_t, normal, spread, w_in, w_out, grad_hidden, sems = refs
    copies = load_weights(near, place_ref, pieces, [(0, w_in), (1, w_out)], sems)
    me = place_ref[0]
    orders = [((z ^ (me >> 3)) + 4 * (y ^ ((me >> 2) & 1)) + 8 * (c ^ ((me >> 1) & 1))) for z in range(4) for y in range(2) for c in range(2)]
    orders = orders if near else []
    tokens, width = tokens_ref.shape
    halves, _, columns = w_in.shape
    gain, shift, bias_out = vectors_ref[2:3, :], vectors_ref[3:4, :], vectors_ref[4:5, :]
    row_blocks = [slice(r, r + ROWS) for r in range(0, tokens, ROWS)]
    spectra = spans(gather_lanes(got_ref, groups))
    span = wide_t_ref.shape[0]
    bias_out_grad = jnp.zeros((1, width), F32)
    for rows in row_blocks:
        first = rows.start % span
        spatial = dot(wide_t_ref[first : first + ROWS, :], spectra[rows.start // span])
        middle = tokens_ref[rows, :].astype(F32) + spatial
        unit, inverse = normalize(middle)
        normal[rows, :] = unit
        spread[rows, :] = inverse
        scaled = (unit * gain + shift).astype(BF16)
        normed[rows, :] = scaled
        place_rows(normed_t, scaled.T, rows, orders)
        total_ref[rows, :] = middle + bias_out
        upstream = cotangent_ref[rows, :]
        place_rows(cotangent_t, upstream.T, rows, orders)
        bias_out_grad = bias_out_grad + jnp.sum(upstream.astype(F32), axis=0, keepdims=True)
    total_ref.flush()
    for copy in copies:
        copy.wait()
    gain_grad = jnp.zeros((1, width), F32)
    shift_grad = jnp.zeros((1, width), F32)
    chunks = [(h, c) for h in range(halves) for c in range(0, columns, CHUNK)]
    bias_grads = [jnp.zeros((1, CHUNK), F32) for _ in chunks]
    for rows in row_blocks:
        for i, (h, c) in enumerate(chunks):
            lanes, flat = slice(c, c + CHUNK), slice(h * columns + c, h * columns + c + CHUNK)
            hidden = dot(normed[rows, :], w_in[h, :, lanes]) + bias_ref[i : i + 1, :]
            value, slope = gelu_pair(hidden)
            active[rows, flat] = value.astype(BF16)
            back = (dot(cotangent_ref[rows, :], w_out[h, :, lanes]) * slope).astype(BF16)
            grad_hidden[rows, flat] = back
            bias_grads[i] = bias_grads[i] + jnp.sum(back.astype(F32), axis=0, keepdims=True)
        back = dot_nt(grad_hidden[rows, :columns], w_in[0])
        for h in range(1, halves):
            back = back + dot_nt(grad_hidden[rows, h * columns : (h + 1) * columns], w_in[h])
        unit = normal[rows, :]
        gain_grad = gain_grad + jnp.sum(back * unit, axis=0, keepdims=True)
        shift_grad = shift_grad + jnp.sum(back, axis=0, keepdims=True)
        middle = cotangent_ref[rows, :].astype(F32) + norm_back(back, unit, spread[rows, :], gain)
        middle_ref[rows, :] = middle.astype(BF16)
    active.flush()
    middle_ref.flush()
    small_ref[0:3, :] = jnp.concatenate([gain_grad, shift_grad, bias_out_grad], axis=0)
    small_ref[3:7, :] = jnp.concatenate(bias_grads, axis=0)
    small_ref[7:8, :] = jnp.zeros((1, width), F32)
    scatter_lanes(send_ref, along_w(wide_ref, middle_ref, tokens), groups)
    send_ref.flush()
    for i, (h, c) in enumerate(chunks):
        flat = slice(h * columns + c, h * columns + c + CHUNK)
        grads = [
            dot(normed_t[...], grad_hidden[:, flat]).astype(BF16), dot(cotangent_t[...], active[:, flat]).astype(BF16)
        ]
        if not near:
            for ref, grad in zip(grad_refs, grads, strict=True):
                ref[h, :, c : c + CHUNK] = grad
            continue
        size = w_in.shape[1] // 16
        x = h ^ (me & 1)
        for core, ref in enumerate(grad_refs):
            for y in range(2):
                for z in range(4):
                    block = core * 8 + y * 4 + z
                    rows = slice(block * size, (block + 1) * size)
                    for q in range(CHUNK // 128):
                        lanes = slice(q * 128, (q + 1) * 128)
                        place = slice((c // 128 + q) * size, (c // 128 + q + 1) * size)
                        ref[0, x, y, z, place, :] = grads[0][rows, lanes]
                        ref[1, y, x, z, place, :] = grads[1][rows, lanes]


def output_kernel(near, place_ref, *refs):
    count = 8 if near else 1
    totals, actives, pieces = refs[:OUT_BLOCKS], refs[OUT_BLOCKS : 2 * OUT_BLOCKS], refs[2 * OUT_BLOCKS :][:count]
    outputs, w_out, sems = refs[2 * OUT_BLOCKS + count], *refs[2 * OUT_BLOCKS + count + 1 :]
    for copy in load_weights(near, place_ref, pieces, [(1, w_out)], sems):
        copy.wait()
    halves, _, columns = w_out.shape
    size = totals[0].shape[0]
    for i, (total, active) in enumerate(zip(totals, actives, strict=True)):
        value = total[...]
        for h in range(halves):
            value = value + dot_nt(active[:, h * columns : (h + 1) * columns], w_out[h])
        outputs[i * size : (i + 1) * size, :] = value.astype(BF16)


def leave_kernel(groups, got_ref, tokens_ref, middle_ref, vectors_ref, table_ref, out_ref):
    spectra = spans(gather_lanes(got_ref, groups))
    span = table_ref.shape[0]
    for start in range(0, tokens_ref.shape[0], ROWS):
        rows = slice(start, start + ROWS)
        first = start % span
        upstream = dot(table_ref[first : first + ROWS, :], spectra[start // span])
        unit, inverse = normalize(tokens_ref[rows, :].astype(F32))
        back = norm_back(upstream, unit, inverse, vectors_ref[0:1, :])
        out_ref[rows, :] = (middle_ref[rows, :].astype(F32) + back).astype(BF16)


def update(weight, gradient, moment, average, decay_rate):
    step_grad = gradient + decay_rate * weight
    new_moment = MOMENTUM * moment + step_grad
    new_weight = weight - LEARNING_RATE * (step_grad + MOMENTUM * new_moment)
    new_average = AVERAGE * average + (1.0 - AVERAGE) * new_weight
    return (new_weight, new_moment, new_average)


class Source:
    def __init__(self, ref, copy):
        self.ref, self.copy, self.shape = ref, copy, ref.shape

    def __getitem__(self, index):
        if self.copy is not None:
            self.copy.wait()
            self.copy = None
        return self.ref[index]


class Sink:
    def __init__(self, ref, copy):
        self.ref, self.copy, self.shape, self.sent = ref, copy, ref.shape, False

    def __getitem__(self, index):
        return self.ref[index]

    def __setitem__(self, index, value):
        self.ref[index] = value

    def flush(self):
        if not self.sent:
            self.copy.start()
            self.sent = True


class Far:
    def __init__(self, *what):
        self.what = what


def call(body, outs, *args, scalars=(), raw=(), scratch=(), flops=0, carry=(), cost=None, vmem=20):
    near, far, there = [pl.BlockSpec(memory_space=m) for m in (pltpu.VMEM, pltpu.HBM, pl.ANY)]
    in_far, out_far = [isinstance(a, Far) for a in args], [isinstance(o, Far) for o in outs]
    index = [a.what[1:] if f else () for a, f in zip(args, in_far, strict=True)]
    args = [
        pltpu.with_memory_space_constraint(*((a.what[0], pltpu.HBM) if f else (a, pltpu.VMEM)))
        for a, f in zip(args, in_far, strict=True)
    ]
    raw = [pltpu.with_memory_space_constraint(a, pltpu.HBM) for a in raw]
    outs = [o.what if f else o for o, f in zip(outs, out_far, strict=True)]
    outs = [jax.ShapeDtypeStruct(s, d) for s, d in outs]
    n_scalar, n_in, n_raw, n_carry, n_out = len(scalars), len(args), len(raw), len(carry), len(outs)
    shapes = [np.empty(a.shape, np.bool_)[i].shape if i else a.shape for a, i in zip(args, index, strict=True)]
    shapes += [o.shape for o in outs]
    buffers = [
        pltpu.VMEM(shape, a.dtype) for shape, a, f in zip(shapes, args + outs, in_far + out_far, strict=True) if f
    ]

    def inner(*refs):
        refs = list(refs)

        def take(count):
            taken = refs[:count]
            del refs[:count]
            return taken

        scalar_refs, in_refs, raw_refs, _, out_refs, _ = [
            take(n) for n in (n_scalar, n_in, n_raw, n_carry, n_out, n_carry)
        ]
        space = take(len(buffers))
        sems = take(1)[0] if buffers else None
        sources, sinks, used = [], [], 0
        for ref, away, part in zip(in_refs, in_far, index, strict=True):
            if away:
                copy = pltpu.make_async_copy(ref.at[part] if part else ref, space[used], sems.at[used])
                copy.start()
                ref = Source(space[used], copy)
                used += 1
            sources.append(ref)
        for ref, away in zip(out_refs, out_far, strict=True):
            if away:
                ref = Sink(space[used], pltpu.make_async_copy(space[used], ref, sems.at[used]))
                used += 1
            sinks.append(ref)
        body(*scalar_refs, *sources, *raw_refs, *sinks, *refs)
        for source in sources:
            if isinstance(source, Source) and source.copy is not None:
                source.copy.wait()
        sinks = [sink for sink in sinks if isinstance(sink, Sink)]
        for sink in sinks:
            sink.flush()
        for sink in sinks:
            sink.copy.wait()

    every = list(args) + list(raw)
    size = sum(math.prod(a.shape) * a.dtype.itemsize for a in every + outs) if cost is None else cost
    sems = [pltpu.SemaphoreType.DMA((len(buffers),))] if buffers else []
    return pl.pallas_call(
        inner,
        out_shape=[(pltpu.HBM if f else pltpu.VMEM)(o.shape, o.dtype) for o, f in zip(outs, out_far, strict=True)]
        + [jax.ShapeDtypeStruct(a.shape, a.dtype) for a in carry],
        in_specs=[pl.BlockSpec(memory_space=pltpu.SMEM)] * n_scalar
        + [far if f else near for f in in_far]
        + [far] * n_raw
        + [there] * n_carry,
        out_specs=[far if f else near for f in out_far] + [there] * n_carry,
        scratch_shapes=buffers + sems + list(scratch),
        input_output_aliases={n_scalar + n_in + n_raw + i: n_out + i for i in range(n_carry)},
        compiler_params=pltpu.CompilerParams(vmem_limit_bytes=vmem << 20),
        cost_estimate=pl.CostEstimate(flops=flops, bytes_accessed=size, transcendentals=0),
    )(*scalars, *args, *raw, *carry)


def on_device(
    tokens, cotangent, w_in, w_out, mixer_weights, vectors, w_in_moment, w_out_moment, mixer_moment, vectors_moment,
    w_in_average, w_out_average, mixer_average, vectors_average,
):
    sp_count, tp_count = lax.axis_size("sp"), lax.axis_size("tp")
    devices = sp_count * tp_count
    grid_rows, grid, width = tokens.shape
    local = grid_rows * grid
    items = grid_rows * devices // grid
    block_count, block = mixer_weights.shape[1], mixer_weights.shape[3]
    hidden = w_in.shape[1] * tp_count
    model = w_in.shape[0] * sp_count
    lanes = 2 * block if devices * 2 * block <= MODES * width else block
    groups = width // lanes
    per_group = devices // groups
    modes = MODES // per_group
    joined = lanes // block
    scale = 1.0 / math.sqrt(local * devices)
    wide_f, wide_i, high, ones = expanded_tables(grid, items)
    me = lax.axis_index("sp") * tp_count + lax.axis_index("tp")
    group = me // per_group
    exchange = functools.partial(lax.all_to_all, axis_name=AXES, split_axis=0, concat_axis=0, tiled=True)
    chunk = (devices, modes * grid_rows * 2, lanes)
    rows_all = tokens.reshape(local, width)
    upstream_all = cotangent.reshape(local, width)
    shard_rows, shard_columns = w_in.shape
    shard_size = shard_rows * shard_columns // 128
    near = devices == 32 and per_group == 8 and shard_rows % 16 == 0

    def permute(values, mask):
        return lax.ppermute(values, AXES, [(d, d ^ mask) for d in range(devices)])

    pair = jnp.stack([w_in.astype(BF16), w_out.astype(BF16)])
    if near:
        line = [pair] + [permute(pair, 8 * z) for z in (1, 2, 3)]
        carried = [jnp.stack([v, permute(v, m)]) for v, m in ((jnp.stack(line[:2]), 1), (jnp.stack(line[2:]), 4))]
    else:
        weights = lax.all_gather(pair, "sp", axis=1, tiled=True)
        pieces, carried = [lax.all_gather(weights, "tp")], []

    own_mixer = lax.dynamic_slice_in_dim(mixer_weights, group * joined, joined, 1).astype(BF16)
    eye = jnp.eye(joined, dtype=BF16)
    real = jnp.einsum("lbio,bc->lbico", own_mixer[:, :, 0], eye).reshape(2, lanes, lanes)
    imag = jnp.einsum("lbio,bc->lbico", own_mixer[:, :, 1], eye).reshape(2, lanes, lanes)
    mats = jnp.concatenate(
        [jnp.concatenate([real, imag], axis=2), jnp.concatenate([-imag, real], axis=2)], axis=1
    )
    own_bias = lax.dynamic_slice_in_dim(
        vectors[9:13].reshape(2, block_count, 2, block), group * joined, joined, 1
    )
    own_bias = jnp.swapaxes(own_bias, 1, 2).reshape(2, 2 * lanes)
    own_gain = lax.dynamic_slice_in_dim(vectors[0:1], group * lanes, lanes, 1)
    own_shift = lax.dynamic_slice_in_dim(vectors[1:2], group * lanes, lanes, 1)
    ones = jnp.asarray(np.swapaxes(ones.reshape(per_group, modes, -1), 1, 2))
    own_ones = lax.dynamic_index_in_dim(ones, me % per_group, 0, keepdims=False)

    wide_f, wide_f_t = jnp.asarray(wide_f), jnp.asarray(wide_f.T)
    wide_i, wide_i_t = jnp.asarray(wide_i), jnp.asarray(wide_i.T)
    high, high_t = jnp.asarray(high), jnp.asarray(high.T)
    wide_flops = 2 * MODES * 2 * local * width * SPAN
    (sent,) = call(
        functools.partial(enter_kernel, groups), [(chunk, BF16)], Far(rows_all), Far(wide_f), flops=wide_flops
    )
    got = exchange(sent)
    half_rows = items * MODES
    sent, hat, modal, inner, active, *carried = call(
        functools.partial(mix_kernel, modes),
        [
            (chunk, BF16),
            Far((2 * half_rows, modes * lanes), F32),
            Far((modes * half_rows, 2 * lanes), BF16),
            Far((modes * half_rows, 2 * lanes), F32),
            Far((modes * half_rows, 2 * lanes), BF16),
        ],
        got, high, high_t, mats, own_bias, own_gain, own_shift, own_ones,
        carry=carried,
    )
    if near:
        pieces = carried + [permute(carried[0], 4), permute(carried[1], 1)]
        pieces += [permute(p, 2) for p in pieces]
    got = exchange(sent)
    steps = hidden // CHUNK
    grads = [((2, 2, 2, 4, shard_size, 128), BF16)] * 2 if near else [((tp_count, model, shard_columns), BF16)] * 2
    gelus, total, middle, sent, mlp_small, *grads = call(
        functools.partial(mlp_kernel, groups, near),
        [
            Far((local, hidden), BF16), Far((local, width), F32), Far((local, width), BF16), Far(chunk, BF16),
            ((8, width), F32),
        ]
        + grads,
        Far(got), Far(wide_i_t), Far(rows_all), Far(upstream_all), vectors, vectors[5:9].reshape(steps, CHUNK), Far(wide_i),
        scalars=[me[None]], raw=pieces,
        scratch=[
            pltpu.VMEM((local, width), BF16),
            pltpu.VMEM((width, local), BF16),
            pltpu.VMEM((width, local), BF16),
            pltpu.VMEM((local, width), F32),
            pltpu.VMEM((local, 1), F32),
            pltpu.VMEM((tp_count, model, shard_columns), BF16),
            pltpu.VMEM((tp_count, model, shard_columns), BF16),
            pltpu.VMEM((local, hidden), BF16),
            pltpu.SemaphoreType.DMA((64 if near else 2,)),
        ],
        flops=12 * local * width * hidden + 2 * wide_flops, vmem=44,
    )

    carried = []
    if near:
        shard = (4, shard_size, 128)
        kept, one = grads[0], permute(grads[1], 2)
        sent_in, sent_out = call(
            first_kernel, [((2,) + shard, BF16)] * 2, kept, Far(one, slice(None), 1), cost=0
        )
        carried = [permute(sent_in, 1), permute(sent_out, 4)]

    step = local // OUT_BLOCKS
    parts = [slice(r, r + step) for r in range(0, local, step)]
    (output,) = call(
        functools.partial(output_kernel, near), [Far((local, width), BF16)],
        *[Far(total, rows) for rows in parts], *[Far(gelus, rows) for rows in parts],
        scalars=[me[None]], raw=pieces, cost=COST, vmem=24,
        scratch=[
            pltpu.VMEM((tp_count, model, shard_columns), BF16),
            pltpu.SemaphoreType.DMA((32 if near else 1,)),
        ],
    )

    got = exchange(sent)
    small_rows = -(-(2 * block + 8 + 8 * (groups // 2)) // 16) * 16
    place = ((me >> 1) & 1 if near else jnp.int32(0))[None]
    sent, small, given, output = call(
        functools.partial(unmix_kernel, modes, block),
        [Far(chunk, BF16), ((small_rows, lanes), BF16), ((small_rows, lanes), BF16)],
        got, Far(high), Far(high_t), Far(mats), own_ones, Far(hat), Far(modal), Far(inner), Far(active), mlp_small,
        scalars=[place], cost=COST, vmem=20 if near else 48, carry=[output],
    )
    if near:
        both = slice(None)
        small, over_y, over_x = call(
            second_kernel, [((small_rows, lanes), BF16)] + [(shard, BF16)] * 2,
            kept, *[Far(a, 1) for a in carried], small, permute(given, 2), Far(one, both, 0, 1), cost=0,
        )
        line, own, *away = call(
            third_kernel,
            [((4, small_rows, lanes), BF16), ((2, shard_size, 128), F32)] + [((2, shard_size, 128), BF16)] * 3,
            kept, *[Far(a, 0) for a in carried], permute(over_y, 4), permute(over_x, 1),
            small, *[permute(small, 8 * z) for z in (1, 2, 3)], Far(one, both, 0, 0),
            scalars=[me[None]], cost=0,
        )
        away = [permute(a, 8 * (z + 1)) for z, a in enumerate(away)]
    got = exchange(sent)
    (grad_tokens,) = call(
        functools.partial(leave_kernel, groups),
        [Far((local, width), BF16)],
        got, Far(rows_all), Far(middle), vectors, Far(wide_f_t), cost=COST,
    )

    if near:
        line, *away, grad_tokens = call(
            plane_kernel, [(line.shape, BF16)], line, *[permute(line, m) for m in (1, 4, 5)], cost=0, carry=[*away, grad_tokens]
        )
        other = permute(line, 2)

    state = [mixer_weights, mixer_moment, mixer_average, vectors, vectors_moment, vectors_average]
    new_state = [Far(a.shape, F32) for a in state]
    if near:
        weights = [w_in, w_out, w_in_moment, w_out_moment, w_in_average, w_out_average]
        *stepped, grad_tokens = call(
            functools.partial(step_all, block, scale),
            [Far(w_in.shape, F32)] * 6 + [Far(w_in.shape, BF16)] * 2 + new_state,
            own, *away, *weights, line, other, *state,
            scalars=[place], scratch=[pltpu.VMEM((16, width), F32)], carry=[grad_tokens], cost=0,
        )
        new_in, new_out = stepped[0:8:2], stepped[1:8:2]
        stepped = stepped[8:]
    else:
        grads = jnp.stack(grads).astype(F32)
        grads = lax.psum_scatter(grads, "tp", scatter_dimension=1, tiled=True)
        grads = lax.psum_scatter(grads, "sp", scatter_dimension=2, tiled=True)
        new_in = update(w_in, grads[0, 0] * scale, w_in_moment, w_in_average, WEIGHT_DECAY)
        new_out = update(w_out, grads[1, 0] * scale, w_out_moment, w_out_average, WEIGHT_DECAY)
        new_in, new_out = new_in + (new_in[0].astype(BF16),), new_out + (new_out[0].astype(BF16),)
        onehot = (jnp.arange(groups, dtype=jnp.int32) == group).astype(F32)[:, None, None]
        line, other = lax.psum((onehot * small.astype(F32), onehot * given.astype(F32)), AXES)
        stepped = call(
            functools.partial(step_rest, block, scale), new_state, line, other, *state,
            scalars=[place], scratch=[pltpu.VMEM((16, width), F32)],
        )
    new_mix, new_vec = stepped[0:3], stepped[3:6]
    shape = tokens.shape
    return (
        output.reshape(shape), grad_tokens.reshape(shape),
        new_in[0], new_out[0], new_mix[0], new_vec[0],
        new_in[1], new_out[1], new_mix[1], new_vec[1],
        new_in[2], new_out[2], new_mix[2], new_vec[2],
        new_in[3], new_out[3],
    )


def solution(mesh):
    rows, split, whole = P(AXES, None, None), P("sp", "tp"), P()
    state = (split, split, whole, whole)
    return jax.shard_map(
        on_device,
        mesh=mesh,
        in_specs=(rows, rows) + state * 3,
        out_specs=(rows, rows) + state * 3 + (split, split),
        check_vma=False,
    )
```

```python
import functools
import math

import jax
import jax.numpy as jnp
import ml_dtypes
import numpy as np
from jax import lax
from jax.experimental import pallas as pl
from jax.experimental.pallas import tpu as pltpu
from jax.sharding import PartitionSpec as P

MODES = 32
EPSILON = 1e-05
LEARNING_RATE = 0.05
MOMENTUM = 0.9
WEIGHT_DECAY = 0.0001
AVERAGE = 0.75
GELU_SCALE = math.sqrt(2.0 / math.pi)
GELU_CUBE = 0.044715
CHUNK = 512
ROWS = 256
SPAN = 4
BF16 = jnp.bfloat16
F32 = jnp.float32
AXES = ("sp", "tp")
COST = 60 << 20
OUT_BLOCKS = 4


def dft_tables(grid):
    positions = np.arange(grid)
    wave = np.arange(MODES)
    root = np.float32(1.0 / math.sqrt(grid))
    step = np.float32(2.0 * math.pi / grid)
    phase_w = (positions[:, None] * wave[None, :] % grid).astype(np.float32) * step
    factor = np.where(wave == 0, 1.0, 2.0).astype(np.float32)
    cos_w, sin_w = np.cos(phase_w) * root, np.sin(phase_w) * root
    forward_w = np.stack([cos_w, -sin_w], axis=1)
    inverse_w = np.stack([cos_w * factor, -sin_w * factor], axis=1)
    frequency = np.where(wave < MODES // 2, wave, wave - MODES)
    phase_h = (frequency[:, None] * positions[None, :] % grid).astype(np.float32) * step
    cos_h, sin_h = np.cos(phase_h) * root, np.sin(phase_h) * root
    forward_h = np.stack([np.stack([cos_h, -sin_h], -1), np.stack([sin_h, cos_h], -1)], -2)
    return [t.astype(ml_dtypes.bfloat16) for t in (forward_w, inverse_w, forward_h)]


def expanded_tables(grid, items):
    forward_w, inverse_w, forward_h = [t.astype(np.float32) for t in dft_tables(grid)]
    eye_r = np.eye(SPAN, dtype=np.float32)
    wide_f = np.einsum("wek,rs->kresw", forward_w, eye_r).reshape(-1, SPAN * grid)
    wide_i = np.einsum("wek,rs->kresw", inverse_w, eye_r).reshape(-1, SPAN * grid)
    eye_i = np.eye(items, dtype=np.float32)
    high = np.einsum("mhef,ij->fimhje", forward_h, eye_i).reshape(2 * items * MODES, -1)
    ones = np.einsum("mhef,ek->kfm", forward_h.astype(np.float64), forward_w.astype(np.float64).sum(0))
    ones = np.repeat(ones[:, :, None], items, axis=2).reshape(MODES, -1).astype(np.float32)
    cast = [t.astype(ml_dtypes.bfloat16) for t in (wide_f, wide_i, high)]
    return cast[0], cast[1], cast[2], ones


def dot(left, right):
    return jnp.dot(left, right, preferred_element_type=F32)


def dot_nt(left, right):
    return lax.dot_general(left, right, (((1,), (1,)), ((), ())), preferred_element_type=F32)


def dot_tn(left, right):
    return lax.dot_general(left, right, (((0,), (0,)), ((), ())), preferred_element_type=F32)


def normalize(values):
    center = values - jnp.mean(values, axis=-1, keepdims=True)
    inverse = lax.rsqrt(jnp.mean(center * center, axis=-1, keepdims=True) + EPSILON)
    return center * inverse, inverse


def norm_back(upstream, normal, inverse, gain):
    scaled = upstream * gain
    centered = scaled - jnp.mean(scaled, axis=-1, keepdims=True)
    centered = centered - normal * jnp.mean(scaled * normal, axis=-1, keepdims=True)
    return centered * inverse


def gelu_pair(values):
    square = values * values
    bent = jnp.tanh(values * (GELU_SCALE + (GELU_SCALE * GELU_CUBE) * square))
    half = 0.5 + 0.5 * bent
    slope = half + (values * half) * (1.0 - bent) * (GELU_SCALE + (3.0 * GELU_SCALE * GELU_CUBE) * square)
    return values * half, slope


def gelu_value(values):
    square = values * values
    bent = jnp.tanh(values * (GELU_SCALE + (GELU_SCALE * GELU_CUBE) * square))
    return values * (0.5 + 0.5 * bent)


def along_w(table_ref, values, rows):
    table = table_ref[...]
    span = table.shape[1]
    parts = [dot(table, values[r : r + span]).reshape(MODES, -1, values.shape[1]) for r in range(0, rows, span)]
    return jnp.concatenate(parts, axis=1).reshape(-1, values.shape[1]).astype(BF16)


def spans(spectrum):
    whole = spectrum.astype(F32).reshape(MODES, -1, spectrum.shape[1])
    size = 2 * SPAN
    return [
        whole[:, r : r + size].reshape(MODES * size, -1).astype(BF16) for r in range(0, whole.shape[1], size)
    ]


def gather_lanes(ref, groups):
    count = ref.shape[0] // groups
    width = ref.shape[2]
    parts = [ref[g * count : (g + 1) * count].reshape(count * ref.shape[1], width) for g in range(groups)]
    return parts[0] if groups == 1 else jnp.concatenate(parts, axis=1)


def scatter_lanes(ref, values, groups):
    count = ref.shape[0] // groups
    width = ref.shape[2]
    for g in range(groups):
        piece = values[:, g * width : (g + 1) * width]
        ref[g * count : (g + 1) * count] = piece.reshape(count, ref.shape[1], width)


def gather_modes(ref, modes):
    rows = ref.shape[1] // modes
    parts = [
        ref[:, k * rows : (k + 1) * rows, :].reshape(ref.shape[0] * rows, ref.shape[2]) for k in range(modes)
    ]
    return parts[0] if modes == 1 else jnp.concatenate(parts, axis=1)


def scatter_modes(ref, values, modes):
    rows = ref.shape[1] // modes
    width = ref.shape[2]
    for k in range(modes):
        piece = values[:, k * width : (k + 1) * width]
        ref[:, k * rows : (k + 1) * rows, :] = piece.reshape(ref.shape[0], rows, width)


def to_mix_rows(values, modes, width):
    half = values.shape[0] // 2
    parts = []
    for k in range(modes):
        piece = values[:, k * width : (k + 1) * width]
        parts.append(jnp.concatenate([piece[:half], piece[half:]], axis=1))
    return parts[0] if modes == 1 else jnp.concatenate(parts, axis=0)


def from_mix_rows(values, modes, width):
    half = values.shape[0] // modes
    parts = []
    for k in range(modes):
        piece = values[k * half : (k + 1) * half]
        parts.append(jnp.concatenate([piece[:, :width], piece[:, width:]], axis=0))
    return parts[0] if modes == 1 else jnp.concatenate(parts, axis=1)


def enter_kernel(groups, tokens_ref, table_ref, send_ref):
    normal, _ = normalize(tokens_ref[...].astype(F32))
    scatter_lanes(send_ref, along_w(table_ref, normal.astype(BF16), normal.shape[0]), groups)


def mix_kernel(
    modes, got_ref, high_ref, back_ref, mats_ref, bias_ref, gain_ref, shift_ref, ones_ref,
    send_ref, hat_ref, modal_ref, inner_ref, active_ref,
):
    width = got_ref.shape[2]
    hat = dot(high_ref[...], gather_modes(got_ref, modes))
    hat_ref[...] = hat
    hat_ref.flush()
    pieces = []
    for k in range(modes):
        piece = hat[:, k * width : (k + 1) * width] * gain_ref[...]
        pieces.append(piece + ones_ref[:, k : k + 1] * shift_ref[...])
    modal = pieces[0] if modes == 1 else jnp.concatenate(pieces, axis=1)
    modal = to_mix_rows(modal.astype(BF16), modes, width)
    modal_ref[...] = modal
    modal_ref.flush()
    inner = dot(modal, mats_ref[0]) + bias_ref[0:1, :]
    inner_ref[...] = inner
    inner_ref.flush()
    active = gelu_value(inner).astype(BF16)
    active_ref[...] = active
    active_ref.flush()
    outer = (dot(active, mats_ref[1]) + bias_ref[1:2, :]).astype(BF16)
    gridded = dot(back_ref[...], from_mix_rows(outer, modes, width)).astype(BF16)
    scatter_modes(send_ref, gridded, modes)


def fold(grad, width, block):
    real = grad[:width, :width] + grad[width:, width:]
    imag = grad[:width, width:] - grad[width:, :width]
    out = []
    for part in (real, imag):
        if width == block:
            out.append(part)
        else:
            lane = lax.broadcasted_iota(jnp.int32, (block, width), 1)
            out.append(jnp.where(lane < block, part[:block], part[block:]))
    return jnp.concatenate(out, axis=0)


def by_block(sums, width, block):
    real, imag = sums[:, :width], sums[:, width:]
    if width == block:
        return [real, imag]
    lane = lax.broadcasted_iota(jnp.int32, real.shape, 1)
    turned_real, turned_imag = pltpu.roll(real, block, 1), pltpu.roll(imag, block, 1)
    return [jnp.where(lane < block, real, turned_imag), jnp.where(lane < block, turned_real, imag)]


def unmix_kernel(
    modes, block, place_ref, got_ref, high_ref, back_ref, mats_ref, ones_ref, hat_ref, modal_ref, inner_ref, active_ref,
    mlp_ref, send_ref, keep_ref, give_ref,
):
    width = got_ref.shape[2]
    grad_outer = dot(high_ref[...], gather_modes(got_ref, modes)).astype(BF16)
    grad_outer = to_mix_rows(grad_outer, modes, width)
    _, slope = gelu_pair(inner_ref[...])
    grad_inner = (dot_nt(grad_outer, mats_ref[1]) * slope).astype(BF16)
    grad_modal = dot_nt(grad_inner, mats_ref[0]).astype(BF16)
    grad_modal = from_mix_rows(grad_modal, modes, width)
    spectrum = dot(back_ref[...], grad_modal).astype(BF16)
    scatter_modes(send_ref, spectrum, modes)
    send_ref.flush()
    rows = 2 * block
    grads = [fold(dot_tn(modal_ref[...], grad_inner), width, block)]
    grads.append(fold(dot_tn(active_ref[...], grad_outer), width, block))
    bias_one = by_block(jnp.sum(grad_inner.astype(F32), axis=0, keepdims=True), width, block)
    bias_two = by_block(jnp.sum(grad_outer.astype(F32), axis=0, keepdims=True), width, block)
    gain = jnp.zeros((1, width), F32)
    shift = jnp.zeros((1, width), F32)
    for k in range(modes):
        lanes = slice(k * width, (k + 1) * width)
        upstream = grad_modal[:, lanes].astype(F32)
        gain = gain + jnp.sum(upstream * hat_ref[:, lanes], axis=0, keepdims=True)
        shift = shift + jnp.sum(upstream * ones_ref[:, k : k + 1], axis=0, keepdims=True)
    tail = jnp.concatenate(bias_one + bias_two + [gain, shift, jnp.zeros((2, width), F32)], axis=0)
    mlp = [mlp_ref[:, q : q + width] for q in range(0, mlp_ref.shape[1], width)]
    count = len(mlp) // 2
    rows = keep_ref.shape[0] - 2 * block - 8 - 8 * count
    rest = [jnp.zeros((rows, width), F32)] if rows else []
    for half, parts in enumerate(([grads[0], tail] + mlp[:count], [grads[1], jnp.zeros_like(tail)] + mlp[count:])):
        message = jnp.concatenate(parts + rest, axis=0).astype(BF16)
        for ref, core in ((keep_ref, half), (give_ref, 1 - half)):

            @pl.when(place_ref[0] == core)
            def _(ref=ref, message=message):
                ref[...] = message


def add_up(*values):
    total = values[0].astype(F32)
    for value in values[1:]:
        total = total + value.astype(F32)
    return total


def first_kernel(kept_ref, one_ref, in_ref, out_ref):
    for part, ref in enumerate((in_ref, out_ref)):
        ref[...] = add_up(kept_ref[part, 1], one_ref[part]).astype(BF16)


def second_kernel(kept_ref, in_ref, out_ref, mine_ref, core_ref, one_ref, small_ref, y_ref, x_ref):
    small_ref[...] = add_up(mine_ref[...], core_ref[...]).astype(BF16)
    for part, source, ref in ((0, in_ref, y_ref), (1, out_ref, x_ref)):
        ref[...] = add_up(kept_ref[part, 0, 1], one_ref[part], source[...]).astype(BF16)


def third_kernel(place_ref, kept_ref, in_ref, out_ref, y_ref, x_ref, *refs):
    small_refs, (one_ref, line_ref, own_ref), away_refs = refs[:4], refs[4:7], refs[7:]
    for z, ref in enumerate(small_refs):
        line_ref[(place_ref[0] >> 3) ^ z] = ref[...]
    for part, source, last in ((0, in_ref, y_ref), (1, out_ref, x_ref)):
        for z in range(4):
            total = add_up(kept_ref[part, 0, 0, z], one_ref[part, z], source[z], last[z])
            if z == 0:
                own_ref[part] = total
            else:
                away_refs[z - 1][part] = total.astype(BF16)


def plane_kernel(mine_ref, x_ref, y_ref, other_ref, total_ref):
    total_ref[...] = (add_up(mine_ref[...], x_ref[...]) + add_up(y_ref[...], other_ref[...])).astype(BF16)


def step_rest(
    block, scale, place_ref, own_ref, other_ref, mixer_ref, moment_ref, average_ref, vectors_ref, vec_moment_ref,
    vec_average_ref, new_mixer, new_moment, new_average, new_vectors, new_vec_moment, new_vec_average, grad_ref,
):
    groups, _, width = own_ref.shape
    joined = width // block
    rows = 2 * block
    slices = groups // 2
    core = place_ref[0]

    def held(half, group, part):
        mine, theirs = own_ref[group, part, :], other_ref[group, part, :]
        return jnp.where(core == half, mine, theirs).astype(F32)

    for group in range(groups):
        for layer in range(2):
            grad = held(layer, group, slice(0, rows)) * scale
            for part in range(2):
                for j in range(joined):
                    b = group * joined + j
                    piece = grad[part * block : (part + 1) * block, j * block : (j + 1) * block]
                    value, moment, average = update(
                        mixer_ref[layer, b, part], piece, moment_ref[layer, b, part], average_ref[layer, b, part],
                        WEIGHT_DECAY,
                    )
                    new_mixer[layer, b, part] = value
                    new_moment[layer, b, part] = moment
                    new_average[layer, b, part] = average
    for ref in (new_mixer, new_moment, new_average):
        ref.flush()
    for group in range(groups):
        tail = held(0, group, slice(rows, rows + 16))
        grad_ref[0:2, group * width : (group + 1) * width] = tail[4:6]
        for layer in range(2):
            for j in range(2):
                b = group * joined + (j if joined == 2 else 0)
                per_row = vectors_ref.shape[1] // (2 * block)
                lane = (b % per_row) * 2 * block + (0 if joined == 2 else j * block)
                row = 9 + layer * 2 + b // per_row
                grad_ref[row : row + 1, lane : lane + width] = tail[2 * layer + j : 2 * layer + j + 1]
    for half in range(2):
        part = slice(rows, rows + 8 + 8 * slices + 8 * ((slices + 1) % 2))
        total = held(half, 0, part)
        for group in range(1, groups):
            total = total + held(half, group, part)
        for q in range(slices):
            lane = (half * slices + q) * width
            grad_ref[2:9, lane : lane + width] = total[8 + 8 * q : 15 + 8 * q]
    value, moment, average = update(
        vectors_ref[...], grad_ref[0:13, :] * scale, vec_moment_ref[...], vec_average_ref[...], 0.0
    )
    new_vectors[...] = value
    new_vec_moment[...] = moment
    new_vec_average[...] = average


def step_all(block, scale, place_ref, *refs):
    step_rest(block, scale, place_ref, *refs[10:18], *refs[26:])
    step_weights(scale, *refs[:10], *refs[18:26])


def step_weights(scale, own_ref, *refs):
    away_refs, weights, new_weights = refs[:3], refs[3:9], refs[9:17]
    for part in range(2):
        total = add_up(own_ref[part], *[ref[part] for ref in away_refs])
        count = weights[part].shape[0]
        for q in range(total.shape[0] // count):
            lanes = slice(q * 128, (q + 1) * 128)
            grad = total[q * count : (q + 1) * count] * scale
            values = update(
                weights[part][:, lanes], grad, weights[2 + part][:, lanes], weights[4 + part][:, lanes], WEIGHT_DECAY
            )
            for i, value in enumerate(values):
                new_weights[2 * i + part][:, lanes] = value
            new_weights[6 + part][:, lanes] = values[0].astype(BF16)
    for ref in new_weights:
        ref.flush()


def load_weights(near, place_ref, pieces, part, target, sems):
    copies = []
    part = () if part is None else (part,)
    every = (slice(None),) * (1 - len(part))
    if not near:
        copies = [(pieces[0].at[(slice(None), *part)], target)]
    else:
        me = place_ref[0]
        at = [(me >> 1) & 1, (me >> 2) & 1, me & 1, me >> 3]
        size = pieces[0].shape[3]
        for i, ref in enumerate(pieces):
            for j in range(2):
                x, y = (i >> 1 & 1, j) if i & 1 else (j, i >> 1 & 1)
                for k in range(2):
                    z = 2 * (i & 1) + k
                    row = (((at[3] ^ z) * 2 + (at[1] ^ y)) * 2 + (at[0] ^ (i >> 2))) * size
                    rows = pl.ds(pl.multiple_of(row, size), size)
                    copies.append((ref.at[(j, k, *part)], target.at[(at[2] ^ x, *every, rows)]))
    copies = [pltpu.make_async_copy(source, target, sems.at[i]) for i, (source, target) in enumerate(copies)]
    for copy in copies:
        copy.start()
    return copies


def place_rows(ref, values, columns, orders):
    if not orders:
        ref[:, columns] = values
        return
    size = values.shape[0] // len(orders)
    for block, order in enumerate(orders):
        ref[pl.ds(pl.multiple_of(order * size, size), size), columns] = values[block * size : (block + 1) * size]


def mlp_kernel(
    groups, near, place_ref, got_ref, wide_t_ref, tokens_ref, cotangent_ref, vectors_ref, bias_ref, wide_ref, *refs
):
    count = 8 if near else 1
    pieces, refs = refs[:count], refs[count:]
    active, total_ref, middle_ref, send_ref, small_ref, *refs = refs
    grad_refs, refs = refs[:2], refs[2:]
    normed, normed_t, cotangent_t, normal, spread, weights, grad_hidden, sems = refs
    copies = load_weights(near, place_ref, pieces, None, weights, sems)
    cotangent_ref.start()
    wide_ref.start()
    w_in, w_out = weights.at[:, 0], weights.at[:, 1]
    me = place_ref[0]
    orders = [((z ^ (me >> 3)) + 4 * (y ^ ((me >> 2) & 1)) + 8 * (c ^ ((me >> 1) & 1))) for z in range(4) for y in range(2) for c in range(2)]
    orders = orders if near else []
    tokens, width = tokens_ref.shape
    halves, _, columns = w_in.shape
    gain, shift, bias_out = vectors_ref[2:3, :], vectors_ref[3:4, :], vectors_ref[4:5, :]
    row_blocks = [slice(r, r + ROWS) for r in range(0, tokens, ROWS)]
    spectra = spans(gather_lanes(got_ref, groups))
    span = wide_t_ref.shape[0]
    bias_out_grad = jnp.zeros((1, width), F32)
    for rows in row_blocks:
        first = rows.start % span
        spatial = dot(wide_t_ref[first : first + ROWS, :], spectra[rows.start // span])
        middle = tokens_ref[rows, :].astype(F32) + spatial
        unit, inverse = normalize(middle)
        normal[rows, :] = unit
        spread[rows, :] = inverse
        scaled = (unit * gain + shift).astype(BF16)
        normed[rows, :] = scaled
        place_rows(normed_t, scaled.T, rows, orders)
        total_ref[rows, :] = middle + bias_out
        upstream = cotangent_ref[rows, :]
        place_rows(cotangent_t, upstream.T, rows, orders)
        bias_out_grad = bias_out_grad + jnp.sum(upstream.astype(F32), axis=0, keepdims=True)
    total_ref.flush()
    for copy in copies:
        copy.wait()
    gain_grad = jnp.zeros((1, width), F32)
    shift_grad = jnp.zeros((1, width), F32)
    chunks = [(h, c) for h in range(halves) for c in range(0, columns, CHUNK)]
    bias_grads = [jnp.zeros((1, CHUNK), F32) for _ in chunks]
    for rows in row_blocks:
        for i, (h, c) in enumerate(chunks):
            lanes, flat = slice(c, c + CHUNK), slice(h * columns + c, h * columns + c + CHUNK)
            hidden = dot(normed[rows, :], w_in[h, :, lanes]) + bias_ref[i : i + 1, :]
            value, slope = gelu_pair(hidden.astype(BF16))
            active[rows, flat] = value.astype(BF16)
            back = (dot(cotangent_ref[rows, :], w_out[h, :, lanes]) * slope).astype(BF16)
            grad_hidden[rows, flat] = back
            bias_grads[i] = bias_grads[i] + jnp.sum(back.astype(F32), axis=0, keepdims=True)
        back = dot_nt(grad_hidden[rows, :columns], w_in[0])
        for h in range(1, halves):
            back = back + dot_nt(grad_hidden[rows, h * columns : (h + 1) * columns], w_in[h])
        unit = normal[rows, :]
        gain_grad = gain_grad + jnp.sum(back * unit, axis=0, keepdims=True)
        shift_grad = shift_grad + jnp.sum(back, axis=0, keepdims=True)
        middle = cotangent_ref[rows, :].astype(F32) + norm_back(back, unit, spread[rows, :], gain)
        middle_ref[rows, :] = middle.astype(BF16)
    active.flush()
    middle_ref.flush()
    small_ref[0:3, :] = jnp.concatenate([gain_grad, shift_grad, bias_out_grad], axis=0)
    small_ref[3:7, :] = jnp.concatenate(bias_grads, axis=0)
    small_ref[7:8, :] = jnp.zeros((1, width), F32)
    scatter_lanes(send_ref, along_w(wide_ref, middle_ref, tokens), groups)
    send_ref.flush()
    for i, (h, c) in enumerate(chunks):
        flat = slice(h * columns + c, h * columns + c + CHUNK)
        grads = [
            dot(normed_t[...], grad_hidden[:, flat]).astype(BF16), dot(cotangent_t[...], active[:, flat]).astype(BF16)
        ]
        if not near:
            for ref, grad in zip(grad_refs, grads, strict=True):
                ref[h, :, c : c + CHUNK] = grad
            continue
        size = w_in.shape[1] // 16
        x = h ^ (me & 1)
        for core, ref in enumerate(grad_refs):
            for y in range(2):
                for z in range(4):
                    block = core * 8 + y * 4 + z
                    rows = slice(block * size, (block + 1) * size)
                    for q in range(CHUNK // 128):
                        lanes = slice(q * 128, (q + 1) * 128)
                        place = slice((c // 128 + q) * size, (c // 128 + q + 1) * size)
                        ref[0, x, y, z, place, :] = grads[0][rows, lanes]
                        ref[1, y, x, z, place, :] = grads[1][rows, lanes]


def output_kernel(near, place_ref, *refs):
    count = 8 if near else 1
    totals, actives, pieces = refs[:OUT_BLOCKS], refs[OUT_BLOCKS : 2 * OUT_BLOCKS], refs[2 * OUT_BLOCKS :][:count]
    outputs, w_out, sems = refs[2 * OUT_BLOCKS + count], *refs[2 * OUT_BLOCKS + count + 1 :]
    for copy in load_weights(near, place_ref, pieces, 1, w_out, sems):
        copy.wait()
    halves, _, columns = w_out.shape
    size = totals[0].shape[0]
    for i, (total, active) in enumerate(zip(totals, actives, strict=True)):
        value = total[...]
        for h in range(halves):
            value = value + dot_nt(active[:, h * columns : (h + 1) * columns], w_out[h])
        outputs[i * size : (i + 1) * size, :] = value.astype(BF16)


def leave_kernel(groups, got_ref, tokens_ref, middle_ref, vectors_ref, table_ref, out_ref):
    spectra = spans(gather_lanes(got_ref, groups))
    span = table_ref.shape[0]
    for start in range(0, tokens_ref.shape[0], ROWS):
        rows = slice(start, start + ROWS)
        first = start % span
        upstream = dot(table_ref[first : first + ROWS, :], spectra[start // span])
        unit, inverse = normalize(tokens_ref[rows, :].astype(F32))
        back = norm_back(upstream, unit, inverse, vectors_ref[0:1, :])
        out_ref[rows, :] = (middle_ref[rows, :].astype(F32) + back).astype(BF16)


def update(weight, gradient, moment, average, decay_rate):
    step_grad = gradient + decay_rate * weight
    new_moment = MOMENTUM * moment + step_grad
    new_weight = weight - LEARNING_RATE * (step_grad + MOMENTUM * new_moment)
    new_average = AVERAGE * average + (1.0 - AVERAGE) * new_weight
    return (new_weight, new_moment, new_average)


class Source:
    def __init__(self, ref, copy):
        self.ref, self.copy, self.shape, self.started = ref, copy, ref.shape, False

    def start(self):
        if not self.started:
            self.copy.start()
            self.started = True

    def __getitem__(self, index):
        if self.copy is not None:
            self.start()
            self.copy.wait()
            self.copy = None
        return self.ref[index]


class Sink:
    def __init__(self, ref, copy):
        self.ref, self.copy, self.shape, self.sent = ref, copy, ref.shape, False

    def __getitem__(self, index):
        return self.ref[index]

    def __setitem__(self, index, value):
        self.ref[index] = value

    def flush(self):
        if not self.sent:
            self.copy.start()
            self.sent = True


class Far:
    def __init__(self, *what):
        self.what = what


class Late(Far):
    pass


def call(body, outs, *args, scalars=(), raw=(), scratch=(), flops=0, carry=(), cost=None, vmem=20):
    near, far, there = [pl.BlockSpec(memory_space=m) for m in (pltpu.VMEM, pltpu.HBM, pl.ANY)]
    in_far, out_far = [isinstance(a, Far) for a in args], [isinstance(o, Far) for o in outs]
    in_late = [isinstance(a, Late) for a in args]
    index = [a.what[1:] if f else () for a, f in zip(args, in_far, strict=True)]
    args = [
        pltpu.with_memory_space_constraint(*((a.what[0], pltpu.HBM) if f else (a, pltpu.VMEM)))
        for a, f in zip(args, in_far, strict=True)
    ]
    raw = [pltpu.with_memory_space_constraint(a, pltpu.HBM) for a in raw]
    outs = [o.what if f else o for o, f in zip(outs, out_far, strict=True)]
    outs = [jax.ShapeDtypeStruct(s, d) for s, d in outs]
    n_scalar, n_in, n_raw, n_carry, n_out = len(scalars), len(args), len(raw), len(carry), len(outs)
    shapes = [np.empty(a.shape, np.bool_)[i].shape if i else a.shape for a, i in zip(args, index, strict=True)]
    shapes += [o.shape for o in outs]
    buffers = [
        pltpu.VMEM(shape, a.dtype) for shape, a, f in zip(shapes, args + outs, in_far + out_far, strict=True) if f
    ]

    def inner(*refs):
        refs = list(refs)

        def take(count):
            taken = refs[:count]
            del refs[:count]
            return taken

        scalar_refs, in_refs, raw_refs, _, out_refs, _ = [
            take(n) for n in (n_scalar, n_in, n_raw, n_carry, n_out, n_carry)
        ]
        space = take(len(buffers))
        sems = take(1)[0] if buffers else None
        sources, sinks, used = [], [], 0
        for ref, away, part, late in zip(in_refs, in_far, index, in_late, strict=True):
            if away:
                copy = pltpu.make_async_copy(ref.at[part] if part else ref, space[used], sems.at[used])
                ref = Source(space[used], copy)
                if not late:
                    ref.start()
                used += 1
            sources.append(ref)
        for ref, away in zip(out_refs, out_far, strict=True):
            if away:
                ref = Sink(space[used], pltpu.make_async_copy(space[used], ref, sems.at[used]))
                used += 1
            sinks.append(ref)
        body(*scalar_refs, *sources, *raw_refs, *sinks, *refs)
        for source in sources:
            if isinstance(source, Source) and source.copy is not None:
                source.copy.wait()
        sinks = [sink for sink in sinks if isinstance(sink, Sink)]
        for sink in sinks:
            sink.flush()
        for sink in sinks:
            sink.copy.wait()

    every = list(args) + list(raw)
    size = sum(math.prod(a.shape) * a.dtype.itemsize for a in every + outs) if cost is None else cost
    sems = [pltpu.SemaphoreType.DMA((len(buffers),))] if buffers else []
    return pl.pallas_call(
        inner,
        out_shape=[(pltpu.HBM if f else pltpu.VMEM)(o.shape, o.dtype) for o, f in zip(outs, out_far, strict=True)]
        + [jax.ShapeDtypeStruct(a.shape, a.dtype) for a in carry],
        in_specs=[pl.BlockSpec(memory_space=pltpu.SMEM)] * n_scalar
        + [far if f else near for f in in_far]
        + [far] * n_raw
        + [there] * n_carry,
        out_specs=[far if f else near for f in out_far] + [there] * n_carry,
        scratch_shapes=buffers + sems + list(scratch),
        input_output_aliases={n_scalar + n_in + n_raw + i: n_out + i for i in range(n_carry)},
        compiler_params=pltpu.CompilerParams(vmem_limit_bytes=vmem << 20),
        cost_estimate=pl.CostEstimate(flops=flops, bytes_accessed=size, transcendentals=0),
    )(*scalars, *args, *raw, *carry)


def on_device(
    tokens, cotangent, w_in, w_out, mixer_weights, vectors, w_in_moment, w_out_moment, mixer_moment, vectors_moment,
    w_in_average, w_out_average, mixer_average, vectors_average,
):
    sp_count, tp_count = lax.axis_size("sp"), lax.axis_size("tp")
    devices = sp_count * tp_count
    grid_rows, grid, width = tokens.shape
    local = grid_rows * grid
    items = grid_rows * devices // grid
    block_count, block = mixer_weights.shape[1], mixer_weights.shape[3]
    hidden = w_in.shape[1] * tp_count
    model = w_in.shape[0] * sp_count
    lanes = 2 * block if devices * 2 * block <= MODES * width else block
    groups = width // lanes
    per_group = devices // groups
    modes = MODES // per_group
    joined = lanes // block
    scale = 1.0 / math.sqrt(local * devices)
    wide_f, wide_i, high, ones = expanded_tables(grid, items)
    me = lax.axis_index("sp") * tp_count + lax.axis_index("tp")
    group = me // per_group
    exchange = functools.partial(lax.all_to_all, axis_name=AXES, split_axis=0, concat_axis=0, tiled=True)
    chunk = (devices, modes * grid_rows * 2, lanes)
    rows_all = tokens.reshape(local, width)
    upstream_all = cotangent.reshape(local, width)
    shard_rows, shard_columns = w_in.shape
    shard_size = shard_rows * shard_columns // 128
    near = devices == 32 and per_group == 8 and shard_rows % 16 == 0

    def permute(values, mask):
        return lax.ppermute(values, AXES, [(d, d ^ mask) for d in range(devices)])

    pair = jnp.stack([w_in.astype(BF16), w_out.astype(BF16)])
    if near:
        line = [pair] + [permute(pair, 8 * z) for z in (1, 2, 3)]
        carried = [jnp.stack([v, permute(v, m)]) for v, m in ((jnp.stack(line[:2]), 1), (jnp.stack(line[2:]), 4))]
    else:
        weights = lax.all_gather(pair, "sp", axis=1, tiled=True)
        pieces, carried = [lax.all_gather(weights, "tp")], []

    own_mixer = lax.dynamic_slice_in_dim(mixer_weights, group * joined, joined, 1).astype(BF16)
    eye = jnp.eye(joined, dtype=BF16)
    real = jnp.einsum("lbio,bc->lbico", own_mixer[:, :, 0], eye).reshape(2, lanes, lanes)
    imag = jnp.einsum("lbio,bc->lbico", own_mixer[:, :, 1], eye).reshape(2, lanes, lanes)
    mats = jnp.concatenate(
        [jnp.concatenate([real, imag], axis=2), jnp.concatenate([-imag, real], axis=2)], axis=1
    )
    own_bias = lax.dynamic_slice_in_dim(
        vectors[9:13].reshape(2, block_count, 2, block), group * joined, joined, 1
    )
    own_bias = jnp.swapaxes(own_bias, 1, 2).reshape(2, 2 * lanes)
    own_gain = lax.dynamic_slice_in_dim(vectors[0:1], group * lanes, lanes, 1)
    own_shift = lax.dynamic_slice_in_dim(vectors[1:2], group * lanes, lanes, 1)
    ones = jnp.asarray(np.swapaxes(ones.reshape(per_group, modes, -1), 1, 2))
    own_ones = lax.dynamic_index_in_dim(ones, me % per_group, 0, keepdims=False)

    wide_f, wide_f_t = jnp.asarray(wide_f), jnp.asarray(wide_f.T)
    wide_i, wide_i_t = jnp.asarray(wide_i), jnp.asarray(wide_i.T)
    high, high_t = jnp.asarray(high), jnp.asarray(high.T)
    wide_flops = 2 * MODES * 2 * local * width * SPAN
    (sent,) = call(
        functools.partial(enter_kernel, groups), [(chunk, BF16)], Far(rows_all), Far(wide_f), flops=wide_flops
    )
    got = exchange(sent)
    half_rows = items * MODES
    sent, hat, modal, inner, active, *carried = call(
        functools.partial(mix_kernel, modes),
        [
            (chunk, BF16),
            Far((2 * half_rows, modes * lanes), F32),
            Far((modes * half_rows, 2 * lanes), BF16),
            Far((modes * half_rows, 2 * lanes), F32),
            Far((modes * half_rows, 2 * lanes), BF16),
        ],
        got, high, high_t, mats, own_bias, own_gain, own_shift, own_ones,
        carry=carried,
    )
    if near:
        pieces = carried + [permute(carried[0], 4), permute(carried[1], 1)]
        pieces += [permute(p, 2) for p in pieces]
    got = exchange(sent)
    steps = hidden // CHUNK
    grads = [((2, 2, 2, 4, shard_size, 128), BF16)] * 2 if near else [((tp_count, model, shard_columns), BF16)] * 2
    gelus, total, middle, sent, mlp_small, *grads = call(
        functools.partial(mlp_kernel, groups, near),
        [
            Far((local, hidden), BF16), Far((local, width), F32), Far((local, width), BF16), Far(chunk, BF16),
            ((8, width), F32),
        ]
        + grads,
        Far(got), Far(wide_i_t), Far(rows_all), Late(upstream_all), vectors, vectors[5:9].reshape(steps, CHUNK), Late(wide_i),
        scalars=[me[None]], raw=pieces,
        scratch=[
            pltpu.VMEM((local, width), BF16),
            pltpu.VMEM((width, local), BF16),
            pltpu.VMEM((width, local), BF16),
            pltpu.VMEM((local, width), F32),
            pltpu.VMEM((local, 1), F32),
            pltpu.VMEM((tp_count, 2, model, shard_columns), BF16),
            pltpu.VMEM((local, hidden), BF16),
            pltpu.SemaphoreType.DMA((32 if near else 1,)),
        ],
        flops=12 * local * width * hidden + 2 * wide_flops, vmem=44,
    )

    carried = []
    if near:
        shard = (4, shard_size, 128)
        kept, one = grads[0], permute(grads[1], 2)
        sent_in, sent_out = call(
            first_kernel, [((2,) + shard, BF16)] * 2, kept, Far(one, slice(None), 1), cost=0
        )
        carried = [permute(sent_in, 1), permute(sent_out, 4)]

    step = local // OUT_BLOCKS
    parts = [slice(r, r + step) for r in range(0, local, step)]
    (output,) = call(
        functools.partial(output_kernel, near), [Far((local, width), BF16)],
        *[Far(total, rows) for rows in parts], *[Far(gelus, rows) for rows in parts],
        scalars=[me[None]], raw=pieces, cost=COST, vmem=24,
        scratch=[
            pltpu.VMEM((tp_count, model, shard_columns), BF16),
            pltpu.SemaphoreType.DMA((32 if near else 1,)),
        ],
    )

    got = exchange(sent)
    small_rows = -(-(2 * block + 8 + 8 * (groups // 2)) // 16) * 16
    place = ((me >> 1) & 1 if near else jnp.int32(0))[None]
    sent, small, given, output = call(
        functools.partial(unmix_kernel, modes, block),
        [Far(chunk, BF16), ((small_rows, lanes), BF16), ((small_rows, lanes), BF16)],
        got, Far(high), Far(high_t), Far(mats), own_ones, Far(hat), Far(modal), Far(inner), Far(active), mlp_small,
        scalars=[place], cost=COST, vmem=20 if near else 48, carry=[output],
    )
    if near:
        both = slice(None)
        small, over_y, over_x = call(
            second_kernel, [((small_rows, lanes), BF16)] + [(shard, BF16)] * 2,
            kept, *[Far(a, 1) for a in carried], small, permute(given, 2), Far(one, both, 0, 1), cost=0,
        )
        line, own, *away = call(
            third_kernel,
            [((4, small_rows, lanes), BF16), ((2, shard_size, 128), F32)] + [((2, shard_size, 128), BF16)] * 3,
            kept, *[Far(a, 0) for a in carried], permute(over_y, 4), permute(over_x, 1),
            small, *[permute(small, 8 * z) for z in (1, 2, 3)], Far(one, both, 0, 0),
            scalars=[me[None]], cost=0,
        )
        away = [permute(a, 8 * (z + 1)) for z, a in enumerate(away)]
    got = exchange(sent)
    (grad_tokens,) = call(
        functools.partial(leave_kernel, groups),
        [Far((local, width), BF16)],
        got, Far(rows_all), Far(middle), vectors, Far(wide_f_t), cost=COST,
    )

    if near:
        line, *away, grad_tokens = call(
            plane_kernel, [(line.shape, BF16)], line, *[permute(line, m) for m in (1, 4, 5)], cost=0, carry=[*away, grad_tokens]
        )
        other = permute(line, 2)

    state = [mixer_weights, mixer_moment, mixer_average, vectors, vectors_moment, vectors_average]
    new_state = [Far(a.shape, F32) for a in state]
    if near:
        weights = [w_in, w_out, w_in_moment, w_out_moment, w_in_average, w_out_average]
        *stepped, grad_tokens = call(
            functools.partial(step_all, block, scale),
            [Far(w_in.shape, F32)] * 6 + [Far(w_in.shape, BF16)] * 2 + new_state,
            own, *away, *weights, line, other, *state,
            scalars=[place], scratch=[pltpu.VMEM((16, width), F32)], carry=[grad_tokens], cost=0,
        )
        new_in, new_out = stepped[0:8:2], stepped[1:8:2]
        stepped = stepped[8:]
    else:
        grads = jnp.stack(grads).astype(F32)
        grads = lax.psum_scatter(grads, "tp", scatter_dimension=1, tiled=True)
        grads = lax.psum_scatter(grads, "sp", scatter_dimension=2, tiled=True)
        new_in = update(w_in, grads[0, 0] * scale, w_in_moment, w_in_average, WEIGHT_DECAY)
        new_out = update(w_out, grads[1, 0] * scale, w_out_moment, w_out_average, WEIGHT_DECAY)
        new_in, new_out = new_in + (new_in[0].astype(BF16),), new_out + (new_out[0].astype(BF16),)
        onehot = (jnp.arange(groups, dtype=jnp.int32) == group).astype(F32)[:, None, None]
        line, other = lax.psum((onehot * small.astype(F32), onehot * given.astype(F32)), AXES)
        stepped = call(
            functools.partial(step_rest, block, scale), new_state, line, other, *state,
            scalars=[place], scratch=[pltpu.VMEM((16, width), F32)],
        )
    new_mix, new_vec = stepped[0:3], stepped[3:6]
    shape = tokens.shape
    return (
        output.reshape(shape), grad_tokens.reshape(shape),
        new_in[0], new_out[0], new_mix[0], new_vec[0],
        new_in[1], new_out[1], new_mix[1], new_vec[1],
        new_in[2], new_out[2], new_mix[2], new_vec[2],
        new_in[3], new_out[3],
    )


def solution(mesh):
    rows, split, whole = P(AXES, None, None), P("sp", "tp"), P()
    state = (split, split, whole, whole)
    return jax.shard_map(
        on_device,
        mesh=mesh,
        in_specs=(rows, rows) + state * 3,
        out_specs=(rows, rows) + state * 3 + (split, split),
        check_vma=False,
    )
```

```python
import functools
import math

import jax
import jax.numpy as jnp
import ml_dtypes
import numpy as np
from jax import lax
from jax.experimental import pallas as pl
from jax.experimental.pallas import tpu as pltpu
from jax.sharding import PartitionSpec as P

MODES = 32
EPSILON = 1e-05
LEARNING_RATE = 0.05
MOMENTUM = 0.9
WEIGHT_DECAY = 0.0001
AVERAGE = 0.75
GELU_SCALE = math.sqrt(2.0 / math.pi)
GELU_CUBE = 0.044715
CHUNK = 512
ROWS = 256
SPAN = 4
BF16 = jnp.bfloat16
F32 = jnp.float32
AXES = ("sp", "tp")
COST = 60 << 20
OUT_BLOCKS = 4


def dft_tables(grid):
    positions = np.arange(grid)
    wave = np.arange(MODES)
    root = np.float32(1.0 / math.sqrt(grid))
    step = np.float32(2.0 * math.pi / grid)
    phase_w = (positions[:, None] * wave[None, :] % grid).astype(np.float32) * step
    factor = np.where(wave == 0, 1.0, 2.0).astype(np.float32)
    cos_w, sin_w = np.cos(phase_w) * root, np.sin(phase_w) * root
    forward_w = np.stack([cos_w, -sin_w], axis=1)
    inverse_w = np.stack([cos_w * factor, -sin_w * factor], axis=1)
    frequency = np.where(wave < MODES // 2, wave, wave - MODES)
    phase_h = (frequency[:, None] * positions[None, :] % grid).astype(np.float32) * step
    cos_h, sin_h = np.cos(phase_h) * root, np.sin(phase_h) * root
    forward_h = np.stack([np.stack([cos_h, -sin_h], -1), np.stack([sin_h, cos_h], -1)], -2)
    return [t.astype(ml_dtypes.bfloat16) for t in (forward_w, inverse_w, forward_h)]


def expanded_tables(grid, items):
    forward_w, inverse_w, forward_h = [t.astype(np.float32) for t in dft_tables(grid)]
    eye_r = np.eye(SPAN, dtype=np.float32)
    wide_f = np.einsum("wek,rs->kresw", forward_w, eye_r).reshape(-1, SPAN * grid)
    wide_i = np.einsum("wek,rs->kresw", inverse_w, eye_r).reshape(-1, SPAN * grid)
    eye_i = np.eye(items, dtype=np.float32)
    high = np.einsum("mhef,ij->fimhje", forward_h, eye_i).reshape(2 * items * MODES, -1)
    ones = np.einsum("mhef,ek->kfm", forward_h.astype(np.float64), forward_w.astype(np.float64).sum(0))
    ones = np.repeat(ones[:, :, None], items, axis=2).reshape(MODES, -1).astype(np.float32)
    cast = [t.astype(ml_dtypes.bfloat16) for t in (wide_f, wide_i, high)]
    return cast[0], cast[1], cast[2], ones


def dot(left, right):
    return jnp.dot(left, right, preferred_element_type=F32)


def dot_nt(left, right):
    return lax.dot_general(left, right, (((1,), (1,)), ((), ())), preferred_element_type=F32)


def dot_tn(left, right):
    return lax.dot_general(left, right, (((0,), (0,)), ((), ())), preferred_element_type=F32)


def normalize(values):
    center = values - jnp.mean(values, axis=-1, keepdims=True)
    inverse = lax.rsqrt(jnp.mean(center * center, axis=-1, keepdims=True) + EPSILON)
    return center * inverse, inverse


def norm_back(upstream, normal, inverse, gain):
    scaled = upstream * gain
    centered = scaled - jnp.mean(scaled, axis=-1, keepdims=True)
    centered = centered - normal * jnp.mean(scaled * normal, axis=-1, keepdims=True)
    return centered * inverse


def gelu_pair(values):
    square = values * values
    bent = jnp.tanh(values * (GELU_SCALE + (GELU_SCALE * GELU_CUBE) * square))
    half = 0.5 + 0.5 * bent
    slope = half + (values * half) * (1.0 - bent) * (GELU_SCALE + (3.0 * GELU_SCALE * GELU_CUBE) * square)
    return values * half, slope


def gelu_value(values):
    square = values * values
    bent = jnp.tanh(values * (GELU_SCALE + (GELU_SCALE * GELU_CUBE) * square))
    return values * (0.5 + 0.5 * bent)


def along_w(table_ref, values, rows):
    table = table_ref[...]
    span = table.shape[1]
    parts = [dot(table, values[r : r + span]).reshape(MODES, -1, values.shape[1]) for r in range(0, rows, span)]
    return jnp.concatenate(parts, axis=1).reshape(-1, values.shape[1]).astype(BF16)


def spans(spectrum):
    whole = spectrum.astype(F32).reshape(MODES, -1, spectrum.shape[1])
    size = 2 * SPAN
    return [
        whole[:, r : r + size].reshape(MODES * size, -1).astype(BF16) for r in range(0, whole.shape[1], size)
    ]


def gather_lanes(ref, groups):
    count = ref.shape[0] // groups
    width = ref.shape[2]
    parts = [ref[g * count : (g + 1) * count].reshape(count * ref.shape[1], width) for g in range(groups)]
    return parts[0] if groups == 1 else jnp.concatenate(parts, axis=1)


def scatter_lanes(ref, values, groups):
    count = ref.shape[0] // groups
    width = ref.shape[2]
    for g in range(groups):
        piece = values[:, g * width : (g + 1) * width]
        ref[g * count : (g + 1) * count] = piece.reshape(count, ref.shape[1], width)


def gather_modes(ref, modes):
    rows = ref.shape[1] // modes
    parts = [
        ref[:, k * rows : (k + 1) * rows, :].reshape(ref.shape[0] * rows, ref.shape[2]) for k in range(modes)
    ]
    return parts[0] if modes == 1 else jnp.concatenate(parts, axis=1)


def scatter_modes(ref, values, modes):
    rows = ref.shape[1] // modes
    width = ref.shape[2]
    for k in range(modes):
        piece = values[:, k * width : (k + 1) * width]
        ref[:, k * rows : (k + 1) * rows, :] = piece.reshape(ref.shape[0], rows, width)


def to_mix_rows(values, modes, width):
    half = values.shape[0] // 2
    parts = []
    for k in range(modes):
        piece = values[:, k * width : (k + 1) * width]
        parts.append(jnp.concatenate([piece[:half], piece[half:]], axis=1))
    return parts[0] if modes == 1 else jnp.concatenate(parts, axis=0)


def from_mix_rows(values, modes, width):
    half = values.shape[0] // modes
    parts = []
    for k in range(modes):
        piece = values[k * half : (k + 1) * half]
        parts.append(jnp.concatenate([piece[:, :width], piece[:, width:]], axis=0))
    return parts[0] if modes == 1 else jnp.concatenate(parts, axis=1)


def enter_kernel(groups, tokens_ref, table_ref, send_ref):
    normal, _ = normalize(tokens_ref[...].astype(F32))
    scatter_lanes(send_ref, along_w(table_ref, normal.astype(BF16), normal.shape[0]), groups)


def mix_kernel(
    modes, got_ref, high_ref, back_ref, mats_ref, bias_ref, gain_ref, shift_ref, ones_ref,
    send_ref, hat_ref, modal_ref, inner_ref, active_ref,
):
    width = got_ref.shape[2]
    hat = dot(high_ref[...], gather_modes(got_ref, modes))
    hat_ref[...] = hat
    hat_ref.flush()
    pieces = []
    for k in range(modes):
        piece = hat[:, k * width : (k + 1) * width] * gain_ref[...]
        pieces.append(piece + ones_ref[:, k : k + 1] * shift_ref[...])
    modal = pieces[0] if modes == 1 else jnp.concatenate(pieces, axis=1)
    modal = to_mix_rows(modal.astype(BF16), modes, width)
    modal_ref[...] = modal
    modal_ref.flush()
    inner = dot(modal, mats_ref[0]) + bias_ref[0:1, :]
    inner_ref[...] = inner
    inner_ref.flush()
    active = gelu_value(inner).astype(BF16)
    active_ref[...] = active
    active_ref.flush()
    outer = (dot(active, mats_ref[1]) + bias_ref[1:2, :]).astype(BF16)
    gridded = dot(back_ref[...], from_mix_rows(outer, modes, width)).astype(BF16)
    scatter_modes(send_ref, gridded, modes)


def fold(grad, width, block):
    real = grad[:width, :width] + grad[width:, width:]
    imag = grad[:width, width:] - grad[width:, :width]
    out = []
    for part in (real, imag):
        if width == block:
            out.append(part)
        else:
            lane = lax.broadcasted_iota(jnp.int32, (block, width), 1)
            out.append(jnp.where(lane < block, part[:block], part[block:]))
    return jnp.concatenate(out, axis=0)


def by_block(sums, width, block):
    real, imag = sums[:, :width], sums[:, width:]
    if width == block:
        return [real, imag]
    lane = lax.broadcasted_iota(jnp.int32, real.shape, 1)
    turned_real, turned_imag = pltpu.roll(real, block, 1), pltpu.roll(imag, block, 1)
    return [jnp.where(lane < block, real, turned_imag), jnp.where(lane < block, turned_real, imag)]


def unmix_kernel(
    modes, block, place_ref, got_ref, high_ref, back_ref, mats_ref, ones_ref, hat_ref, modal_ref, inner_ref, active_ref,
    mlp_ref, send_ref, keep_ref, give_ref,
):
    width = got_ref.shape[2]
    grad_outer = dot(high_ref[...], gather_modes(got_ref, modes)).astype(BF16)
    grad_outer = to_mix_rows(grad_outer, modes, width)
    _, slope = gelu_pair(inner_ref[...])
    grad_inner = (dot_nt(grad_outer, mats_ref[1]) * slope).astype(BF16)
    grad_modal = dot_nt(grad_inner, mats_ref[0]).astype(BF16)
    grad_modal = from_mix_rows(grad_modal, modes, width)
    spectrum = dot(back_ref[...], grad_modal).astype(BF16)
    scatter_modes(send_ref, spectrum, modes)
    send_ref.flush()
    rows = 2 * block
    grads = [fold(dot_tn(modal_ref[...], grad_inner), width, block)]
    grads.append(fold(dot_tn(active_ref[...], grad_outer), width, block))
    bias_one = by_block(jnp.sum(grad_inner.astype(F32), axis=0, keepdims=True), width, block)
    bias_two = by_block(jnp.sum(grad_outer.astype(F32), axis=0, keepdims=True), width, block)
    gain = jnp.zeros((1, width), F32)
    shift = jnp.zeros((1, width), F32)
    for k in range(modes):
        lanes = slice(k * width, (k + 1) * width)
        upstream = grad_modal[:, lanes].astype(F32)
        gain = gain + jnp.sum(upstream * hat_ref[:, lanes], axis=0, keepdims=True)
        shift = shift + jnp.sum(upstream * ones_ref[:, k : k + 1], axis=0, keepdims=True)
    tail = jnp.concatenate(bias_one + bias_two + [gain, shift, jnp.zeros((2, width), F32)], axis=0)
    mlp = [mlp_ref[:, q : q + width] for q in range(0, mlp_ref.shape[1], width)]
    count = len(mlp) // 2
    rows = keep_ref.shape[0] - 2 * block - 8 - 8 * count
    rest = [jnp.zeros((rows, width), F32)] if rows else []
    for half, parts in enumerate(([grads[0], tail] + mlp[:count], [grads[1], jnp.zeros_like(tail)] + mlp[count:])):
        message = jnp.concatenate(parts + rest, axis=0).astype(BF16)
        for ref, core in ((keep_ref, half), (give_ref, 1 - half)):

            @pl.when(place_ref[0] == core)
            def _(ref=ref, message=message):
                ref[...] = message


def add_up(*values):
    total = values[0].astype(F32)
    for value in values[1:]:
        total = total + value.astype(F32)
    return total


def first_kernel(kept_ref, one_ref, in_ref, out_ref):
    for part, ref in enumerate((in_ref, out_ref)):
        ref[...] = add_up(kept_ref[part, 1], one_ref[part]).astype(BF16)


def second_kernel(kept_ref, in_ref, out_ref, mine_ref, core_ref, one_ref, small_ref, y_ref, x_ref):
    small_ref[...] = add_up(mine_ref[...], core_ref[...]).astype(BF16)
    for part, source, ref in ((0, in_ref, y_ref), (1, out_ref, x_ref)):
        ref[...] = add_up(kept_ref[part, 0, 1], one_ref[part], source[...]).astype(BF16)


def third_kernel(place_ref, kept_ref, in_ref, out_ref, y_ref, x_ref, *refs):
    small_refs, (one_ref, line_ref, own_ref), away_refs = refs[:4], refs[4:7], refs[7:]
    for z, ref in enumerate(small_refs):
        line_ref[(place_ref[0] >> 3) ^ z] = ref[...]
    for part, source, last in ((0, in_ref, y_ref), (1, out_ref, x_ref)):
        for z in range(4):
            total = add_up(kept_ref[part, 0, 0, z], one_ref[part, z], source[z], last[z])
            if z == 0:
                own_ref[part] = total
            else:
                away_refs[z - 1][part] = total.astype(BF16)


def plane_kernel(mine_ref, x_ref, y_ref, other_ref, total_ref):
    total_ref[...] = (add_up(mine_ref[...], x_ref[...]) + add_up(y_ref[...], other_ref[...])).astype(BF16)


def step_rest(
    block, scale, place_ref, own_ref, other_ref, mixer_ref, moment_ref, average_ref, vectors_ref, vec_moment_ref,
    vec_average_ref, new_mixer, new_moment, new_average, new_vectors, new_vec_moment, new_vec_average, grad_ref,
):
    groups, _, width = own_ref.shape
    joined = width // block
    rows = 2 * block
    slices = groups // 2
    core = place_ref[0]

    def held(half, group, part):
        mine, theirs = own_ref[group, part, :], other_ref[group, part, :]
        return jnp.where(core == half, mine, theirs).astype(F32)

    for group in range(groups):
        for layer in range(2):
            grad = held(layer, group, slice(0, rows)) * scale
            for part in range(2):
                for j in range(joined):
                    b = group * joined + j
                    piece = grad[part * block : (part + 1) * block, j * block : (j + 1) * block]
                    value, moment, average = update(
                        mixer_ref[layer, b, part], piece, moment_ref[layer, b, part], average_ref[layer, b, part],
                        WEIGHT_DECAY,
                    )
                    new_mixer[layer, b, part] = value
                    new_moment[layer, b, part] = moment
                    new_average[layer, b, part] = average
    for ref in (new_mixer, new_moment, new_average):
        ref.flush()
    for group in range(groups):
        tail = held(0, group, slice(rows, rows + 16))
        grad_ref[0:2, group * width : (group + 1) * width] = tail[4:6]
        for layer in range(2):
            for j in range(2):
                b = group * joined + (j if joined == 2 else 0)
                per_row = vectors_ref.shape[1] // (2 * block)
                lane = (b % per_row) * 2 * block + (0 if joined == 2 else j * block)
                row = 9 + layer * 2 + b // per_row
                grad_ref[row : row + 1, lane : lane + width] = tail[2 * layer + j : 2 * layer + j + 1]
    for half in range(2):
        part = slice(rows, rows + 8 + 8 * slices + 8 * ((slices + 1) % 2))
        total = held(half, 0, part)
        for group in range(1, groups):
            total = total + held(half, group, part)
        for q in range(slices):
            lane = (half * slices + q) * width
            grad_ref[2:9, lane : lane + width] = total[8 + 8 * q : 15 + 8 * q]
    value, moment, average = update(
        vectors_ref[...], grad_ref[0:13, :] * scale, vec_moment_ref[...], vec_average_ref[...], 0.0
    )
    new_vectors[...] = value
    new_vec_moment[...] = moment
    new_vec_average[...] = average


def step_all(block, scale, place_ref, *refs):
    step_rest(block, scale, place_ref, *refs[10:18], *refs[26:])
    step_weights(scale, *refs[:10], *refs[18:26])


def step_weights(scale, own_ref, *refs):
    away_refs, weights, new_weights = refs[:3], refs[3:9], refs[9:17]
    for part in range(2):
        total = add_up(own_ref[part], *[ref[part] for ref in away_refs])
        count = weights[part].shape[0]
        for q in range(total.shape[0] // count):
            lanes = slice(q * 128, (q + 1) * 128)
            grad = total[q * count : (q + 1) * count] * scale
            values = update(
                weights[part][:, lanes], grad, weights[2 + part][:, lanes], weights[4 + part][:, lanes], WEIGHT_DECAY
            )
            for i, value in enumerate(values):
                new_weights[2 * i + part][:, lanes] = value
            new_weights[6 + part][:, lanes] = values[0].astype(BF16)
    for ref in new_weights:
        ref.flush()


def load_weights(near, place_ref, pieces, part, target, sem):
    copies = []
    part = () if part is None else (part,)
    every = (slice(None),) * (1 - len(part))
    if not near:
        copies = [(pieces[0].at[(slice(None), *part)], target)]
    else:
        me = place_ref[0]
        at = [(me >> 1) & 1, (me >> 2) & 1, me & 1, me >> 3]
        size = pieces[0].shape[3]
        for i, ref in enumerate(pieces):
            for j in range(2):
                x, y = (i >> 1 & 1, j) if i & 1 else (j, i >> 1 & 1)
                for k in range(2):
                    z = 2 * (i & 1) + k
                    row = (((at[3] ^ z) * 2 + (at[1] ^ y)) * 2 + (at[0] ^ (i >> 2))) * size
                    rows = pl.ds(pl.multiple_of(row, size), size)
                    copies.append((ref.at[(j, k, *part)], target.at[(at[2] ^ x, *every, rows)]))
    for source, place in copies:
        pltpu.make_async_copy(source, place, sem).start(priority=1)
    return pltpu.make_async_copy(target, target, sem)


def place_rows(ref, values, columns, orders):
    if not orders:
        ref[:, columns] = values
        return
    size = values.shape[0] // len(orders)
    for block, order in enumerate(orders):
        ref[pl.ds(pl.multiple_of(order * size, size), size), columns] = values[block * size : (block + 1) * size]


def mlp_kernel(
    groups, near, place_ref, got_ref, wide_t_ref, tokens_ref, cotangent_ref, vectors_ref, bias_ref, wide_ref, *refs
):
    count = 8 if near else 1
    pieces, refs = refs[:count], refs[count:]
    active, total_ref, middle_ref, send_ref, small_ref, *refs = refs
    grad_refs, refs = refs[:2], refs[2:]
    normed, normed_t, cotangent_t, normal, spread, weights, grad_hidden, sem = refs
    arrival = load_weights(near, place_ref, pieces, None, weights, sem)
    cotangent_ref.start()
    wide_ref.start()
    w_in, w_out = weights.at[:, 0], weights.at[:, 1]
    me = place_ref[0]
    orders = [((z ^ (me >> 3)) + 4 * (y ^ ((me >> 2) & 1)) + 8 * (c ^ ((me >> 1) & 1))) for z in range(4) for y in range(2) for c in range(2)]
    orders = orders if near else []
    tokens, width = tokens_ref.shape
    halves, _, columns = w_in.shape
    gain, shift, bias_out = vectors_ref[2:3, :], vectors_ref[3:4, :], vectors_ref[4:5, :]
    row_blocks = [slice(r, r + ROWS) for r in range(0, tokens, ROWS)]
    spectra = spans(gather_lanes(got_ref, groups))
    span = wide_t_ref.shape[0]
    bias_out_grad = jnp.zeros((1, width), F32)
    for rows in row_blocks:
        first = rows.start % span
        spatial = dot(wide_t_ref[first : first + ROWS, :], spectra[rows.start // span])
        middle = tokens_ref[rows, :].astype(F32) + spatial
        unit, inverse = normalize(middle)
        normal[rows, :] = unit
        spread[rows, :] = inverse
        scaled = (unit * gain + shift).astype(BF16)
        normed[rows, :] = scaled
        place_rows(normed_t, scaled.T, rows, orders)
        total_ref[rows, :] = middle + bias_out
        upstream = cotangent_ref[rows, :]
        place_rows(cotangent_t, upstream.T, rows, orders)
        bias_out_grad = bias_out_grad + jnp.sum(upstream.astype(F32), axis=0, keepdims=True)
    total_ref.flush()
    arrival.wait()
    gain_grad = jnp.zeros((1, width), F32)
    shift_grad = jnp.zeros((1, width), F32)
    chunks = [(h, c) for h in range(halves) for c in range(0, columns, CHUNK)]
    bias_grads = [jnp.zeros((1, CHUNK), F32) for _ in chunks]
    for rows in row_blocks:
        for i, (h, c) in enumerate(chunks):
            lanes, flat = slice(c, c + CHUNK), slice(h * columns + c, h * columns + c + CHUNK)
            hidden = dot(normed[rows, :], w_in[h, :, lanes]) + bias_ref[i : i + 1, :]
            value, slope = gelu_pair(hidden.astype(BF16))
            active[rows, flat] = value.astype(BF16)
            back = (dot(cotangent_ref[rows, :], w_out[h, :, lanes]) * slope).astype(BF16)
            grad_hidden[rows, flat] = back
            bias_grads[i] = bias_grads[i] + jnp.sum(back.astype(F32), axis=0, keepdims=True)
        back = dot_nt(grad_hidden[rows, :columns], w_in[0])
        for h in range(1, halves):
            back = back + dot_nt(grad_hidden[rows, h * columns : (h + 1) * columns], w_in[h])
        unit = normal[rows, :]
        gain_grad = gain_grad + jnp.sum(back * unit, axis=0, keepdims=True)
        shift_grad = shift_grad + jnp.sum(back, axis=0, keepdims=True)
        middle = cotangent_ref[rows, :].astype(F32) + norm_back(back, unit, spread[rows, :], gain)
        middle_ref[rows, :] = middle.astype(BF16)
    active.flush()
    middle_ref.flush()
    small_ref[0:3, :] = jnp.concatenate([gain_grad, shift_grad, bias_out_grad], axis=0)
    small_ref[3:7, :] = jnp.concatenate(bias_grads, axis=0)
    small_ref[7:8, :] = jnp.zeros((1, width), F32)
    scatter_lanes(send_ref, along_w(wide_ref, middle_ref, tokens), groups)
    send_ref.flush()
    for i, (h, c) in enumerate(chunks):
        flat = slice(h * columns + c, h * columns + c + CHUNK)
        grads = [
            dot(normed_t[...], grad_hidden[:, flat]).astype(BF16), dot(cotangent_t[...], active[:, flat]).astype(BF16)
        ]
        if not near:
            for ref, grad in zip(grad_refs, grads, strict=True):
                ref[h, :, c : c + CHUNK] = grad
            continue
        size = w_in.shape[1] // 16
        x = h ^ (me & 1)
        for core, ref in enumerate(grad_refs):
            for y in range(2):
                for z in range(4):
                    block = core * 8 + y * 4 + z
                    rows = slice(block * size, (block + 1) * size)
                    for q in range(CHUNK // 128):
                        lanes = slice(q * 128, (q + 1) * 128)
                        place = slice((c // 128 + q) * size, (c // 128 + q + 1) * size)
                        ref[0, x, y, z, place, :] = grads[0][rows, lanes]
                        ref[1, y, x, z, place, :] = grads[1][rows, lanes]


def output_kernel(near, place_ref, *refs):
    count = 8 if near else 1
    totals, actives, pieces = refs[:OUT_BLOCKS], refs[OUT_BLOCKS : 2 * OUT_BLOCKS], refs[2 * OUT_BLOCKS :][:count]
    outputs, w_out, sem = refs[2 * OUT_BLOCKS + count], *refs[2 * OUT_BLOCKS + count + 1 :]
    load_weights(near, place_ref, pieces, 1, w_out, sem).wait()
    halves, _, columns = w_out.shape
    size = totals[0].shape[0]
    for i, (total, active) in enumerate(zip(totals, actives, strict=True)):
        value = total[...]
        for h in range(halves):
            value = value + dot_nt(active[:, h * columns : (h + 1) * columns], w_out[h])
        outputs[i * size : (i + 1) * size, :] = value.astype(BF16)


def leave_kernel(groups, got_ref, tokens_ref, middle_ref, vectors_ref, table_ref, out_ref):
    spectra = spans(gather_lanes(got_ref, groups))
    span = table_ref.shape[0]
    for start in range(0, tokens_ref.shape[0], ROWS):
        rows = slice(start, start + ROWS)
        first = start % span
        upstream = dot(table_ref[first : first + ROWS, :], spectra[start // span])
        unit, inverse = normalize(tokens_ref[rows, :].astype(F32))
        back = norm_back(upstream, unit, inverse, vectors_ref[0:1, :])
        out_ref[rows, :] = (middle_ref[rows, :].astype(F32) + back).astype(BF16)


def update(weight, gradient, moment, average, decay_rate):
    step_grad = gradient + decay_rate * weight
    new_moment = MOMENTUM * moment + step_grad
    new_weight = weight - LEARNING_RATE * (step_grad + MOMENTUM * new_moment)
    new_average = AVERAGE * average + (1.0 - AVERAGE) * new_weight
    return (new_weight, new_moment, new_average)


class Source:
    def __init__(self, ref, copy):
        self.ref, self.copy, self.shape, self.started = ref, copy, ref.shape, False

    def start(self):
        if not self.started:
            self.copy.start()
            self.started = True

    def __getitem__(self, index):
        if self.copy is not None:
            self.start()
            self.copy.wait()
            self.copy = None
        return self.ref[index]


class Sink:
    def __init__(self, ref, copy):
        self.ref, self.copy, self.shape, self.sent = ref, copy, ref.shape, False

    def __getitem__(self, index):
        return self.ref[index]

    def __setitem__(self, index, value):
        self.ref[index] = value

    def flush(self):
        if not self.sent:
            self.copy.start()
            self.sent = True


class Far:
    def __init__(self, *what):
        self.what = what


class Late(Far):
    pass


def call(body, outs, *args, scalars=(), raw=(), scratch=(), flops=0, carry=(), cost=None, vmem=20):
    near, far, there = [pl.BlockSpec(memory_space=m) for m in (pltpu.VMEM, pltpu.HBM, pl.ANY)]
    in_far, out_far = [isinstance(a, Far) for a in args], [isinstance(o, Far) for o in outs]
    in_late = [isinstance(a, Late) for a in args]
    index = [a.what[1:] if f else () for a, f in zip(args, in_far, strict=True)]
    args = [
        pltpu.with_memory_space_constraint(*((a.what[0], pltpu.HBM) if f else (a, pltpu.VMEM)))
        for a, f in zip(args, in_far, strict=True)
    ]
    raw = [pltpu.with_memory_space_constraint(a, pltpu.HBM) for a in raw]
    outs = [o.what if f else o for o, f in zip(outs, out_far, strict=True)]
    outs = [jax.ShapeDtypeStruct(s, d) for s, d in outs]
    n_scalar, n_in, n_raw, n_carry, n_out = len(scalars), len(args), len(raw), len(carry), len(outs)
    shapes = [np.empty(a.shape, np.bool_)[i].shape if i else a.shape for a, i in zip(args, index, strict=True)]
    shapes += [o.shape for o in outs]
    buffers = [
        pltpu.VMEM(shape, a.dtype) for shape, a, f in zip(shapes, args + outs, in_far + out_far, strict=True) if f
    ]

    def inner(*refs):
        refs = list(refs)

        def take(count):
            taken = refs[:count]
            del refs[:count]
            return taken

        scalar_refs, in_refs, raw_refs, _, out_refs, _ = [
            take(n) for n in (n_scalar, n_in, n_raw, n_carry, n_out, n_carry)
        ]
        space = take(len(buffers))
        sems = take(1)[0] if buffers else None
        sources, sinks, used = [], [], 0
        for ref, away, part, late in zip(in_refs, in_far, index, in_late, strict=True):
            if away:
                copy = pltpu.make_async_copy(ref.at[part] if part else ref, space[used], sems.at[used])
                ref = Source(space[used], copy)
                if not late:
                    ref.start()
                used += 1
            sources.append(ref)
        for ref, away in zip(out_refs, out_far, strict=True):
            if away:
                ref = Sink(space[used], pltpu.make_async_copy(space[used], ref, sems.at[used]))
                used += 1
            sinks.append(ref)
        body(*scalar_refs, *sources, *raw_refs, *sinks, *refs)
        for source in sources:
            if isinstance(source, Source) and source.copy is not None:
                source.copy.wait()
        sinks = [sink for sink in sinks if isinstance(sink, Sink)]
        for sink in sinks:
            sink.flush()
        for sink in sinks:
            sink.copy.wait()

    every = list(args) + list(raw)
    size = sum(math.prod(a.shape) * a.dtype.itemsize for a in every + outs) if cost is None else cost
    sems = [pltpu.SemaphoreType.DMA((len(buffers),))] if buffers else []
    return pl.pallas_call(
        inner,
        out_shape=[(pltpu.HBM if f else pltpu.VMEM)(o.shape, o.dtype) for o, f in zip(outs, out_far, strict=True)]
        + [jax.ShapeDtypeStruct(a.shape, a.dtype) for a in carry],
        in_specs=[pl.BlockSpec(memory_space=pltpu.SMEM)] * n_scalar
        + [far if f else near for f in in_far]
        + [far] * n_raw
        + [there] * n_carry,
        out_specs=[far if f else near for f in out_far] + [there] * n_carry,
        scratch_shapes=buffers + sems + list(scratch),
        input_output_aliases={n_scalar + n_in + n_raw + i: n_out + i for i in range(n_carry)},
        compiler_params=pltpu.CompilerParams(vmem_limit_bytes=vmem << 20),
        cost_estimate=pl.CostEstimate(flops=flops, bytes_accessed=size, transcendentals=0),
    )(*scalars, *args, *raw, *carry)


def on_device(
    tokens, cotangent, w_in, w_out, mixer_weights, vectors, w_in_moment, w_out_moment, mixer_moment, vectors_moment,
    w_in_average, w_out_average, mixer_average, vectors_average,
):
    sp_count, tp_count = lax.axis_size("sp"), lax.axis_size("tp")
    devices = sp_count * tp_count
    grid_rows, grid, width = tokens.shape
    local = grid_rows * grid
    items = grid_rows * devices // grid
    block_count, block = mixer_weights.shape[1], mixer_weights.shape[3]
    hidden = w_in.shape[1] * tp_count
    model = w_in.shape[0] * sp_count
    lanes = 2 * block if devices * 2 * block <= MODES * width else block
    groups = width // lanes
    per_group = devices // groups
    modes = MODES // per_group
    joined = lanes // block
    scale = 1.0 / math.sqrt(local * devices)
    wide_f, wide_i, high, ones = expanded_tables(grid, items)
    me = lax.axis_index("sp") * tp_count + lax.axis_index("tp")
    group = me // per_group
    exchange = functools.partial(lax.all_to_all, axis_name=AXES, split_axis=0, concat_axis=0, tiled=True)
    chunk = (devices, modes * grid_rows * 2, lanes)
    rows_all = tokens.reshape(local, width)
    upstream_all = cotangent.reshape(local, width)
    shard_rows, shard_columns = w_in.shape
    shard_size = shard_rows * shard_columns // 128
    near = devices == 32 and per_group == 8 and shard_rows % 16 == 0

    def permute(values, mask):
        return lax.ppermute(values, AXES, [(d, d ^ mask) for d in range(devices)])

    pair = jnp.stack([w_in.astype(BF16), w_out.astype(BF16)])
    if near:
        line = [pair] + [permute(pair, 8 * z) for z in (1, 2, 3)]
        carried = [jnp.stack([v, permute(v, m)]) for v, m in ((jnp.stack(line[:2]), 1), (jnp.stack(line[2:]), 4))]
    else:
        weights = lax.all_gather(pair, "sp", axis=1, tiled=True)
        pieces, carried = [lax.all_gather(weights, "tp")], []

    own_mixer = lax.dynamic_slice_in_dim(mixer_weights, group * joined, joined, 1).astype(BF16)
    eye = jnp.eye(joined, dtype=BF16)
    real = jnp.einsum("lbio,bc->lbico", own_mixer[:, :, 0], eye).reshape(2, lanes, lanes)
    imag = jnp.einsum("lbio,bc->lbico", own_mixer[:, :, 1], eye).reshape(2, lanes, lanes)
    mats = jnp.concatenate(
        [jnp.concatenate([real, imag], axis=2), jnp.concatenate([-imag, real], axis=2)], axis=1
    )
    own_bias = lax.dynamic_slice_in_dim(
        vectors[9:13].reshape(2, block_count, 2, block), group * joined, joined, 1
    )
    own_bias = jnp.swapaxes(own_bias, 1, 2).reshape(2, 2 * lanes)
    own_gain = lax.dynamic_slice_in_dim(vectors[0:1], group * lanes, lanes, 1)
    own_shift = lax.dynamic_slice_in_dim(vectors[1:2], group * lanes, lanes, 1)
    ones = jnp.asarray(np.swapaxes(ones.reshape(per_group, modes, -1), 1, 2))
    own_ones = lax.dynamic_index_in_dim(ones, me % per_group, 0, keepdims=False)

    wide_f, wide_f_t = jnp.asarray(wide_f), jnp.asarray(wide_f.T)
    wide_i, wide_i_t = jnp.asarray(wide_i), jnp.asarray(wide_i.T)
    high, high_t = jnp.asarray(high), jnp.asarray(high.T)
    wide_flops = 2 * MODES * 2 * local * width * SPAN
    (sent,) = call(
        functools.partial(enter_kernel, groups), [(chunk, BF16)], Far(rows_all), Far(wide_f), flops=wide_flops
    )
    got = exchange(sent)
    half_rows = items * MODES
    sent, hat, modal, inner, active, *carried = call(
        functools.partial(mix_kernel, modes),
        [
            (chunk, BF16),
            Far((2 * half_rows, modes * lanes), F32),
            Far((modes * half_rows, 2 * lanes), BF16),
            Far((modes * half_rows, 2 * lanes), F32),
            Far((modes * half_rows, 2 * lanes), BF16),
        ],
        got, high, high_t, mats, own_bias, own_gain, own_shift, own_ones,
        carry=carried,
    )
    if near:
        pieces = carried + [permute(carried[0], 4), permute(carried[1], 1)]
        pieces += [permute(p, 2) for p in pieces]
    got = exchange(sent)
    steps = hidden // CHUNK
    grads = [((2, 2, 2, 4, shard_size, 128), BF16)] * 2 if near else [((tp_count, model, shard_columns), BF16)] * 2
    gelus, total, middle, sent, mlp_small, *grads = call(
        functools.partial(mlp_kernel, groups, near),
        [
            Far((local, hidden), BF16), Far((local, width), F32), Far((local, width), BF16), Far(chunk, BF16),
            ((8, width), F32),
        ]
        + grads,
        Far(got), Far(wide_i_t), Far(rows_all), Late(upstream_all), vectors, vectors[5:9].reshape(steps, CHUNK), Late(wide_i),
        scalars=[me[None]], raw=pieces,
        scratch=[
            pltpu.VMEM((local, width), BF16),
            pltpu.VMEM((width, local), BF16),
            pltpu.VMEM((width, local), BF16),
            pltpu.VMEM((local, width), F32),
            pltpu.VMEM((local, 1), F32),
            pltpu.VMEM((tp_count, 2, model, shard_columns), BF16),
            pltpu.VMEM((local, hidden), BF16),
            pltpu.SemaphoreType.DMA,
        ],
        flops=12 * local * width * hidden + 2 * wide_flops, vmem=44,
    )

    carried = []
    if near:
        shard = (4, shard_size, 128)
        kept, one = grads[0], permute(grads[1], 2)
        sent_in, sent_out = call(
            first_kernel, [((2,) + shard, BF16)] * 2, kept, Far(one, slice(None), 1), cost=0
        )
        carried = [permute(sent_in, 1), permute(sent_out, 4)]

    step = local // OUT_BLOCKS
    parts = [slice(r, r + step) for r in range(0, local, step)]
    (output,) = call(
        functools.partial(output_kernel, near), [Far((local, width), BF16)],
        *[Far(total, rows) for rows in parts], *[Far(gelus, rows) for rows in parts],
        scalars=[me[None]], raw=pieces, cost=COST, vmem=24,
        scratch=[
            pltpu.VMEM((tp_count, model, shard_columns), BF16),
            pltpu.SemaphoreType.DMA,
        ],
    )

    got = exchange(sent)
    small_rows = -(-(2 * block + 8 + 8 * (groups // 2)) // 16) * 16
    place = ((me >> 1) & 1 if near else jnp.int32(0))[None]
    sent, small, given, output = call(
        functools.partial(unmix_kernel, modes, block),
        [Far(chunk, BF16), ((small_rows, lanes), BF16), ((small_rows, lanes), BF16)],
        got, Far(high), Far(high_t), Far(mats), own_ones, Far(hat), Far(modal), Far(inner), Far(active), mlp_small,
        scalars=[place], cost=COST, vmem=20 if near else 48, carry=[output],
    )
    if near:
        both = slice(None)
        small, over_y, over_x = call(
            second_kernel, [((small_rows, lanes), BF16)] + [(shard, BF16)] * 2,
            kept, *[Far(a, 1) for a in carried], small, permute(given, 2), Far(one, both, 0, 1), cost=0,
        )
        line, own, *away = call(
            third_kernel,
            [((4, small_rows, lanes), BF16), ((2, shard_size, 128), F32)] + [((2, shard_size, 128), BF16)] * 3,
            kept, *[Far(a, 0) for a in carried], permute(over_y, 4), permute(over_x, 1),
            small, *[permute(small, 8 * z) for z in (1, 2, 3)], Far(one, both, 0, 0),
            scalars=[me[None]], cost=0,
        )
        away = [permute(a, 8 * (z + 1)) for z, a in enumerate(away)]
    got = exchange(sent)
    (grad_tokens,) = call(
        functools.partial(leave_kernel, groups),
        [Far((local, width), BF16)],
        got, Far(rows_all), Far(middle), vectors, Far(wide_f_t), cost=COST,
    )

    if near:
        line, *away, grad_tokens = call(
            plane_kernel, [(line.shape, BF16)], line, *[permute(line, m) for m in (1, 4, 5)], cost=0, carry=[*away, grad_tokens]
        )
        other = permute(line, 2)

    state = [mixer_weights, mixer_moment, mixer_average, vectors, vectors_moment, vectors_average]
    new_state = [Far(a.shape, F32) for a in state]
    if near:
        weights = [w_in, w_out, w_in_moment, w_out_moment, w_in_average, w_out_average]
        *stepped, grad_tokens = call(
            functools.partial(step_all, block, scale),
            [Far(w_in.shape, F32)] * 6 + [Far(w_in.shape, BF16)] * 2 + new_state,
            own, *away, *weights, line, other, *state,
            scalars=[place], scratch=[pltpu.VMEM((16, width), F32)], carry=[grad_tokens], cost=0,
        )
        new_in, new_out = stepped[0:8:2], stepped[1:8:2]
        stepped = stepped[8:]
    else:
        grads = jnp.stack(grads).astype(F32)
        grads = lax.psum_scatter(grads, "tp", scatter_dimension=1, tiled=True)
        grads = lax.psum_scatter(grads, "sp", scatter_dimension=2, tiled=True)
        new_in = update(w_in, grads[0, 0] * scale, w_in_moment, w_in_average, WEIGHT_DECAY)
        new_out = update(w_out, grads[1, 0] * scale, w_out_moment, w_out_average, WEIGHT_DECAY)
        new_in, new_out = new_in + (new_in[0].astype(BF16),), new_out + (new_out[0].astype(BF16),)
        onehot = (jnp.arange(groups, dtype=jnp.int32) == group).astype(F32)[:, None, None]
        line, other = lax.psum((onehot * small.astype(F32), onehot * given.astype(F32)), AXES)
        stepped = call(
            functools.partial(step_rest, block, scale), new_state, line, other, *state,
            scalars=[place], scratch=[pltpu.VMEM((16, width), F32)],
        )
    new_mix, new_vec = stepped[0:3], stepped[3:6]
    shape = tokens.shape
    return (
        output.reshape(shape), grad_tokens.reshape(shape),
        new_in[0], new_out[0], new_mix[0], new_vec[0],
        new_in[1], new_out[1], new_mix[1], new_vec[1],
        new_in[2], new_out[2], new_mix[2], new_vec[2],
        new_in[3], new_out[3],
    )


def solution(mesh):
    rows, split, whole = P(AXES, None, None), P("sp", "tp"), P()
    state = (split, split, whole, whole)
    return jax.shard_map(
        on_device,
        mesh=mesh,
        in_specs=(rows, rows) + state * 3,
        out_specs=(rows, rows) + state * 3 + (split, split),
        check_vma=False,
    )
```

```python
import functools
import math

import jax
import jax.numpy as jnp
import ml_dtypes
import numpy as np
from jax import lax
from jax.experimental import pallas as pl
from jax.experimental.pallas import tpu as pltpu
from jax.sharding import PartitionSpec as P

MODES = 32
EPSILON = 1e-05
LEARNING_RATE = 0.05
MOMENTUM = 0.9
WEIGHT_DECAY = 0.0001
AVERAGE = 0.75
GELU_SCALE = math.sqrt(2.0 / math.pi)
GELU_CUBE = 0.044715
CHUNK = 512
ROWS = 256
SPAN = 4
BF16 = jnp.bfloat16
F32 = jnp.float32
AXES = ("sp", "tp")
COST = 60 << 20
OUT_BLOCKS = 4


def dft_tables(grid):
    positions = np.arange(grid)
    wave = np.arange(MODES)
    root = np.float32(1.0 / math.sqrt(grid))
    step = np.float32(2.0 * math.pi / grid)
    phase_w = (positions[:, None] * wave[None, :] % grid).astype(np.float32) * step
    factor = np.where(wave == 0, 1.0, 2.0).astype(np.float32)
    cos_w, sin_w = np.cos(phase_w) * root, np.sin(phase_w) * root
    forward_w = np.stack([cos_w, -sin_w], axis=1)
    inverse_w = np.stack([cos_w * factor, -sin_w * factor], axis=1)
    frequency = np.where(wave < MODES // 2, wave, wave - MODES)
    phase_h = (frequency[:, None] * positions[None, :] % grid).astype(np.float32) * step
    cos_h, sin_h = np.cos(phase_h) * root, np.sin(phase_h) * root
    forward_h = np.stack([np.stack([cos_h, -sin_h], -1), np.stack([sin_h, cos_h], -1)], -2)
    return [t.astype(ml_dtypes.bfloat16) for t in (forward_w, inverse_w, forward_h)]


def expanded_tables(grid, items):
    forward_w, inverse_w, forward_h = [t.astype(np.float32) for t in dft_tables(grid)]
    eye_r = np.eye(SPAN, dtype=np.float32)
    wide_f = np.einsum("wek,rs->kresw", forward_w, eye_r).reshape(-1, SPAN * grid)
    wide_i = np.einsum("wek,rs->kresw", inverse_w, eye_r).reshape(-1, SPAN * grid)
    eye_i = np.eye(items, dtype=np.float32)
    high = np.einsum("mhef,ij->fimhje", forward_h, eye_i).reshape(2 * items * MODES, -1)
    ones = np.einsum("mhef,ek->kfm", forward_h.astype(np.float64), forward_w.astype(np.float64).sum(0))
    ones = np.repeat(ones[:, :, None], items, axis=2).reshape(MODES, -1).astype(np.float32)
    cast = [t.astype(ml_dtypes.bfloat16) for t in (wide_f, wide_i, high)]
    return cast[0], cast[1], cast[2], ones


def dot(left, right):
    return jnp.dot(left, right, preferred_element_type=F32)


def dot_nt(left, right):
    return lax.dot_general(left, right, (((1,), (1,)), ((), ())), preferred_element_type=F32)


def dot_tn(left, right):
    return lax.dot_general(left, right, (((0,), (0,)), ((), ())), preferred_element_type=F32)


def normalize(values):
    center = values - jnp.mean(values, axis=-1, keepdims=True)
    inverse = lax.rsqrt(jnp.mean(center * center, axis=-1, keepdims=True) + EPSILON)
    return center * inverse, inverse


def norm_back(upstream, normal, inverse, gain):
    scaled = upstream * gain
    centered = scaled - jnp.mean(scaled, axis=-1, keepdims=True)
    centered = centered - normal * jnp.mean(scaled * normal, axis=-1, keepdims=True)
    return centered * inverse


def gelu_pair(values):
    square = values * values
    bent = jnp.tanh(values * (GELU_SCALE + (GELU_SCALE * GELU_CUBE) * square))
    half = 0.5 + 0.5 * bent
    slope = half + (values * half) * (1.0 - bent) * (GELU_SCALE + (3.0 * GELU_SCALE * GELU_CUBE) * square)
    return values * half, slope


def gelu_value(values):
    square = values * values
    bent = jnp.tanh(values * (GELU_SCALE + (GELU_SCALE * GELU_CUBE) * square))
    return values * (0.5 + 0.5 * bent)


def along_w(table_ref, values, rows):
    table = table_ref[...]
    span = table.shape[1]
    parts = [dot(table, values[r : r + span]).reshape(MODES, -1, values.shape[1]) for r in range(0, rows, span)]
    return jnp.concatenate(parts, axis=1).reshape(-1, values.shape[1]).astype(BF16)


def spans(spectrum):
    whole = spectrum.astype(F32).reshape(MODES, -1, spectrum.shape[1])
    size = 2 * SPAN
    return [
        whole[:, r : r + size].reshape(MODES * size, -1).astype(BF16) for r in range(0, whole.shape[1], size)
    ]


def gather_lanes(ref, groups):
    count = ref.shape[0] // groups
    width = ref.shape[2]
    parts = [ref[g * count : (g + 1) * count].reshape(count * ref.shape[1], width) for g in range(groups)]
    return parts[0] if groups == 1 else jnp.concatenate(parts, axis=1)


def scatter_lanes(ref, values, groups):
    count = ref.shape[0] // groups
    width = ref.shape[2]
    for g in range(groups):
        piece = values[:, g * width : (g + 1) * width]
        ref[g * count : (g + 1) * count] = piece.reshape(count, ref.shape[1], width)


def gather_modes(ref, modes):
    rows = ref.shape[1] // modes
    parts = [
        ref[:, k * rows : (k + 1) * rows, :].reshape(ref.shape[0] * rows, ref.shape[2]) for k in range(modes)
    ]
    return parts[0] if modes == 1 else jnp.concatenate(parts, axis=1)


def scatter_modes(ref, values, modes):
    rows = ref.shape[1] // modes
    width = ref.shape[2]
    for k in range(modes):
        piece = values[:, k * width : (k + 1) * width]
        ref[:, k * rows : (k + 1) * rows, :] = piece.reshape(ref.shape[0], rows, width)


def to_mix_rows(values, modes, width):
    half = values.shape[0] // 2
    parts = []
    for k in range(modes):
        piece = values[:, k * width : (k + 1) * width]
        parts.append(jnp.concatenate([piece[:half], piece[half:]], axis=1))
    return parts[0] if modes == 1 else jnp.concatenate(parts, axis=0)


def from_mix_rows(values, modes, width):
    half = values.shape[0] // modes
    parts = []
    for k in range(modes):
        piece = values[k * half : (k + 1) * half]
        parts.append(jnp.concatenate([piece[:, :width], piece[:, width:]], axis=0))
    return parts[0] if modes == 1 else jnp.concatenate(parts, axis=1)


def enter_kernel(groups, tokens_ref, table_ref, send_ref):
    normal, _ = normalize(tokens_ref[...].astype(F32))
    scatter_lanes(send_ref, along_w(table_ref, normal.astype(BF16), normal.shape[0]), groups)


def mix_kernel(
    modes, got_ref, high_ref, back_ref, mats_ref, bias_ref, gain_ref, shift_ref, ones_ref,
    send_ref, hat_ref, modal_ref, inner_ref, active_ref,
):
    width = got_ref.shape[2]
    hat = dot(high_ref[...], gather_modes(got_ref, modes))
    hat_ref[...] = hat
    hat_ref.flush()
    pieces = []
    for k in range(modes):
        piece = hat[:, k * width : (k + 1) * width] * gain_ref[...]
        pieces.append(piece + ones_ref[:, k : k + 1] * shift_ref[...])
    modal = pieces[0] if modes == 1 else jnp.concatenate(pieces, axis=1)
    modal = to_mix_rows(modal.astype(BF16), modes, width)
    modal_ref[...] = modal
    modal_ref.flush()
    inner = dot(modal, mats_ref[0]) + bias_ref[0:1, :]
    inner_ref[...] = inner
    inner_ref.flush()
    active = gelu_value(inner).astype(BF16)
    active_ref[...] = active
    active_ref.flush()
    outer = (dot(active, mats_ref[1]) + bias_ref[1:2, :]).astype(BF16)
    gridded = dot(back_ref[...], from_mix_rows(outer, modes, width)).astype(BF16)
    scatter_modes(send_ref, gridded, modes)


def fold(grad, width, block):
    real = grad[:width, :width] + grad[width:, width:]
    imag = grad[:width, width:] - grad[width:, :width]
    out = []
    for part in (real, imag):
        if width == block:
            out.append(part)
        else:
            lane = lax.broadcasted_iota(jnp.int32, (block, width), 1)
            out.append(jnp.where(lane < block, part[:block], part[block:]))
    return jnp.concatenate(out, axis=0)


def by_block(sums, width, block):
    real, imag = sums[:, :width], sums[:, width:]
    if width == block:
        return [real, imag]
    lane = lax.broadcasted_iota(jnp.int32, real.shape, 1)
    turned_real, turned_imag = pltpu.roll(real, block, 1), pltpu.roll(imag, block, 1)
    return [jnp.where(lane < block, real, turned_imag), jnp.where(lane < block, turned_real, imag)]


def unmix_kernel(
    modes, block, place_ref, got_ref, high_ref, back_ref, mats_ref, ones_ref, hat_ref, modal_ref, inner_ref, active_ref,
    mlp_ref, send_ref, keep_ref, give_ref,
):
    width = got_ref.shape[2]
    grad_outer = dot(high_ref[...], gather_modes(got_ref, modes)).astype(BF16)
    grad_outer = to_mix_rows(grad_outer, modes, width)
    _, slope = gelu_pair(inner_ref[...])
    grad_inner = (dot_nt(grad_outer, mats_ref[1]) * slope).astype(BF16)
    grad_modal = dot_nt(grad_inner, mats_ref[0]).astype(BF16)
    grad_modal = from_mix_rows(grad_modal, modes, width)
    spectrum = dot(back_ref[...], grad_modal).astype(BF16)
    scatter_modes(send_ref, spectrum, modes)
    send_ref.flush()
    rows = 2 * block
    grads = [fold(dot_tn(modal_ref[...], grad_inner), width, block)]
    grads.append(fold(dot_tn(active_ref[...], grad_outer), width, block))
    bias_one = by_block(jnp.sum(grad_inner.astype(F32), axis=0, keepdims=True), width, block)
    bias_two = by_block(jnp.sum(grad_outer.astype(F32), axis=0, keepdims=True), width, block)
    gain = jnp.zeros((1, width), F32)
    shift = jnp.zeros((1, width), F32)
    for k in range(modes):
        lanes = slice(k * width, (k + 1) * width)
        upstream = grad_modal[:, lanes].astype(F32)
        gain = gain + jnp.sum(upstream * hat_ref[:, lanes], axis=0, keepdims=True)
        shift = shift + jnp.sum(upstream * ones_ref[:, k : k + 1], axis=0, keepdims=True)
    tail = jnp.concatenate(bias_one + bias_two + [gain, shift, jnp.zeros((2, width), F32)], axis=0)
    mlp = [mlp_ref[:, q : q + width] for q in range(0, mlp_ref.shape[1], width)]
    count = len(mlp) // 2
    rows = keep_ref.shape[0] - 2 * block - 8 - 8 * count
    rest = [jnp.zeros((rows, width), F32)] if rows else []
    for half, parts in enumerate(([grads[0], tail] + mlp[:count], [grads[1], jnp.zeros_like(tail)] + mlp[count:])):
        message = jnp.concatenate(parts + rest, axis=0).astype(BF16)
        for ref, core in ((keep_ref, half), (give_ref, 1 - half)):

            @pl.when(place_ref[0] == core)
            def _(ref=ref, message=message):
                ref[...] = message


def add_up(*values):
    total = values[0].astype(F32)
    for value in values[1:]:
        total = total + value.astype(F32)
    return total


def first_kernel(kept_ref, one_ref, in_ref, out_ref):
    for part, ref in enumerate((in_ref, out_ref)):
        ref[...] = add_up(kept_ref[part, 1], one_ref[part]).astype(BF16)


def second_kernel(kept_ref, in_ref, out_ref, mine_ref, core_ref, one_ref, small_ref, y_ref, x_ref):
    small_ref[...] = add_up(mine_ref[...], core_ref[...]).astype(BF16)
    for part, source, ref in ((0, in_ref, y_ref), (1, out_ref, x_ref)):
        ref[...] = add_up(kept_ref[part, 0, 1], one_ref[part], source[...]).astype(BF16)


def third_kernel(place_ref, kept_ref, in_ref, out_ref, y_ref, x_ref, *refs):
    small_refs, (one_ref, line_ref, own_ref), away_refs = refs[:4], refs[4:7], refs[7:]
    for z, ref in enumerate(small_refs):
        line_ref[(place_ref[0] >> 3) ^ z] = ref[...]
    for part, source, last in ((0, in_ref, y_ref), (1, out_ref, x_ref)):
        for z in range(4):
            total = add_up(kept_ref[part, 0, 0, z], one_ref[part, z], source[z], last[z])
            if z == 0:
                own_ref[part] = total
            else:
                away_refs[z - 1][part] = total.astype(BF16)


def plane_kernel(mine_ref, x_ref, y_ref, other_ref, total_ref):
    total_ref[...] = (add_up(mine_ref[...], x_ref[...]) + add_up(y_ref[...], other_ref[...])).astype(BF16)


def step_rest(
    block, scale, place_ref, own_ref, other_ref, mixer_ref, moment_ref, average_ref, vectors_ref, vec_moment_ref,
    vec_average_ref, new_mixer, new_moment, new_average, new_vectors, new_vec_moment, new_vec_average, grad_ref,
):
    groups, _, width = own_ref.shape
    joined = width // block
    rows = 2 * block
    slices = groups // 2
    core = place_ref[0]

    def held(half, group, part):
        mine, theirs = own_ref[group, part, :], other_ref[group, part, :]
        return jnp.where(core == half, mine, theirs).astype(F32)

    for group in range(groups):
        for layer in range(2):
            grad = held(layer, group, slice(0, rows)) * scale
            for part in range(2):
                for j in range(joined):
                    b = group * joined + j
                    piece = grad[part * block : (part + 1) * block, j * block : (j + 1) * block]
                    value, moment, average = update(
                        mixer_ref[layer, b, part], piece, moment_ref[layer, b, part], average_ref[layer, b, part],
                        WEIGHT_DECAY,
                    )
                    new_mixer[layer, b, part] = value
                    new_moment[layer, b, part] = moment
                    new_average[layer, b, part] = average
    for ref in (new_mixer, new_moment, new_average):
        ref.flush()
    for group in range(groups):
        tail = held(0, group, slice(rows, rows + 16))
        grad_ref[0:2, group * width : (group + 1) * width] = tail[4:6]
        for layer in range(2):
            for j in range(2):
                b = group * joined + (j if joined == 2 else 0)
                per_row = vectors_ref.shape[1] // (2 * block)
                lane = (b % per_row) * 2 * block + (0 if joined == 2 else j * block)
                row = 9 + layer * 2 + b // per_row
                grad_ref[row : row + 1, lane : lane + width] = tail[2 * layer + j : 2 * layer + j + 1]
    for half in range(2):
        part = slice(rows, rows + 8 + 8 * slices + 8 * ((slices + 1) % 2))
        total = held(half, 0, part)
        for group in range(1, groups):
            total = total + held(half, group, part)
        for q in range(slices):
            lane = (half * slices + q) * width
            grad_ref[2:9, lane : lane + width] = total[8 + 8 * q : 15 + 8 * q]
    value, moment, average = update(
        vectors_ref[...], grad_ref[0:13, :] * scale, vec_moment_ref[...], vec_average_ref[...], 0.0
    )
    new_vectors[...] = value
    new_vec_moment[...] = moment
    new_vec_average[...] = average


def step_all(block, scale, place_ref, *refs):
    step_rest(block, scale, place_ref, *refs[10:18], *refs[26:])
    step_weights(scale, *refs[:10], *refs[18:26])


def step_weights(scale, own_ref, *refs):
    away_refs, weights, new_weights = refs[:3], refs[3:9], refs[9:17]
    for part in range(2):
        total = add_up(own_ref[part], *[ref[part] for ref in away_refs])
        count = weights[part].shape[0]
        for q in range(total.shape[0] // count):
            lanes = slice(q * 128, (q + 1) * 128)
            grad = total[q * count : (q + 1) * count] * scale
            values = update(
                weights[part][:, lanes], grad, weights[2 + part][:, lanes], weights[4 + part][:, lanes], WEIGHT_DECAY
            )
            for i, value in enumerate(values):
                new_weights[2 * i + part][:, lanes] = value
            new_weights[6 + part][:, lanes] = values[0].astype(BF16)
    for ref in new_weights:
        ref.flush()


def load_weights(near, place_ref, pieces, part, target, sem):
    copies = []
    part = () if part is None else (part,)
    every = (slice(None),) * (1 - len(part))
    if not near:
        copies = [(pieces[0].at[(slice(None), *part)], target)]
    else:
        me = place_ref[0]
        at = [(me >> 1) & 1, (me >> 2) & 1, me & 1, me >> 3]
        size = pieces[0].shape[3]
        for i, ref in enumerate(pieces):
            for j in range(2):
                x, y = (i >> 1 & 1, j) if i & 1 else (j, i >> 1 & 1)
                for k in range(2):
                    z = 2 * (i & 1) + k
                    row = (((at[3] ^ z) * 2 + (at[1] ^ y)) * 2 + (at[0] ^ (i >> 2))) * size
                    rows = pl.ds(pl.multiple_of(row, size), size)
                    copies.append((ref.at[(j, k, *part)], target.at[(at[2] ^ x, *every, rows)]))
    for source, place in copies:
        pltpu.make_async_copy(source, place, sem).start(priority=1)
    return pltpu.make_async_copy(target, target, sem)


def place_rows(ref, values, columns, orders):
    if not orders:
        ref[:, columns] = values
        return
    size = values.shape[0] // len(orders)
    for block, order in enumerate(orders):
        ref[pl.ds(pl.multiple_of(order * size, size), size), columns] = values[block * size : (block + 1) * size]


def mlp_kernel(
    groups, near, place_ref, got_ref, wide_t_ref, tokens_ref, cotangent_ref, vectors_ref, bias_ref, wide_ref, *refs
):
    count = 8 if near else 1
    pieces, refs = refs[:count], refs[count:]
    active, total_ref, middle_ref, send_ref, small_ref, *refs = refs
    grad_refs, refs = refs[:2], refs[2:]
    normed, normed_t, cotangent_t, normal, spread, weights, grad_hidden, sem = refs
    arrival = load_weights(near, place_ref, pieces, None, weights, sem)
    cotangent_ref.start()
    wide_ref.start()
    w_in, w_out = weights.at[:, 0], weights.at[:, 1]
    me = place_ref[0]
    orders = [((z ^ (me >> 3)) + 4 * (y ^ ((me >> 2) & 1)) + 8 * (c ^ ((me >> 1) & 1))) for z in range(4) for y in range(2) for c in range(2)]
    orders = orders if near else []
    tokens, width = tokens_ref.shape
    halves, _, columns = w_in.shape
    gain, shift, bias_out = vectors_ref[2:3, :], vectors_ref[3:4, :], vectors_ref[4:5, :]
    row_blocks = [slice(r, r + ROWS) for r in range(0, tokens, ROWS)]
    spectra = spans(gather_lanes(got_ref, groups))
    span = wide_t_ref.shape[0]
    bias_out_grad = jnp.zeros((1, width), F32)
    for rows in row_blocks:
        first = rows.start % span
        spatial = dot(wide_t_ref[first : first + ROWS, :], spectra[rows.start // span])
        middle = tokens_ref[rows, :].astype(F32) + spatial
        unit, inverse = normalize(middle)
        normal[rows, :] = unit
        spread[rows, :] = inverse
        scaled = (unit * gain + shift).astype(BF16)
        normed[rows, :] = scaled
        place_rows(normed_t, scaled.T, rows, orders)
        total_ref[rows, :] = middle + bias_out
        upstream = cotangent_ref[rows, :]
        place_rows(cotangent_t, upstream.T, rows, orders)
        bias_out_grad = bias_out_grad + jnp.sum(upstream.astype(F32), axis=0, keepdims=True)
    total_ref.flush()
    arrival.wait()
    gain_grad = jnp.zeros((1, width), F32)
    shift_grad = jnp.zeros((1, width), F32)
    chunks = [(h, c) for h in range(halves) for c in range(0, columns, CHUNK)]
    bias_grads = [jnp.zeros((1, CHUNK), F32) for _ in chunks]
    for rows in row_blocks:
        for i, (h, c) in enumerate(chunks):
            lanes, flat = slice(c, c + CHUNK), slice(h * columns + c, h * columns + c + CHUNK)
            hidden = dot(normed[rows, :], w_in[h, :, lanes]) + bias_ref[i : i + 1, :]
            value, slope = gelu_pair(hidden.astype(BF16))
            active[rows, flat] = value.astype(BF16)
            back = dot(cotangent_ref[rows, :], w_out[h, :, lanes]).astype(BF16) * slope
            grad_hidden[rows, flat] = back
            bias_grads[i] = bias_grads[i] + jnp.sum(back.astype(F32), axis=0, keepdims=True)
        back = dot_nt(grad_hidden[rows, :columns], w_in[0])
        for h in range(1, halves):
            back = back + dot_nt(grad_hidden[rows, h * columns : (h + 1) * columns], w_in[h])
        unit = normal[rows, :]
        gain_grad = gain_grad + jnp.sum(back * unit, axis=0, keepdims=True)
        shift_grad = shift_grad + jnp.sum(back, axis=0, keepdims=True)
        middle = cotangent_ref[rows, :].astype(F32) + norm_back(back, unit, spread[rows, :], gain)
        middle_ref[rows, :] = middle.astype(BF16)
    active.flush()
    middle_ref.flush()
    small_ref[0:3, :] = jnp.concatenate([gain_grad, shift_grad, bias_out_grad], axis=0)
    small_ref[3:7, :] = jnp.concatenate(bias_grads, axis=0)
    small_ref[7:8, :] = jnp.zeros((1, width), F32)
    scatter_lanes(send_ref, along_w(wide_ref, middle_ref, tokens), groups)
    send_ref.flush()
    for i, (h, c) in enumerate(chunks):
        flat = slice(h * columns + c, h * columns + c + CHUNK)
        grads = [
            dot(normed_t[...], grad_hidden[:, flat]).astype(BF16), dot(cotangent_t[...], active[:, flat]).astype(BF16)
        ]
        if not near:
            for ref, grad in zip(grad_refs, grads, strict=True):
                ref[h, :, c : c + CHUNK] = grad
            continue
        size = w_in.shape[1] // 16
        x = h ^ (me & 1)
        for core, ref in enumerate(grad_refs):
            for y in range(2):
                for z in range(4):
                    block = core * 8 + y * 4 + z
                    rows = slice(block * size, (block + 1) * size)
                    for q in range(CHUNK // 128):
                        lanes = slice(q * 128, (q + 1) * 128)
                        place = slice((c // 128 + q) * size, (c // 128 + q + 1) * size)
                        ref[0, x, y, z, place, :] = grads[0][rows, lanes]
                        ref[1, y, x, z, place, :] = grads[1][rows, lanes]


def output_kernel(near, place_ref, *refs):
    count = 8 if near else 1
    totals, actives, refs = refs[:OUT_BLOCKS], refs[OUT_BLOCKS : 2 * OUT_BLOCKS], refs[2 * OUT_BLOCKS :]
    ahead = (len(refs) - count - 3) // 2
    sources, pieces, outputs, sinks, (w_out, sem) = (
        refs[:ahead], refs[ahead : ahead + count], refs[ahead + count], refs[ahead + count + 1 : -2], refs[-2:]
    )
    load_weights(near, place_ref, pieces, 1, w_out, sem).wait()
    halves, _, columns = w_out.shape
    size = totals[0].shape[0]
    for i, (total, active) in enumerate(zip(totals, actives, strict=True)):
        value = total[...]
        for h in range(halves):
            value = value + dot_nt(active[:, h * columns : (h + 1) * columns], w_out[h])
        outputs[i * size : (i + 1) * size, :] = value.astype(BF16)
    outputs.flush()
    for source, sink in zip(sources, sinks, strict=True):
        sink[...] = source[...]


def leave_kernel(groups, got_ref, tokens_ref, middle_ref, vectors_ref, table_ref, out_ref):
    spectra = spans(gather_lanes(got_ref, groups))
    span = table_ref.shape[0]
    for start in range(0, tokens_ref.shape[0], ROWS):
        rows = slice(start, start + ROWS)
        first = start % span
        upstream = dot(table_ref[first : first + ROWS, :], spectra[start // span])
        unit, inverse = normalize(tokens_ref[rows, :].astype(F32))
        back = norm_back(upstream, unit, inverse, vectors_ref[0:1, :])
        out_ref[rows, :] = (middle_ref[rows, :].astype(F32) + back).astype(BF16)


def update(weight, gradient, moment, average, decay_rate):
    step_grad = gradient + decay_rate * weight
    new_moment = MOMENTUM * moment + step_grad
    new_weight = weight - LEARNING_RATE * (step_grad + MOMENTUM * new_moment)
    new_average = AVERAGE * average + (1.0 - AVERAGE) * new_weight
    return (new_weight, new_moment, new_average)


class Source:
    def __init__(self, ref, copy):
        self.ref, self.copy, self.shape, self.started = ref, copy, ref.shape, False

    def start(self):
        if not self.started:
            self.copy.start()
            self.started = True

    def __getitem__(self, index):
        if self.copy is not None:
            self.start()
            self.copy.wait()
            self.copy = None
        return self.ref[index]


class Sink:
    def __init__(self, ref, copy):
        self.ref, self.copy, self.shape, self.sent = ref, copy, ref.shape, False

    def __getitem__(self, index):
        return self.ref[index]

    def __setitem__(self, index, value):
        self.ref[index] = value

    def flush(self):
        if not self.sent:
            self.copy.start()
            self.sent = True


class Far:
    def __init__(self, *what):
        self.what = what


class Late(Far):
    pass


def call(body, outs, *args, scalars=(), raw=(), scratch=(), flops=0, carry=(), cost=None, vmem=20):
    near, far, there = [pl.BlockSpec(memory_space=m) for m in (pltpu.VMEM, pltpu.HBM, pl.ANY)]
    in_far, out_far = [isinstance(a, Far) for a in args], [isinstance(o, Far) for o in outs]
    in_late = [isinstance(a, Late) for a in args]
    index = [a.what[1:] if f else () for a, f in zip(args, in_far, strict=True)]
    args = [
        pltpu.with_memory_space_constraint(*((a.what[0], pltpu.HBM) if f else (a, pltpu.VMEM)))
        for a, f in zip(args, in_far, strict=True)
    ]
    raw = [pltpu.with_memory_space_constraint(a, pltpu.HBM) for a in raw]
    outs = [o.what if f else o for o, f in zip(outs, out_far, strict=True)]
    outs = [jax.ShapeDtypeStruct(s, d) for s, d in outs]
    n_scalar, n_in, n_raw, n_carry, n_out = len(scalars), len(args), len(raw), len(carry), len(outs)
    shapes = [np.empty(a.shape, np.bool_)[i].shape if i else a.shape for a, i in zip(args, index, strict=True)]
    shapes += [o.shape for o in outs]
    buffers = [
        pltpu.VMEM(shape, a.dtype) for shape, a, f in zip(shapes, args + outs, in_far + out_far, strict=True) if f
    ]

    def inner(*refs):
        refs = list(refs)

        def take(count):
            taken = refs[:count]
            del refs[:count]
            return taken

        scalar_refs, in_refs, raw_refs, _, out_refs, _ = [
            take(n) for n in (n_scalar, n_in, n_raw, n_carry, n_out, n_carry)
        ]
        space = take(len(buffers))
        sems = take(1)[0] if buffers else None
        sources, sinks, used = [], [], 0
        for ref, away, part, late in zip(in_refs, in_far, index, in_late, strict=True):
            if away:
                copy = pltpu.make_async_copy(ref.at[part] if part else ref, space[used], sems.at[used])
                ref = Source(space[used], copy)
                if not late:
                    ref.start()
                used += 1
            sources.append(ref)
        for ref, away in zip(out_refs, out_far, strict=True):
            if away:
                ref = Sink(space[used], pltpu.make_async_copy(space[used], ref, sems.at[used]))
                used += 1
            sinks.append(ref)
        body(*scalar_refs, *sources, *raw_refs, *sinks, *refs)
        for source in sources:
            if isinstance(source, Source) and source.copy is not None:
                source.copy.wait()
        sinks = [sink for sink in sinks if isinstance(sink, Sink)]
        for sink in sinks:
            sink.flush()
        for sink in sinks:
            sink.copy.wait()

    every = list(args) + list(raw)
    size = sum(math.prod(a.shape) * a.dtype.itemsize for a in every + outs) if cost is None else cost
    sems = [pltpu.SemaphoreType.DMA((len(buffers),))] if buffers else []
    return pl.pallas_call(
        inner,
        out_shape=[(pltpu.HBM if f else pltpu.VMEM)(o.shape, o.dtype) for o, f in zip(outs, out_far, strict=True)]
        + [jax.ShapeDtypeStruct(a.shape, a.dtype) for a in carry],
        in_specs=[pl.BlockSpec(memory_space=pltpu.SMEM)] * n_scalar
        + [far if f else near for f in in_far]
        + [far] * n_raw
        + [there] * n_carry,
        out_specs=[far if f else near for f in out_far] + [there] * n_carry,
        scratch_shapes=buffers + sems + list(scratch),
        input_output_aliases={n_scalar + n_in + n_raw + i: n_out + i for i in range(n_carry)},
        compiler_params=pltpu.CompilerParams(vmem_limit_bytes=vmem << 20),
        cost_estimate=pl.CostEstimate(flops=flops, bytes_accessed=size, transcendentals=0),
    )(*scalars, *args, *raw, *carry)


def on_device(
    tokens, cotangent, w_in, w_out, mixer_weights, vectors, w_in_moment, w_out_moment, mixer_moment, vectors_moment,
    w_in_average, w_out_average, mixer_average, vectors_average,
):
    sp_count, tp_count = lax.axis_size("sp"), lax.axis_size("tp")
    devices = sp_count * tp_count
    grid_rows, grid, width = tokens.shape
    local = grid_rows * grid
    items = grid_rows * devices // grid
    block_count, block = mixer_weights.shape[1], mixer_weights.shape[3]
    hidden = w_in.shape[1] * tp_count
    model = w_in.shape[0] * sp_count
    lanes = 2 * block if devices * 2 * block <= MODES * width else block
    groups = width // lanes
    per_group = devices // groups
    modes = MODES // per_group
    joined = lanes // block
    scale = 1.0 / math.sqrt(local * devices)
    wide_f, wide_i, high, ones = expanded_tables(grid, items)
    me = lax.axis_index("sp") * tp_count + lax.axis_index("tp")
    group = me // per_group
    exchange = functools.partial(lax.all_to_all, axis_name=AXES, split_axis=0, concat_axis=0, tiled=True)
    chunk = (devices, modes * grid_rows * 2, lanes)
    rows_all = tokens.reshape(local, width)
    upstream_all = cotangent.reshape(local, width)
    shard_rows, shard_columns = w_in.shape
    shard_size = shard_rows * shard_columns // 128
    near = devices == 32 and per_group == 8 and shard_rows % 16 == 0

    def permute(values, mask):
        return lax.ppermute(values, AXES, [(d, d ^ mask) for d in range(devices)])

    pair = jnp.stack([w_in.astype(BF16), w_out.astype(BF16)])
    if near:
        line = [pair] + [permute(pair, 8 * z) for z in (1, 2, 3)]
        carried = [jnp.stack([v, permute(v, m)]) for v, m in ((jnp.stack(line[:2]), 1), (jnp.stack(line[2:]), 4))]
    else:
        weights = lax.all_gather(pair, "sp", axis=1, tiled=True)
        pieces, carried = [lax.all_gather(weights, "tp")], []

    own_mixer = lax.dynamic_slice_in_dim(mixer_weights, group * joined, joined, 1).astype(BF16)
    eye = jnp.eye(joined, dtype=BF16)
    real = jnp.einsum("lbio,bc->lbico", own_mixer[:, :, 0], eye).reshape(2, lanes, lanes)
    imag = jnp.einsum("lbio,bc->lbico", own_mixer[:, :, 1], eye).reshape(2, lanes, lanes)
    mats = jnp.concatenate(
        [jnp.concatenate([real, imag], axis=2), jnp.concatenate([-imag, real], axis=2)], axis=1
    )
    own_bias = lax.dynamic_slice_in_dim(
        vectors[9:13].reshape(2, block_count, 2, block), group * joined, joined, 1
    )
    own_bias = jnp.swapaxes(own_bias, 1, 2).reshape(2, 2 * lanes)
    own_gain = lax.dynamic_slice_in_dim(vectors[0:1], group * lanes, lanes, 1)
    own_shift = lax.dynamic_slice_in_dim(vectors[1:2], group * lanes, lanes, 1)
    ones = jnp.asarray(np.swapaxes(ones.reshape(per_group, modes, -1), 1, 2))
    own_ones = lax.dynamic_index_in_dim(ones, me % per_group, 0, keepdims=False)

    wide_f, wide_f_t = jnp.asarray(wide_f), jnp.asarray(wide_f.T)
    wide_i, wide_i_t = jnp.asarray(wide_i), jnp.asarray(wide_i.T)
    high, high_t = jnp.asarray(high), jnp.asarray(high.T)
    wide_flops = 2 * MODES * 2 * local * width * SPAN
    (sent,) = call(
        functools.partial(enter_kernel, groups), [(chunk, BF16)], Far(rows_all), Far(wide_f), flops=wide_flops
    )
    got = exchange(sent)
    half_rows = items * MODES
    sent, hat, modal, inner, active, *carried = call(
        functools.partial(mix_kernel, modes),
        [
            (chunk, BF16),
            Far((2 * half_rows, modes * lanes), F32),
            Far((modes * half_rows, 2 * lanes), BF16),
            Far((modes * half_rows, 2 * lanes), F32),
            Far((modes * half_rows, 2 * lanes), BF16),
        ],
        got, high, high_t, mats, own_bias, own_gain, own_shift, own_ones,
        carry=carried,
    )
    if near:
        pieces = carried + [permute(carried[0], 4), permute(carried[1], 1)]
        pieces += [permute(p, 2) for p in pieces]
    got = exchange(sent)
    steps = hidden // CHUNK
    grads = [((2, 2, 2, 4, shard_size, 128), BF16)] * 2 if near else [((tp_count, model, shard_columns), BF16)] * 2
    gelus, total, middle, sent, mlp_small, *grads = call(
        functools.partial(mlp_kernel, groups, near),
        [
            Far((local, hidden), BF16), Far((local, width), F32), Far((local, width), BF16), Far(chunk, BF16),
            ((8, width), F32),
        ]
        + grads,
        Far(got), Far(wide_i_t), Far(rows_all), Late(upstream_all), vectors, vectors[5:9].reshape(steps, CHUNK), Late(wide_i),
        scalars=[me[None]], raw=pieces,
        scratch=[
            pltpu.VMEM((local, width), BF16),
            pltpu.VMEM((width, local), BF16),
            pltpu.VMEM((width, local), BF16),
            pltpu.VMEM((local, width), F32),
            pltpu.VMEM((local, 1), F32),
            pltpu.VMEM((tp_count, 2, model, shard_columns), BF16),
            pltpu.VMEM((local, hidden), BF16),
            pltpu.SemaphoreType.DMA,
        ],
        flops=12 * local * width * hidden + 2 * wide_flops, vmem=44,
    )

    carried = []
    if near:
        shard = (4, shard_size, 128)
        kept, one = grads[0], permute(grads[1], 2)
        sent_in, sent_out = call(
            first_kernel, [((2,) + shard, BF16)] * 2, kept, Far(one, slice(None), 1), cost=0
        )
        carried = [permute(sent_in, 1), permute(sent_out, 4)]

    step = local // OUT_BLOCKS
    parts = [slice(r, r + step) for r in range(0, local, step)]
    kept_forward = [high, high_t, mats, hat, modal, inner, active]
    ahead = kept_forward[:3] if near else []
    output, *ahead = call(
        functools.partial(output_kernel, near),
        [Far((local, width), BF16)] + [(a.shape, a.dtype) for a in ahead],
        *[Far(total, rows) for rows in parts], *[Far(gelus, rows) for rows in parts], *[Far(a) for a in ahead],
        scalars=[me[None]], raw=pieces, cost=COST, vmem=24,
        scratch=[
            pltpu.VMEM((tp_count, model, shard_columns), BF16),
            pltpu.SemaphoreType.DMA,
        ],
    )

    kept_forward = ahead + [Far(a) for a in kept_forward[len(ahead) :]]
    got = exchange(sent)
    small_rows = -(-(2 * block + 8 + 8 * (groups // 2)) // 16) * 16
    place = ((me >> 1) & 1 if near else jnp.int32(0))[None]
    sent, small, given, output = call(
        functools.partial(unmix_kernel, modes, block),
        [Far(chunk, BF16), ((small_rows, lanes), BF16), ((small_rows, lanes), BF16)],
        got, *kept_forward[:3], own_ones, *kept_forward[3:], mlp_small,
        scalars=[place], cost=COST, vmem=20 if near else 48, carry=[output],
    )
    if near:
        both = slice(None)
        small, over_y, over_x = call(
            second_kernel, [((small_rows, lanes), BF16)] + [(shard, BF16)] * 2,
            kept, *[Far(a, 1) for a in carried], small, permute(given, 2), Far(one, both, 0, 1), cost=0,
        )
        line, own, *away = call(
            third_kernel,
            [((4, small_rows, lanes), BF16), ((2, shard_size, 128), F32)] + [((2, shard_size, 128), BF16)] * 3,
            kept, *[Far(a, 0) for a in carried], permute(over_y, 4), permute(over_x, 1),
            small, *[permute(small, 8 * z) for z in (1, 2, 3)], Far(one, both, 0, 0),
            scalars=[me[None]], cost=0,
        )
        away = [permute(a, 8 * (z + 1)) for z, a in enumerate(away)]
    got = exchange(sent)
    (grad_tokens,) = call(
        functools.partial(leave_kernel, groups),
        [Far((local, width), BF16)],
        got, Far(rows_all), Far(middle), vectors, Far(wide_f_t), cost=COST,
    )

    if near:
        line, *away, grad_tokens = call(
            plane_kernel, [(line.shape, BF16)], line, *[permute(line, m) for m in (1, 4, 5)], cost=0, carry=[*away, grad_tokens]
        )
        other = permute(line, 2)

    state = [mixer_weights, mixer_moment, mixer_average, vectors, vectors_moment, vectors_average]
    new_state = [Far(a.shape, F32) for a in state]
    if near:
        weights = [w_in, w_out, w_in_moment, w_out_moment, w_in_average, w_out_average]
        *stepped, grad_tokens = call(
            functools.partial(step_all, block, scale),
            [Far(w_in.shape, F32)] * 6 + [Far(w_in.shape, BF16)] * 2 + new_state,
            own, *away, *weights, line, other, *state,
            scalars=[place], scratch=[pltpu.VMEM((16, width), F32)], carry=[grad_tokens], cost=0,
        )
        new_in, new_out = stepped[0:8:2], stepped[1:8:2]
        stepped = stepped[8:]
    else:
        grads = jnp.stack(grads).astype(F32)
        grads = lax.psum_scatter(grads, "tp", scatter_dimension=1, tiled=True)
        grads = lax.psum_scatter(grads, "sp", scatter_dimension=2, tiled=True)
        new_in = update(w_in, grads[0, 0] * scale, w_in_moment, w_in_average, WEIGHT_DECAY)
        new_out = update(w_out, grads[1, 0] * scale, w_out_moment, w_out_average, WEIGHT_DECAY)
        new_in, new_out = new_in + (new_in[0].astype(BF16),), new_out + (new_out[0].astype(BF16),)
        onehot = (jnp.arange(groups, dtype=jnp.int32) == group).astype(F32)[:, None, None]
        line, other = lax.psum((onehot * small.astype(F32), onehot * given.astype(F32)), AXES)
        stepped = call(
            functools.partial(step_rest, block, scale), new_state, line, other, *state,
            scalars=[place], scratch=[pltpu.VMEM((16, width), F32)],
        )
    new_mix, new_vec = stepped[0:3], stepped[3:6]
    shape = tokens.shape
    return (
        output.reshape(shape), grad_tokens.reshape(shape),
        new_in[0], new_out[0], new_mix[0], new_vec[0],
        new_in[1], new_out[1], new_mix[1], new_vec[1],
        new_in[2], new_out[2], new_mix[2], new_vec[2],
        new_in[3], new_out[3],
    )


def solution(mesh):
    rows, split, whole = P(AXES, None, None), P("sp", "tp"), P()
    state = (split, split, whole, whole)
    return jax.shard_map(
        on_device,
        mesh=mesh,
        in_specs=(rows, rows) + state * 3,
        out_specs=(rows, rows) + state * 3 + (split, split),
        check_vma=False,
    )
```

```python
import functools
import math

import jax
import jax.numpy as jnp
import ml_dtypes
import numpy as np
from jax import lax
from jax.experimental import pallas as pl
from jax.experimental.pallas import tpu as pltpu
from jax.sharding import PartitionSpec as P

MODES = 32
EPSILON = 1e-05
LEARNING_RATE = 0.05
MOMENTUM = 0.9
WEIGHT_DECAY = 0.0001
AVERAGE = 0.75
GELU_SCALE = math.sqrt(2.0 / math.pi)
GELU_CUBE = 0.044715
CHUNK = 512
ROWS = 256
SPAN = 4
BF16 = jnp.bfloat16
F32 = jnp.float32
AXES = ("sp", "tp")
COST = 60 << 20
OUT_BLOCKS = 4


def dft_tables(grid):
    positions = np.arange(grid)
    wave = np.arange(MODES)
    root = np.float32(1.0 / math.sqrt(grid))
    step = np.float32(2.0 * math.pi / grid)
    phase_w = (positions[:, None] * wave[None, :] % grid).astype(np.float32) * step
    factor = np.where(wave == 0, 1.0, 2.0).astype(np.float32)
    cos_w, sin_w = np.cos(phase_w) * root, np.sin(phase_w) * root
    forward_w = np.stack([cos_w, -sin_w], axis=1)
    inverse_w = np.stack([cos_w * factor, -sin_w * factor], axis=1)
    frequency = np.where(wave < MODES // 2, wave, wave - MODES)
    phase_h = (frequency[:, None] * positions[None, :] % grid).astype(np.float32) * step
    cos_h, sin_h = np.cos(phase_h) * root, np.sin(phase_h) * root
    forward_h = np.stack([np.stack([cos_h, -sin_h], -1), np.stack([sin_h, cos_h], -1)], -2)
    return [t.astype(ml_dtypes.bfloat16) for t in (forward_w, inverse_w, forward_h)]


def expanded_tables(grid, items):
    forward_w, inverse_w, forward_h = [t.astype(np.float32) for t in dft_tables(grid)]
    eye_r = np.eye(SPAN, dtype=np.float32)
    wide_f = np.einsum("wek,rs->kresw", forward_w, eye_r).reshape(-1, SPAN * grid)
    wide_i = np.einsum("wek,rs->kresw", inverse_w, eye_r).reshape(-1, SPAN * grid)
    eye_i = np.eye(items, dtype=np.float32)
    high = np.einsum("mhef,ij->fimhje", forward_h, eye_i).reshape(2 * items * MODES, -1)
    ones = np.einsum("mhef,ek->kfm", forward_h.astype(np.float64), forward_w.astype(np.float64).sum(0))
    ones = np.repeat(ones[:, :, None], items, axis=2).reshape(MODES, -1).astype(np.float32)
    cast = [t.astype(ml_dtypes.bfloat16) for t in (wide_f, wide_i, high)]
    return cast[0], cast[1], cast[2], ones


def dot(left, right):
    return jnp.dot(left, right, preferred_element_type=F32)


def dot_nt(left, right):
    return lax.dot_general(left, right, (((1,), (1,)), ((), ())), preferred_element_type=F32)


def dot_tn(left, right):
    return lax.dot_general(left, right, (((0,), (0,)), ((), ())), preferred_element_type=F32)


def normalize(values):
    center = values - jnp.mean(values, axis=-1, keepdims=True)
    inverse = lax.rsqrt(jnp.mean(center * center, axis=-1, keepdims=True) + EPSILON)
    return center * inverse, inverse


def norm_back(upstream, normal, inverse, gain):
    scaled = upstream * gain
    centered = scaled - jnp.mean(scaled, axis=-1, keepdims=True)
    centered = centered - normal * jnp.mean(scaled * normal, axis=-1, keepdims=True)
    return centered * inverse


def gelu_pair(values):
    square = values * values
    bent = jnp.tanh(values * (GELU_SCALE + (GELU_SCALE * GELU_CUBE) * square))
    half = 0.5 + 0.5 * bent
    slope = half + (values * half) * (1.0 - bent) * (GELU_SCALE + (3.0 * GELU_SCALE * GELU_CUBE) * square)
    return values * half, slope


def gelu_value(values):
    square = values * values
    bent = jnp.tanh(values * (GELU_SCALE + (GELU_SCALE * GELU_CUBE) * square))
    return values * (0.5 + 0.5 * bent)


def along_w(table_ref, values, rows):
    table = table_ref[...]
    span = table.shape[1]
    parts = [dot(table, values[r : r + span]).reshape(MODES, -1, values.shape[1]) for r in range(0, rows, span)]
    return jnp.concatenate(parts, axis=1).reshape(-1, values.shape[1]).astype(BF16)


def spans(spectrum):
    whole = spectrum.astype(F32).reshape(MODES, -1, spectrum.shape[1])
    size = 2 * SPAN
    return [
        whole[:, r : r + size].reshape(MODES * size, -1).astype(BF16) for r in range(0, whole.shape[1], size)
    ]


def gather_lanes(ref, groups):
    count = ref.shape[0] // groups
    width = ref.shape[2]
    parts = [ref[g * count : (g + 1) * count].reshape(count * ref.shape[1], width) for g in range(groups)]
    return parts[0] if groups == 1 else jnp.concatenate(parts, axis=1)


def scatter_lanes(ref, values, groups):
    count = ref.shape[0] // groups
    width = ref.shape[2]
    for g in range(groups):
        piece = values[:, g * width : (g + 1) * width]
        ref[g * count : (g + 1) * count] = piece.reshape(count, ref.shape[1], width)


def gather_modes(ref, modes):
    rows = ref.shape[1] // modes
    parts = [
        ref[:, k * rows : (k + 1) * rows, :].reshape(ref.shape[0] * rows, ref.shape[2]) for k in range(modes)
    ]
    return parts[0] if modes == 1 else jnp.concatenate(parts, axis=1)


def scatter_modes(ref, values, modes):
    rows = ref.shape[1] // modes
    width = ref.shape[2]
    for k in range(modes):
        piece = values[:, k * width : (k + 1) * width]
        ref[:, k * rows : (k + 1) * rows, :] = piece.reshape(ref.shape[0], rows, width)


def to_mix_rows(values, modes, width):
    half = values.shape[0] // 2
    parts = []
    for k in range(modes):
        piece = values[:, k * width : (k + 1) * width]
        parts.append(jnp.concatenate([piece[:half], piece[half:]], axis=1))
    return parts[0] if modes == 1 else jnp.concatenate(parts, axis=0)


def from_mix_rows(values, modes, width):
    half = values.shape[0] // modes
    parts = []
    for k in range(modes):
        piece = values[k * half : (k + 1) * half]
        parts.append(jnp.concatenate([piece[:, :width], piece[:, width:]], axis=0))
    return parts[0] if modes == 1 else jnp.concatenate(parts, axis=1)


def enter_kernel(groups, place_ref, tokens_ref, table_ref, *refs):
    if len(refs) > 1:
        ones_ref, mixer_ref, *refs, held, sems = refs
        joined = held.shape[1]
        blocks = pl.ds(place_ref[1] * joined, joined)
        copies = [
            pltpu.make_async_copy(mixer_ref.at[:, blocks], held, sems.at[0]),
            pltpu.make_async_copy(ones_ref.at[place_ref[0]], refs[1], sems.at[1]),
        ]
        for copy in copies:
            copy.start(priority=1)
    normal, _ = normalize(tokens_ref[...].astype(F32))
    scatter_lanes(refs[0], along_w(table_ref, normal.astype(BF16), normal.shape[0]), groups)
    if len(refs) > 1:
        for copy in copies:
            copy.wait()
        refs[2][...] = held[...].astype(BF16)


def mix_kernel(
    modes, got_ref, high_ref, back_ref, mats_ref, bias_ref, gain_ref, shift_ref, ones_ref,
    send_ref, hat_ref, modal_ref, inner_ref, active_ref,
):
    width = got_ref.shape[2]
    hat = dot(high_ref[...], gather_modes(got_ref, modes))
    hat_ref[...] = hat
    hat_ref.flush()
    pieces = []
    for k in range(modes):
        piece = hat[:, k * width : (k + 1) * width] * gain_ref[...]
        pieces.append(piece + ones_ref[:, k : k + 1] * shift_ref[...])
    modal = pieces[0] if modes == 1 else jnp.concatenate(pieces, axis=1)
    modal = to_mix_rows(modal.astype(BF16), modes, width)
    modal_ref[...] = modal
    modal_ref.flush()
    inner = dot(modal, mats_ref[0]) + bias_ref[0:1, :]
    inner_ref[...] = inner
    inner_ref.flush()
    active = gelu_value(inner).astype(BF16)
    active_ref[...] = active
    active_ref.flush()
    outer = (dot(active, mats_ref[1]) + bias_ref[1:2, :]).astype(BF16)
    gridded = dot(back_ref[...], from_mix_rows(outer, modes, width)).astype(BF16)
    scatter_modes(send_ref, gridded, modes)


def fold(grad, width, block):
    real = grad[:width, :width] + grad[width:, width:]
    imag = grad[:width, width:] - grad[width:, :width]
    out = []
    for part in (real, imag):
        if width == block:
            out.append(part)
        else:
            lane = lax.broadcasted_iota(jnp.int32, (block, width), 1)
            out.append(jnp.where(lane < block, part[:block], part[block:]))
    return jnp.concatenate(out, axis=0)


def by_block(sums, width, block):
    real, imag = sums[:, :width], sums[:, width:]
    if width == block:
        return [real, imag]
    lane = lax.broadcasted_iota(jnp.int32, real.shape, 1)
    turned_real, turned_imag = pltpu.roll(real, block, 1), pltpu.roll(imag, block, 1)
    return [jnp.where(lane < block, real, turned_imag), jnp.where(lane < block, turned_real, imag)]


def unmix_kernel(
    modes, block, place_ref, got_ref, high_ref, back_ref, mats_ref, ones_ref, hat_ref, modal_ref, inner_ref, active_ref,
    mlp_ref, send_ref, keep_ref, give_ref,
):
    width = got_ref.shape[2]
    grad_outer = dot(high_ref[...], gather_modes(got_ref, modes)).astype(BF16)
    grad_outer = to_mix_rows(grad_outer, modes, width)
    _, slope = gelu_pair(inner_ref[...])
    grad_inner = (dot_nt(grad_outer, mats_ref[1]) * slope).astype(BF16)
    grad_modal = dot_nt(grad_inner, mats_ref[0]).astype(BF16)
    grad_modal = from_mix_rows(grad_modal, modes, width)
    spectrum = dot(back_ref[...], grad_modal).astype(BF16)
    scatter_modes(send_ref, spectrum, modes)
    send_ref.flush()
    rows = 2 * block
    grads = [fold(dot_tn(modal_ref[...], grad_inner), width, block)]
    grads.append(fold(dot_tn(active_ref[...], grad_outer), width, block))
    bias_one = by_block(jnp.sum(grad_inner.astype(F32), axis=0, keepdims=True), width, block)
    bias_two = by_block(jnp.sum(grad_outer.astype(F32), axis=0, keepdims=True), width, block)
    gain = jnp.zeros((1, width), F32)
    shift = jnp.zeros((1, width), F32)
    for k in range(modes):
        lanes = slice(k * width, (k + 1) * width)
        upstream = grad_modal[:, lanes].astype(F32)
        gain = gain + jnp.sum(upstream * hat_ref[:, lanes], axis=0, keepdims=True)
        shift = shift + jnp.sum(upstream * ones_ref[:, k : k + 1], axis=0, keepdims=True)
    tail = jnp.concatenate(bias_one + bias_two + [gain, shift, jnp.zeros((2, width), F32)], axis=0)
    mlp = [mlp_ref[:, q : q + width] for q in range(0, mlp_ref.shape[1], width)]
    count = len(mlp) // 2
    rows = keep_ref.shape[0] - 2 * block - 8 - 8 * count
    rest = [jnp.zeros((rows, width), F32)] if rows else []
    for half, parts in enumerate(([grads[0], tail] + mlp[:count], [grads[1], jnp.zeros_like(tail)] + mlp[count:])):
        message = jnp.concatenate(parts + rest, axis=0).astype(BF16)
        for ref, core in ((keep_ref, half), (give_ref, 1 - half)):

            @pl.when(place_ref[0] == core)
            def _(ref=ref, message=message):
                ref[...] = message


def add_up(*values):
    total = values[0].astype(F32)
    for value in values[1:]:
        total = total + value.astype(F32)
    return total


def first_kernel(kept_ref, one_ref, in_ref, out_ref):
    for part, ref in enumerate((in_ref, out_ref)):
        ref[...] = add_up(kept_ref[part, 1], one_ref[part]).astype(BF16)


def second_kernel(kept_ref, in_ref, out_ref, mine_ref, core_ref, one_ref, small_ref, y_ref, x_ref):
    small_ref[...] = add_up(mine_ref[...], core_ref[...]).astype(BF16)
    for part, source, ref in ((0, in_ref, y_ref), (1, out_ref, x_ref)):
        ref[...] = add_up(kept_ref[part, 0, 1], one_ref[part], source[...]).astype(BF16)


def third_kernel(place_ref, kept_ref, in_ref, out_ref, y_ref, x_ref, *refs):
    small_refs, (one_ref, line_ref, own_ref), away_refs = refs[:4], refs[4:7], refs[7:]
    for z, ref in enumerate(small_refs):
        line_ref[(place_ref[0] >> 3) ^ z] = ref[...]
    for part, source, last in ((0, in_ref, y_ref), (1, out_ref, x_ref)):
        for z in range(4):
            total = add_up(kept_ref[part, 0, 0, z], one_ref[part, z], source[z], last[z])
            if z == 0:
                own_ref[part] = total
            else:
                away_refs[z - 1][part] = total.astype(BF16)


def plane_kernel(mine_ref, x_ref, y_ref, other_ref, total_ref):
    total_ref[...] = (add_up(mine_ref[...], x_ref[...]) + add_up(y_ref[...], other_ref[...])).astype(BF16)


def step_rest(
    block, scale, place_ref, own_ref, other_ref, mixer_ref, moment_ref, average_ref, vectors_ref, vec_moment_ref,
    vec_average_ref, new_mixer, new_moment, new_average, new_vectors, new_vec_moment, new_vec_average, grad_ref,
):
    groups, _, width = own_ref.shape
    joined = width // block
    rows = 2 * block
    slices = groups // 2
    core = place_ref[0]

    def held(half, group, part):
        mine, theirs = own_ref[group, part, :], other_ref[group, part, :]
        return jnp.where(core == half, mine, theirs).astype(F32)

    for group in range(groups):
        for layer in range(2):
            grad = held(layer, group, slice(0, rows)) * scale
            for part in range(2):
                for j in range(joined):
                    b = group * joined + j
                    piece = grad[part * block : (part + 1) * block, j * block : (j + 1) * block]
                    value, moment, average = update(
                        mixer_ref[layer, b, part], piece, moment_ref[layer, b, part], average_ref[layer, b, part],
                        WEIGHT_DECAY,
                    )
                    new_mixer[layer, b, part] = value
                    new_moment[layer, b, part] = moment
                    new_average[layer, b, part] = average
    for ref in (new_mixer, new_moment, new_average):
        ref.flush()
    for group in range(groups):
        tail = held(0, group, slice(rows, rows + 16))
        grad_ref[0:2, group * width : (group + 1) * width] = tail[4:6]
        for layer in range(2):
            for j in range(2):
                b = group * joined + (j if joined == 2 else 0)
                per_row = vectors_ref.shape[1] // (2 * block)
                lane = (b % per_row) * 2 * block + (0 if joined == 2 else j * block)
                row = 9 + layer * 2 + b // per_row
                grad_ref[row : row + 1, lane : lane + width] = tail[2 * layer + j : 2 * layer + j + 1]
    for half in range(2):
        part = slice(rows, rows + 8 + 8 * slices + 8 * ((slices + 1) % 2))
        total = held(half, 0, part)
        for group in range(1, groups):
            total = total + held(half, group, part)
        for q in range(slices):
            lane = (half * slices + q) * width
            grad_ref[2:9, lane : lane + width] = total[8 + 8 * q : 15 + 8 * q]
    value, moment, average = update(
        vectors_ref[...], grad_ref[0:13, :] * scale, vec_moment_ref[...], vec_average_ref[...], 0.0
    )
    new_vectors[...] = value
    new_vec_moment[...] = moment
    new_vec_average[...] = average


def step_all(block, scale, place_ref, *refs):
    step_rest(block, scale, place_ref, *refs[10:18], *refs[26:])
    step_weights(scale, *refs[:10], *refs[18:26])


def step_weights(scale, own_ref, *refs):
    away_refs, weights, new_weights = refs[:3], refs[3:9], refs[9:17]
    for part in range(2):
        total = add_up(own_ref[part], *[ref[part] for ref in away_refs])
        count = weights[part].shape[0]
        for q in range(total.shape[0] // count):
            lanes = slice(q * 128, (q + 1) * 128)
            grad = total[q * count : (q + 1) * count] * scale
            values = update(
                weights[part][:, lanes], grad, weights[2 + part][:, lanes], weights[4 + part][:, lanes], WEIGHT_DECAY
            )
            for i, value in enumerate(values):
                new_weights[2 * i + part][:, lanes] = value
            new_weights[6 + part][:, lanes] = values[0].astype(BF16)
    for ref in new_weights:
        ref.flush()


def load_weights(near, place_ref, pieces, part, target, sem):
    copies = []
    part = () if part is None else (part,)
    every = (slice(None),) * (1 - len(part))
    if not near:
        copies = [(pieces[0].at[(slice(None), *part)], target)]
    else:
        me = place_ref[0]
        at = [(me >> 1) & 1, (me >> 2) & 1, me & 1, me >> 3]
        size = pieces[0].shape[3]
        for i, ref in enumerate(pieces):
            for j in range(2):
                x, y = (i >> 1 & 1, j) if i & 1 else (j, i >> 1 & 1)
                for k in range(2):
                    z = 2 * (i & 1) + k
                    row = (((at[3] ^ z) * 2 + (at[1] ^ y)) * 2 + (at[0] ^ (i >> 2))) * size
                    rows = pl.ds(pl.multiple_of(row, size), size)
                    copies.append((ref.at[(j, k, *part)], target.at[(at[2] ^ x, *every, rows)]))
    for source, place in copies:
        pltpu.make_async_copy(source, place, sem).start(priority=1)
    return pltpu.make_async_copy(target, target, sem)


def place_rows(ref, values, columns, orders):
    if not orders:
        ref[:, columns] = values
        return
    size = values.shape[0] // len(orders)
    for block, order in enumerate(orders):
        ref[pl.ds(pl.multiple_of(order * size, size), size), columns] = values[block * size : (block + 1) * size]


def mlp_kernel(
    groups, near, place_ref, got_ref, wide_t_ref, tokens_ref, cotangent_ref, vectors_ref, bias_ref, wide_ref, *refs
):
    count = 8 if near else 1
    pieces, refs = refs[:count], refs[count:]
    active, total_ref, middle_ref, send_ref, small_ref, *refs = refs
    grad_refs, refs = refs[:2], refs[2:]
    normed, normed_t, cotangent_t, normal, spread, weights, grad_hidden, sem = refs
    arrival = load_weights(near, place_ref, pieces, None, weights, sem)
    cotangent_ref.start()
    wide_ref.start()
    w_in, w_out = weights.at[:, 0], weights.at[:, 1]
    me = place_ref[0]
    orders = [((z ^ (me >> 3)) + 4 * (y ^ ((me >> 2) & 1)) + 8 * (c ^ ((me >> 1) & 1))) for z in range(4) for y in range(2) for c in range(2)]
    orders = orders if near else []
    tokens, width = tokens_ref.shape
    halves, _, columns = w_in.shape
    gain, shift, bias_out = vectors_ref[2:3, :], vectors_ref[3:4, :], vectors_ref[4:5, :]
    row_blocks = [slice(r, r + ROWS) for r in range(0, tokens, ROWS)]
    spectra = spans(gather_lanes(got_ref, groups))
    span = wide_t_ref.shape[0]
    bias_out_grad = jnp.zeros((1, width), F32)
    for rows in row_blocks:
        first = rows.start % span
        spatial = dot(wide_t_ref[first : first + ROWS, :], spectra[rows.start // span])
        middle = tokens_ref[rows, :].astype(F32) + spatial
        unit, inverse = normalize(middle)
        normal[rows, :] = unit
        spread[rows, :] = inverse
        scaled = (unit * gain + shift).astype(BF16)
        normed[rows, :] = scaled
        place_rows(normed_t, scaled.T, rows, orders)
        total_ref[rows, :] = middle + bias_out
        upstream = cotangent_ref[rows, :]
        place_rows(cotangent_t, upstream.T, rows, orders)
        bias_out_grad = bias_out_grad + jnp.sum(upstream.astype(F32), axis=0, keepdims=True)
    total_ref.flush()
    arrival.wait()
    gain_grad = jnp.zeros((1, width), F32)
    shift_grad = jnp.zeros((1, width), F32)
    chunks = [(h, c) for h in range(halves) for c in range(0, columns, CHUNK)]
    bias_grads = [jnp.zeros((1, CHUNK), F32) for _ in chunks]
    for rows in row_blocks:
        for i, (h, c) in enumerate(chunks):
            lanes, flat = slice(c, c + CHUNK), slice(h * columns + c, h * columns + c + CHUNK)
            hidden = dot(normed[rows, :], w_in[h, :, lanes]) + bias_ref[i : i + 1, :]
            value, slope = gelu_pair(hidden.astype(BF16))
            active[rows, flat] = value.astype(BF16)
            back = dot(cotangent_ref[rows, :], w_out[h, :, lanes]).astype(BF16) * slope
            grad_hidden[rows, flat] = back
            bias_grads[i] = bias_grads[i] + jnp.sum(back.astype(F32), axis=0, keepdims=True)
        back = dot_nt(grad_hidden[rows, :columns], w_in[0])
        for h in range(1, halves):
            back = back + dot_nt(grad_hidden[rows, h * columns : (h + 1) * columns], w_in[h])
        unit = normal[rows, :]
        gain_grad = gain_grad + jnp.sum(back * unit, axis=0, keepdims=True)
        shift_grad = shift_grad + jnp.sum(back, axis=0, keepdims=True)
        middle = cotangent_ref[rows, :].astype(F32) + norm_back(back, unit, spread[rows, :], gain)
        middle_ref[rows, :] = middle.astype(BF16)
    active.flush()
    middle_ref.flush()
    small_ref[0:3, :] = jnp.concatenate([gain_grad, shift_grad, bias_out_grad], axis=0)
    small_ref[3:7, :] = jnp.concatenate(bias_grads, axis=0)
    small_ref[7:8, :] = jnp.zeros((1, width), F32)
    scatter_lanes(send_ref, along_w(wide_ref, middle_ref, tokens), groups)
    send_ref.flush()
    for i, (h, c) in enumerate(chunks):
        flat = slice(h * columns + c, h * columns + c + CHUNK)
        grads = [
            dot(normed_t[...], grad_hidden[:, flat]).astype(BF16), dot(cotangent_t[...], active[:, flat]).astype(BF16)
        ]
        if not near:
            for ref, grad in zip(grad_refs, grads, strict=True):
                ref[h, :, c : c + CHUNK] = grad
            continue
        size = w_in.shape[1] // 16
        x = h ^ (me & 1)
        for core, ref in enumerate(grad_refs):
            for y in range(2):
                for z in range(4):
                    block = core * 8 + y * 4 + z
                    rows = slice(block * size, (block + 1) * size)
                    for q in range(CHUNK // 128):
                        lanes = slice(q * 128, (q + 1) * 128)
                        place = slice((c // 128 + q) * size, (c // 128 + q + 1) * size)
                        ref[0, x, y, z, place, :] = grads[0][rows, lanes]
                        ref[1, y, x, z, place, :] = grads[1][rows, lanes]


def output_kernel(near, place_ref, *refs):
    count = 8 if near else 1
    totals, actives, refs = refs[:OUT_BLOCKS], refs[OUT_BLOCKS : 2 * OUT_BLOCKS], refs[2 * OUT_BLOCKS :]
    ahead = (len(refs) - count - 3) // 2
    sources, pieces, outputs, sinks, (w_out, sem) = (
        refs[:ahead], refs[ahead : ahead + count], refs[ahead + count], refs[ahead + count + 1 : -2], refs[-2:]
    )
    load_weights(near, place_ref, pieces, 1, w_out, sem).wait()
    halves, _, columns = w_out.shape
    size = totals[0].shape[0]
    for i, (total, active) in enumerate(zip(totals, actives, strict=True)):
        value = total[...]
        for h in range(halves):
            value = value + dot_nt(active[:, h * columns : (h + 1) * columns], w_out[h])
        outputs[i * size : (i + 1) * size, :] = value.astype(BF16)
    outputs.flush()
    for source, sink in zip(sources, sinks, strict=True):
        sink[...] = source[...]


def leave_kernel(groups, got_ref, tokens_ref, middle_ref, vectors_ref, table_ref, out_ref):
    spectra = spans(gather_lanes(got_ref, groups))
    span = table_ref.shape[0]
    for start in range(0, tokens_ref.shape[0], ROWS):
        rows = slice(start, start + ROWS)
        first = start % span
        upstream = dot(table_ref[first : first + ROWS, :], spectra[start // span])
        unit, inverse = normalize(tokens_ref[rows, :].astype(F32))
        back = norm_back(upstream, unit, inverse, vectors_ref[0:1, :])
        out_ref[rows, :] = (middle_ref[rows, :].astype(F32) + back).astype(BF16)


def update(weight, gradient, moment, average, decay_rate):
    step_grad = gradient + decay_rate * weight
    new_moment = MOMENTUM * moment + step_grad
    new_weight = weight - LEARNING_RATE * (step_grad + MOMENTUM * new_moment)
    new_average = AVERAGE * average + (1.0 - AVERAGE) * new_weight
    return (new_weight, new_moment, new_average)


class Source:
    def __init__(self, ref, copy):
        self.ref, self.copy, self.shape, self.started = ref, copy, ref.shape, False

    def start(self):
        if not self.started:
            self.copy.start()
            self.started = True

    def __getitem__(self, index):
        if self.copy is not None:
            self.start()
            self.copy.wait()
            self.copy = None
        return self.ref[index]


class Sink:
    def __init__(self, ref, copy):
        self.ref, self.copy, self.shape, self.sent = ref, copy, ref.shape, False

    def __getitem__(self, index):
        return self.ref[index]

    def __setitem__(self, index, value):
        self.ref[index] = value

    def flush(self):
        if not self.sent:
            self.copy.start()
            self.sent = True


class Far:
    def __init__(self, *what):
        self.what = what


class Late(Far):
    pass


def call(body, outs, *args, scalars=(), raw=(), scratch=(), flops=0, carry=(), cost=None, vmem=20):
    near, far, there = [pl.BlockSpec(memory_space=m) for m in (pltpu.VMEM, pltpu.HBM, pl.ANY)]
    in_far, out_far = [isinstance(a, Far) for a in args], [isinstance(o, Far) for o in outs]
    in_late = [isinstance(a, Late) for a in args]
    index = [a.what[1:] if f else () for a, f in zip(args, in_far, strict=True)]
    args = [
        pltpu.with_memory_space_constraint(*((a.what[0], pltpu.HBM) if f else (a, pltpu.VMEM)))
        for a, f in zip(args, in_far, strict=True)
    ]
    raw = [pltpu.with_memory_space_constraint(a, pltpu.HBM) for a in raw]
    outs = [o.what if f else o for o, f in zip(outs, out_far, strict=True)]
    outs = [jax.ShapeDtypeStruct(s, d) for s, d in outs]
    n_scalar, n_in, n_raw, n_carry, n_out = len(scalars), len(args), len(raw), len(carry), len(outs)
    shapes = [np.empty(a.shape, np.bool_)[i].shape if i else a.shape for a, i in zip(args, index, strict=True)]
    shapes += [o.shape for o in outs]
    buffers = [
        pltpu.VMEM(shape, a.dtype) for shape, a, f in zip(shapes, args + outs, in_far + out_far, strict=True) if f
    ]

    def inner(*refs):
        refs = list(refs)

        def take(count):
            taken = refs[:count]
            del refs[:count]
            return taken

        scalar_refs, in_refs, raw_refs, _, out_refs, _ = [
            take(n) for n in (n_scalar, n_in, n_raw, n_carry, n_out, n_carry)
        ]
        space = take(len(buffers))
        sems = take(1)[0] if buffers else None
        sources, sinks, used = [], [], 0
        for ref, away, part, late in zip(in_refs, in_far, index, in_late, strict=True):
            if away:
                copy = pltpu.make_async_copy(ref.at[part] if part else ref, space[used], sems.at[used])
                ref = Source(space[used], copy)
                if not late:
                    ref.start()
                used += 1
            sources.append(ref)
        for ref, away in zip(out_refs, out_far, strict=True):
            if away:
                ref = Sink(space[used], pltpu.make_async_copy(space[used], ref, sems.at[used]))
                used += 1
            sinks.append(ref)
        body(*scalar_refs, *sources, *raw_refs, *sinks, *refs)
        for source in sources:
            if isinstance(source, Source) and source.copy is not None:
                source.copy.wait()
        sinks = [sink for sink in sinks if isinstance(sink, Sink)]
        for sink in sinks:
            sink.flush()
        for sink in sinks:
            sink.copy.wait()

    every = list(args) + list(raw)
    size = sum(math.prod(a.shape) * a.dtype.itemsize for a in every + outs) if cost is None else cost
    sems = [pltpu.SemaphoreType.DMA((len(buffers),))] if buffers else []
    return pl.pallas_call(
        inner,
        out_shape=[(pltpu.HBM if f else pltpu.VMEM)(o.shape, o.dtype) for o, f in zip(outs, out_far, strict=True)]
        + [jax.ShapeDtypeStruct(a.shape, a.dtype) for a in carry],
        in_specs=[pl.BlockSpec(memory_space=pltpu.SMEM)] * n_scalar
        + [far if f else near for f in in_far]
        + [far] * n_raw
        + [there] * n_carry,
        out_specs=[far if f else near for f in out_far] + [there] * n_carry,
        scratch_shapes=buffers + sems + list(scratch),
        input_output_aliases={n_scalar + n_in + n_raw + i: n_out + i for i in range(n_carry)},
        compiler_params=pltpu.CompilerParams(vmem_limit_bytes=vmem << 20),
        cost_estimate=pl.CostEstimate(flops=flops, bytes_accessed=size, transcendentals=0),
    )(*scalars, *args, *raw, *carry)


def on_device(
    tokens, cotangent, w_in, w_out, mixer_weights, vectors, w_in_moment, w_out_moment, mixer_moment, vectors_moment,
    w_in_average, w_out_average, mixer_average, vectors_average,
):
    sp_count, tp_count = lax.axis_size("sp"), lax.axis_size("tp")
    devices = sp_count * tp_count
    grid_rows, grid, width = tokens.shape
    local = grid_rows * grid
    items = grid_rows * devices // grid
    block_count, block = mixer_weights.shape[1], mixer_weights.shape[3]
    hidden = w_in.shape[1] * tp_count
    model = w_in.shape[0] * sp_count
    lanes = 2 * block if devices * 2 * block <= MODES * width else block
    groups = width // lanes
    per_group = devices // groups
    modes = MODES // per_group
    joined = lanes // block
    scale = 1.0 / math.sqrt(local * devices)
    wide_f, wide_i, high, ones = expanded_tables(grid, items)
    me = lax.axis_index("sp") * tp_count + lax.axis_index("tp")
    group = me // per_group
    exchange = functools.partial(lax.all_to_all, axis_name=AXES, split_axis=0, concat_axis=0, tiled=True)
    chunk = (devices, modes * grid_rows * 2, lanes)
    rows_all = tokens.reshape(local, width)
    upstream_all = cotangent.reshape(local, width)
    shard_rows, shard_columns = w_in.shape
    shard_size = shard_rows * shard_columns // 128
    near = devices == 32 and per_group == 8 and shard_rows % 16 == 0

    def permute(values, mask):
        return lax.ppermute(values, AXES, [(d, d ^ mask) for d in range(devices)])

    pair = jnp.stack([w_in.astype(BF16), w_out.astype(BF16)])
    if near:
        line = [pair] + [permute(pair, 8 * z) for z in (1, 2, 3)]
        carried = [jnp.stack([v, permute(v, m)]) for v, m in ((jnp.stack(line[:2]), 1), (jnp.stack(line[2:]), 4))]
    else:
        weights = lax.all_gather(pair, "sp", axis=1, tiled=True)
        pieces, carried = [lax.all_gather(weights, "tp")], []

    wide_f, wide_f_t = jnp.asarray(wide_f), jnp.asarray(wide_f.T)
    wide_i, wide_i_t = jnp.asarray(wide_i), jnp.asarray(wide_i.T)
    high, high_t = jnp.asarray(high), jnp.asarray(high.T)
    wide_flops = 2 * MODES * 2 * local * width * SPAN
    place = jnp.stack([me % per_group, group])
    ones = jnp.asarray(np.swapaxes(ones.reshape(per_group, modes, -1), 1, 2))
    part = (2, joined, 2, block, block)
    cut = near and dict(
        raw=[ones, mixer_weights], scratch=[pltpu.VMEM(part, F32), pltpu.SemaphoreType.DMA((2,))]
    )
    sent, *own = call(
        functools.partial(enter_kernel, groups),
        [(chunk, BF16)] + ([(ones.shape[1:], F32), (part, BF16)] if near else []),
        Far(rows_all), Far(wide_f), scalars=[place], flops=wide_flops, **(cut or {}),
    )
    if near:
        own_ones, own_mixer = own
    else:
        own_mixer = lax.dynamic_slice_in_dim(mixer_weights, group * joined, joined, 1).astype(BF16)
        own_ones = lax.dynamic_index_in_dim(ones, me % per_group, 0, keepdims=False)
    eye = jnp.eye(joined, dtype=BF16)
    real = jnp.einsum("lbio,bc->lbico", own_mixer[:, :, 0], eye).reshape(2, lanes, lanes)
    imag = jnp.einsum("lbio,bc->lbico", own_mixer[:, :, 1], eye).reshape(2, lanes, lanes)
    mats = jnp.concatenate(
        [jnp.concatenate([real, imag], axis=2), jnp.concatenate([-imag, real], axis=2)], axis=1
    )
    own_bias = lax.dynamic_slice_in_dim(
        vectors[9:13].reshape(2, block_count, 2, block), group * joined, joined, 1
    )
    own_bias = jnp.swapaxes(own_bias, 1, 2).reshape(2, 2 * lanes)
    own_gain = lax.dynamic_slice_in_dim(vectors[0:1], group * lanes, lanes, 1)
    own_shift = lax.dynamic_slice_in_dim(vectors[1:2], group * lanes, lanes, 1)

    got = exchange(sent)
    half_rows = items * MODES
    sent, hat, modal, inner, active, *carried = call(
        functools.partial(mix_kernel, modes),
        [
            (chunk, BF16),
            Far((2 * half_rows, modes * lanes), F32),
            Far((modes * half_rows, 2 * lanes), BF16),
            Far((modes * half_rows, 2 * lanes), F32),
            Far((modes * half_rows, 2 * lanes), BF16),
        ],
        got, high, high_t, mats, own_bias, own_gain, own_shift, own_ones,
        carry=carried,
    )
    if near:
        pieces = carried + [permute(carried[0], 4), permute(carried[1], 1)]
        pieces += [permute(p, 2) for p in pieces]
    got = exchange(sent)
    steps = hidden // CHUNK
    grads = [((2, 2, 2, 4, shard_size, 128), BF16)] * 2 if near else [((tp_count, model, shard_columns), BF16)] * 2
    gelus, total, middle, sent, mlp_small, *grads = call(
        functools.partial(mlp_kernel, groups, near),
        [
            Far((local, hidden), BF16), Far((local, width), F32), Far((local, width), BF16), Far(chunk, BF16),
            ((8, width), F32),
        ]
        + grads,
        Far(got), Far(wide_i_t), Far(rows_all), Late(upstream_all), vectors, vectors[5:9].reshape(steps, CHUNK), Late(wide_i),
        scalars=[me[None]], raw=pieces,
        scratch=[
            pltpu.VMEM((local, width), BF16),
            pltpu.VMEM((width, local), BF16),
            pltpu.VMEM((width, local), BF16),
            pltpu.VMEM((local, width), F32),
            pltpu.VMEM((local, 1), F32),
            pltpu.VMEM((tp_count, 2, model, shard_columns), BF16),
            pltpu.VMEM((local, hidden), BF16),
            pltpu.SemaphoreType.DMA,
        ],
        flops=12 * local * width * hidden + 2 * wide_flops, vmem=44,
    )

    carried = []
    if near:
        shard = (4, shard_size, 128)
        kept, one = grads[0], permute(grads[1], 2)
        sent_in, sent_out = call(
            first_kernel, [((2,) + shard, BF16)] * 2, kept, Far(one, slice(None), 1), cost=0
        )
        carried = [permute(sent_in, 1), permute(sent_out, 4)]

    step = local // OUT_BLOCKS
    parts = [slice(r, r + step) for r in range(0, local, step)]
    kept_forward = [high, high_t, mats, hat, modal, inner, active]
    ahead = kept_forward[:3] if near else []
    output, *ahead = call(
        functools.partial(output_kernel, near),
        [Far((local, width), BF16)] + [(a.shape, a.dtype) for a in ahead],
        *[Far(total, rows) for rows in parts], *[Far(gelus, rows) for rows in parts], *[Far(a) for a in ahead],
        scalars=[me[None]], raw=pieces, cost=COST, vmem=24,
        scratch=[
            pltpu.VMEM((tp_count, model, shard_columns), BF16),
            pltpu.SemaphoreType.DMA,
        ],
    )

    kept_forward = ahead + [Far(a) for a in kept_forward[len(ahead) :]]
    got = exchange(sent)
    small_rows = -(-(2 * block + 8 + 8 * (groups // 2)) // 16) * 16
    place = ((me >> 1) & 1 if near else jnp.int32(0))[None]
    sent, small, given, output = call(
        functools.partial(unmix_kernel, modes, block),
        [Far(chunk, BF16), ((small_rows, lanes), BF16), ((small_rows, lanes), BF16)],
        got, *kept_forward[:3], own_ones, *kept_forward[3:], mlp_small,
        scalars=[place], cost=COST, vmem=20 if near else 48, carry=[output],
    )
    if near:
        both = slice(None)
        small, over_y, over_x = call(
            second_kernel, [((small_rows, lanes), BF16)] + [(shard, BF16)] * 2,
            kept, *[Far(a, 1) for a in carried], small, permute(given, 2), Far(one, both, 0, 1), cost=0,
        )
        line, own, *away = call(
            third_kernel,
            [((4, small_rows, lanes), BF16), ((2, shard_size, 128), F32)] + [((2, shard_size, 128), BF16)] * 3,
            kept, *[Far(a, 0) for a in carried], permute(over_y, 4), permute(over_x, 1),
            small, *[permute(small, 8 * z) for z in (1, 2, 3)], Far(one, both, 0, 0),
            scalars=[me[None]], cost=0,
        )
        away = [permute(a, 8 * (z + 1)) for z, a in enumerate(away)]
    got = exchange(sent)
    (grad_tokens,) = call(
        functools.partial(leave_kernel, groups),
        [Far((local, width), BF16)],
        got, Far(rows_all), Far(middle), vectors, Far(wide_f_t), cost=COST,
    )

    if near:
        line, *away, grad_tokens = call(
            plane_kernel, [(line.shape, BF16)], line, *[permute(line, m) for m in (1, 4, 5)], cost=0, carry=[*away, grad_tokens]
        )
        other = permute(line, 2)

    state = [mixer_weights, mixer_moment, mixer_average, vectors, vectors_moment, vectors_average]
    new_state = [Far(a.shape, F32) for a in state]
    if near:
        weights = [w_in, w_out, w_in_moment, w_out_moment, w_in_average, w_out_average]
        *stepped, grad_tokens = call(
            functools.partial(step_all, block, scale),
            [Far(w_in.shape, F32)] * 6 + [Far(w_in.shape, BF16)] * 2 + new_state,
            own, *away, *weights, line, other, *state,
            scalars=[place], scratch=[pltpu.VMEM((16, width), F32)], carry=[grad_tokens], cost=0,
        )
        new_in, new_out = stepped[0:8:2], stepped[1:8:2]
        stepped = stepped[8:]
    else:
        grads = jnp.stack(grads).astype(F32)
        grads = lax.psum_scatter(grads, "tp", scatter_dimension=1, tiled=True)
        grads = lax.psum_scatter(grads, "sp", scatter_dimension=2, tiled=True)
        new_in = update(w_in, grads[0, 0] * scale, w_in_moment, w_in_average, WEIGHT_DECAY)
        new_out = update(w_out, grads[1, 0] * scale, w_out_moment, w_out_average, WEIGHT_DECAY)
        new_in, new_out = new_in + (new_in[0].astype(BF16),), new_out + (new_out[0].astype(BF16),)
        onehot = (jnp.arange(groups, dtype=jnp.int32) == group).astype(F32)[:, None, None]
        line, other = lax.psum((onehot * small.astype(F32), onehot * given.astype(F32)), AXES)
        stepped = call(
            functools.partial(step_rest, block, scale), new_state, line, other, *state,
            scalars=[place], scratch=[pltpu.VMEM((16, width), F32)],
        )
    new_mix, new_vec = stepped[0:3], stepped[3:6]
    shape = tokens.shape
    return (
        output.reshape(shape), grad_tokens.reshape(shape),
        new_in[0], new_out[0], new_mix[0], new_vec[0],
        new_in[1], new_out[1], new_mix[1], new_vec[1],
        new_in[2], new_out[2], new_mix[2], new_vec[2],
        new_in[3], new_out[3],
    )


def solution(mesh):
    rows, split, whole = P(AXES, None, None), P("sp", "tp"), P()
    state = (split, split, whole, whole)
    return jax.shard_map(
        on_device,
        mesh=mesh,
        in_specs=(rows, rows) + state * 3,
        out_specs=(rows, rows) + state * 3 + (split, split),
        check_vma=False,
    )
```
